256 devices in a mesh: rows: 32 (over x, y, core), snaps: 8 (over z).
Axes of the slice: x: 4, y: 4, z: 8, core: 2. Of those that a mesh axis runs over, the one named last changes fastest.
Arguments:
- snapshots: bfloat16 [262144, 4096], P('rows', 'snaps'), may hold values from -22 to 22
- sketch: bfloat16 [4096, 128], P('snaps'), may hold values from -0.09375 to 0.09375
Outputs:
- basis: float32 [262144, 128], P(('rows', 'snaps'))
- projected: float32 [128, 4096], P('rows', 'snaps')
The draws below stay inside these ranges and needn't reach their ends.
All inputs are finite; a program needn't handle non-finite values.
Results may differ from the reference program's by a relative error of at most 0.00055.
Values may be sent and summed in bfloat16 or wider, within the bound.
A program may use at most 64 MiB of HBM per device.

```python
import math
import jax
import jax.numpy as jnp
from jax import lax

SNAPSHOTS = 4096
RANK = 128
ROWS = 262144


def draw_snapshots(key, part):
    key = jax.random.fold_in(key, 11)
    key_row, key_col, key_base = jax.random.split(key, 3)
    half_ten = 0.5 * math.log(10.0)
    half_three = 0.5 * math.log(3.0)
    row_scale = jnp.exp(jax.random.uniform(key_row, (ROWS, 1), jnp.float32, -half_ten, half_ten))
    col_scale = jnp.exp(jax.random.uniform(key_col, (1, SNAPSHOTS), jnp.float32, -half_three, half_three))
    base = jnp.clip(jax.random.normal(key_base, (ROWS, SNAPSHOTS), jnp.float32), -4.0, 4.0)
    return (base * row_scale * col_scale).astype(jnp.bfloat16)


def block_scale(key, dims, shards, least, top_value):
    def one(dim, blocks):
        draws = jax.random.uniform(jax.random.fold_in(jax.random.fold_in(key, 6), dim), (blocks,), jnp.float32, least / len(shards), top_value / len(shards))
        return jnp.repeat(jnp.exp(draws), dims[dim] // blocks).reshape((-1,) + (1,) * (len(dims) - dim - 1))

    loudness = one(*shards[0])
    for cut in shards[1:]:
        loudness = loudness * one(*cut)
    return loudness


def noise(stream_key, extent, deviation, bound, pieces=(), dtype=jnp.bfloat16):
    entries = deviation * jax.random.normal(stream_key, extent, jnp.float32)
    if pieces:
        entries = entries * block_scale(stream_key, extent, pieces, -0.22, 0.18)
    return jnp.clip(entries, -bound, bound).astype(dtype)


def setup_inputs(seed: int = 0) -> dict:
    seeds = jax.random.split(jax.random.key(seed), 3)
    return {
        "snapshots": draw_snapshots(jax.random.fold_in(seeds[2], 71), 0),
        "sketch": noise(seeds[1], (SNAPSHOTS, RANK), SNAPSHOTS ** -0.5, 0.09375, ((0, 8),)),
    }


def reference(snapshots, sketch):
    sampled = jnp.dot(snapshots.astype(jnp.float32), sketch.astype(jnp.float32), preferred_element_type=jnp.float32)
    gram = jnp.dot(sampled.T, sampled, precision=lax.Precision.HIGHEST) / ROWS
    lower = jnp.linalg.cholesky(gram)
    basis = lax.linalg.triangular_solve(lower, sampled, left_side=False, lower=True, transpose_a=True)
    coarse = basis.astype(jnp.bfloat16)
    projected = jnp.dot(coarse.T.astype(jnp.float32), snapshots.astype(jnp.float32), preferred_element_type=jnp.float32) / math.sqrt(ROWS)
    return (basis, projected)
```

```python
import functools
import math

import jax
import jax.numpy as jnp
from jax import lax
from jax.experimental import pallas as pl
from jax.experimental.pallas import tpu as pltpu
from jax.sharding import PartitionSpec as P

MESH = pl.DeviceIdType.MESH
HIGHEST = lax.Precision.HIGHEST
F32, BF16 = jnp.float32, jnp.bfloat16

RING = 8
PIECES = 4
EVENTS = 2 * (RING - 1)
SPAN = 120.0
BLOCK = 16


def encode(value, buf):
    rows, rank = value.shape
    groups = value.reshape(rows // 16, 16, rank)
    size = jnp.abs(groups)
    top = (jnp.max(size, axis=0) * 1.01 + 1e-30).astype(BF16)
    buf[rows : rows + 16, :] = top
    gain = (2.0 * SPAN) / top.astype(F32)
    code = jnp.exp2(size * gain[None] - SPAN)
    code = jnp.where(groups < 0.0, -code, code)
    buf[0:rows, :] = code.reshape(rows, rank).astype(BF16)


def decode(buf):
    rows, rank = buf.shape[0] - 16, buf.shape[1]
    code = buf[0:rows, :].astype(F32).reshape(rows // 16, 16, rank)
    top = buf[rows : rows + 16, :].astype(F32)
    gain = top * (1.0 / (2.0 * SPAN * math.log(2.0)))
    size = (jnp.log(jnp.abs(code)) + SPAN * math.log(2.0)) * gain[None]
    return jnp.where(code < 0.0, -size, size).reshape(rows, rank)


def split(value):
    high = value.astype(BF16)
    return high, (value - high.astype(F32)).astype(BF16)


def factor_block(x, block):
    rank = x.shape[0]
    first = pl.multiple_of(block * BLOCK, BLOCK)
    shape = (BLOCK, rank)
    panel = x[pl.ds(first, BLOCK), :]
    left, right = panel[:, :rank], panel[:, rank:]
    corner = pltpu.roll(left, lax.rem(rank - first, rank), 1)
    row = lax.broadcasted_iota(jnp.int32, shape, 0)
    lane = lax.broadcasted_iota(jnp.int32, shape, 1)
    columns = [jnp.broadcast_to(corner[:, j : j + 1], shape) for j in range(BLOCK)]

    def spread(value, i):
        return jnp.broadcast_to(value[i : i + 1, :], shape)

    first_pivot = cross = determinant = jnp.zeros(shape, F32)
    for i in range(0, BLOCK, 2):
        one, two = columns[i], columns[i + 1]
        a, b, d = spread(one, i), spread(one, i + 1), spread(two, i + 1)
        det = a * d - b * b
        here = (row == i) | (row == i + 1)
        first_pivot = jnp.where(here, a, first_pivot)
        cross = jnp.where(row == i + 1, b, cross)
        determinant = jnp.where(here, det, determinant)
        if i + 2 == BLOCK:
            break
        inverse = jnp.where(row > i + 1, 1.0 / det, 0.0)
        u, v = (one * d - two * b) * inverse, (two * a - one * b) * inverse
        for j in range(i + 2, BLOCK):
            columns[j] = columns[j] - (u * spread(columns[j], i) + v * spread(columns[j], i + 1))
        left = left - (u * spread(left, i) + v * spread(left, i + 1))
        right = right - (u * spread(right, i) + v * spread(right, i + 1))
    odd = row % 2 == 1
    factor = cross / first_pivot
    scale = jnp.where(odd, first_pivot * lax.rsqrt(first_pivot * determinant), lax.rsqrt(first_pivot))
    left = (left - factor * pltpu.roll(left, 1, 0)) * scale
    right = (right - factor * pltpu.roll(right, 1, 0)) * scale
    whole = jnp.concatenate([left, right], axis=1)
    x[pl.ds(first, BLOCK), :] = whole
    r1, r2 = split(whole)
    r3 = (whole - r1.astype(F32) - r2.astype(F32)).astype(BF16)
    later = jnp.where(lane >= first + BLOCK, left, 0.0)
    l1, l2 = split(later)
    l3 = (later - l1.astype(F32) - l2.astype(F32)).astype(BF16)
    x[...] -= lax.dot_general(
        jnp.concatenate([l1, l1, l2, l1, l2, l3], axis=0),
        jnp.concatenate([r1, r2, r1, r3, r2, r1], axis=0),
        (((0,), (0,)), ((), ())),
        preferred_element_type=F32,
    )


def kernel(
    total, s_hbm, k_hbm, basis_hbm, proj_ref,
    s, k, part, tx, rx, everyone, z_sum, gg, g, g1, g2, g3, x, give, take, pair, zr, white,
    load_sem, rs_send, rs_recv, ag_send, ag_recv, g1_send, g1_recv, g2_send, g2_recv, g3_send, g3_recv,
    zr_send, zr_recv, mate_send, mate_recv, out_sem,
):
    chips = lax.axis_size("rows") // 2
    r, z = lax.axis_index("rows"), lax.axis_index("snaps")
    chip, core = lax.div(r, 2), lax.rem(r, 2)
    spot = z * 2 + core
    shard = part.shape[1]
    size = shard // PIECES
    rank = k.shape[1]
    own = rank // chips

    def at(step):
        return lax.rem(z + step + RING, RING)

    def load(offset, slot):
        rows = pl.ds(pl.multiple_of(at(offset) * shard, shard), shard)
        return pltpu.make_async_copy(s_hbm.at[rows, :], s.at[rows, :], load_sem.at[slot])

    order = (4, 3, -3, 2, -2, 1, -1, 0)
    sketch_copy = pltpu.make_async_copy(k_hbm, k, load_sem.at[RING])
    sketch_copy.start()
    for slot, offset in enumerate(order):
        load(offset, slot).start()

    barrier = pltpu.get_barrier_semaphore()

    def other_chip(step):
        return lax.rem(chip + step, chips)

    def other_spot(step):
        return lax.rem(spot + step, 2 * RING)

    def to_chip(step):
        return {"rows": other_chip(step) * 2 + core, "snaps": z}

    def to_spot(step):
        there = other_spot(step)
        return {"rows": chip * 2 + lax.rem(there, 2), "snaps": lax.div(there, 2)}

    @pl.loop(1, chips)
    def _(step):
        pl.semaphore_signal(barrier, inc=1, device_id=to_chip(step), device_id_type=MESH)

    @pl.loop(1, 2 * RING)
    def _(step):
        pl.semaphore_signal(barrier, inc=1, device_id=to_spot(step), device_id_type=MESH)

    def ring(side, src, dst, send, recv):
        return pltpu.make_async_remote_copy(
            src_ref=src,
            dst_ref=dst,
            send_sem=send,
            recv_sem=recv,
            device_id={"rows": r, "snaps": at(1 - 2 * side)},
            device_id_type=MESH,
        )

    def sum_copy(side, t):
        return ring(side, tx.at[side, t], rx.at[side, t], rs_send.at[side, t], rs_recv.at[side, t])

    def piece(q):
        return pl.ds(pl.multiple_of(q * size, size), size)

    def sketch(offset, slot):
        load(offset, slot).wait()
        j = at(offset)

        @pl.loop(0, PIECES)
        def _(q):
            rows = pl.ds(pl.multiple_of(j * shard + q * size, size), size)
            part[j, piece(q), :] = jnp.dot(s[rows, :], k[...], preferred_element_type=F32)

    def head(side, t, offset, q):
        encode(part[at(offset), piece(q), :], tx.at[side, t])
        sum_copy(side, t).start()

    sketch_copy.wait()
    sketch(order[0], 0)
    pl.semaphore_wait(barrier, chips - 1 + 2 * RING - 1)

    @pl.loop(0, 2)
    def _(i):
        head(0, i, 4, i)
        head(1, i, 4, 2 + i)

    sketch(order[1], 1)

    @pl.loop(0, 2)
    def _(i):
        head(0, 2 + i, 3, 2 + i)

    sketch(order[2], 2)

    @pl.loop(0, 2)
    def _(i):
        head(1, 2 + i, -3, i)

    for slot in range(3, RING):
        sketch(order[slot], slot)

    def turn(side, t):
        pair, i = t // 2, t % 2
        odd = pair % 2
        far = 4 - (pair + 1) // 2
        return far, i + 2 * (odd if side == 0 else 1 - odd)

    @pl.loop(0, EVENTS - 4)
    def _(t):
        for side in range(2):
            far, q = turn(side, t)
            j = at((1 - 2 * side) * (far - 1))
            sum_copy(side, t).wait_recv()
            encode(part[j, piece(q), :] + decode(rx.at[side, t]), tx.at[side, t + 4])
            sum_copy(side, t + 4).start()

    def gather_copy(side, e, j, q):
        block = everyone.at[j, piece(q), :]
        return ring(side, block, block, ag_send.at[side, e], ag_recv.at[side, e])

    def gather_piece(side, e):
        hop = jnp.minimum(e // 4 + 1, 4)
        i = jnp.where(e < 12, e % 4, 2 * (e - 12))
        odd = i % 2
        return hop, 2 * (odd if side == 0 else 1 - odd) + i // 2

    @pl.loop(EVENTS - 4, EVENTS - 2)
    def _(t):
        for side in range(2):
            _, q = turn(side, t)
            sum_copy(side, t).wait_recv()
            part[z, piece(q), :] += decode(rx.at[side, t])

    def gram(q):
        both = jnp.concatenate(split(part[z, piece(q), :]), axis=1)
        gg[...] += lax.dot_general(both, both, (((0,), (0,)), ((), ())), preferred_element_type=F32)

    gg[...] = jnp.zeros_like(gg)

    @pl.loop(EVENTS - 2, EVENTS)
    def _(t):
        for side in range(2):
            _, q = turn(side, t)
            sum_copy(side, t).wait_recv()
            mine = part[z, piece(q), :] + decode(rx.at[side, t])
            part[z, piece(q), :] = mine
            everyone[z, piece(q), :] = mine.astype(BF16)
        for side in range(2):
            for odd in range(2):
                e = 2 * (t - (EVENTS - 2)) + odd
                gather_copy(side, e, z, gather_piece(side, e)[1]).start()

        for side in range(2):
            gram(turn(side, t)[1])

    g[...] = gg[:rank, :rank] + gg[:rank, rank:] + gg[rank:, :rank] + gg[rank:, rank:]

    def block_of(index):
        return pl.ds(pl.multiple_of(index * own, own), own)

    def plane_copy(step, src, dst, send, recv, slot):
        return pltpu.make_async_remote_copy(
            src_ref=src,
            dst_ref=dst,
            send_sem=send.at[step],
            recv_sem=recv.at[slot],
            device_id=to_chip(step),
            device_id_type=MESH,
        )

    def g1_copy(step, slot):
        return plane_copy(step, g.at[block_of(other_chip(step)), :], g1.at[slot], g1_send, g1_recv, slot)

    def g2_copy(step, slot):
        return pltpu.make_async_remote_copy(
            src_ref=g2.at[spot],
            dst_ref=g2.at[slot],
            send_sem=g2_send.at[step],
            recv_sem=g2_recv.at[slot],
            device_id=to_spot(step),
            device_id_type=MESH,
        )

    def g3_copy(step, slot):
        return plane_copy(step, g3.at[block_of(chip), :], g3.at[block_of(slot), :], g3_send, g3_recv, slot)

    def zr_copy(step, slot):
        return plane_copy(step, pair.at[other_chip(step)], zr.at[slot], zr_send, zr_recv, slot)

    @pl.loop(1, chips)
    def _(step):
        g1_copy(step, chip).start()

    z_sum[...] = jnp.zeros_like(z_sum)

    def project(j, q):
        rows = pl.ds(pl.multiple_of(j * shard + q * size, size), size)
        z_sum[...] += lax.dot_general(
            everyone[j, piece(q), :], s[rows, :], (((0,), (0,)), ((), ())), preferred_element_type=F32
        )

    def gather(e):
        for side in range(2):
            hop, q = gather_piece(side, e)
            j = at(-(1 - 2 * side) * hop)
            gather_copy(side, e, j, q).wait_recv()

            @pl.when((e < 8) | (e == 8) | (e == 10))
            def _():
                gather_copy(side, jnp.where(e < 8, e + 4, 12 + (e - 8) // 2), j, q).start()

        for side in range(2):
            hop, q = gather_piece(side, e)
            project(at(-(1 - 2 * side) * hop), q)

    @pl.loop(0, PIECES)
    def _(q):
        project(z, q)

    gather(0)

    @pl.loop(1, chips)
    def _(step):
        g1_copy(step, other_chip(step)).wait_recv()

    g1[chip] = g[block_of(chip), :]
    g2[spot] = jnp.sum(g1[...], axis=0)

    @pl.loop(1, 2 * RING)
    def _(step):
        g2_copy(step, spot).start()

    @pl.loop(1, 3)
    def _(e):
        gather(e)

    @pl.loop(1, 2 * RING)
    def _(step):
        g2_copy(step, other_spot(step)).wait_recv()

    g3[block_of(chip), :] = jnp.sum(g2[...], axis=0) * (1.0 / total)

    @pl.loop(1, chips)
    def _(step):
        g3_copy(step, chip).start()

    @pl.loop(3, 5)
    def _(e):
        gather(e)

    @pl.loop(1, chips)
    def _(step):
        g3_copy(step, other_chip(step)).wait_recv()

    eye = lax.broadcasted_iota(jnp.int32, (rank, rank), 0) == lax.broadcasted_iota(jnp.int32, (rank, rank), 1)
    full = g3[...]
    diagonal = jnp.where(eye, full, 0.0)
    down = lax.rsqrt(jnp.sum(diagonal, axis=1, keepdims=True))
    across = lax.rsqrt(jnp.sum(diagonal, axis=0, keepdims=True))
    x[...] = jnp.concatenate([full * down * across, jnp.where(eye, down, 0.0)], axis=1)

    @pl.loop(5, EVENTS - 1)
    def _(e):
        gather(e)
        factor_block(x, e - 5)

    gather(EVENTS - 1)

    l1, l2 = split(x[:, rank:])
    z1, z2 = split(z_sum[...])
    term = jnp.dot(
        jnp.concatenate([l1, l2, l1], axis=1),
        jnp.concatenate([z1, z1, z2], axis=0),
        preferred_element_type=F32,
    ) * (1.0 / math.sqrt(total))
    half = own // 2
    z_sum[...] = term
    for c in range(chips):
        rows = z_sum[c * own : (c + 1) * own, :]
        low, high = rows[:half], rows[half:]
        give[c] = jnp.where(core == 0, high, low)
        pair[c] = jnp.where(core == 0, low, high)
    mate = pltpu.make_async_remote_copy(
        src_ref=give,
        dst_ref=take,
        send_sem=mate_send,
        recv_sem=mate_recv,
        device_id={"rows": chip * 2 + 1 - core, "snaps": z},
        device_id_type=MESH,
    )
    mate.start()
    i1, i2 = split(x[:, rank:])
    mate.wait_recv()
    pair[...] += take[...]

    @pl.loop(1, chips)
    def _(step):
        zr_copy(step, chip).start()

    def basis_copy(q):
        return pltpu.make_async_copy(white.at[piece(q), :], basis_hbm.at[piece(q), :], out_sem.at[q])

    @pl.loop(0, PIECES)
    def _(q):
        y1, y2 = split(part[z, piece(q), :])
        white[piece(q), :] = lax.dot_general(
            jnp.concatenate([y1, y1, y2], axis=1),
            jnp.concatenate([i1, i2, i1], axis=1),
            (((1,), (1,)), ((), ())),
            preferred_element_type=F32,
        )
        basis_copy(q).start()

    @pl.loop(1, chips)
    def _(step):
        zr_copy(step, other_chip(step)).wait_recv()

    zr[chip] = pair[chip]
    proj_ref[...] = jnp.sum(zr[...], axis=0)

    @pl.loop(0, EVENTS)
    def _(t):
        for side in range(2):
            sum_copy(side, t).wait_send()
            gather_copy(side, t, z, 0).wait_send()

    @pl.loop(1, chips)
    def _(step):
        g1_copy(step, chip).wait_send()
        g3_copy(step, chip).wait_send()
        zr_copy(step, chip).wait_send()

    @pl.loop(1, 2 * RING)
    def _(step):
        g2_copy(step, spot).wait_send()

    @pl.loop(0, PIECES)
    def _(q):
        basis_copy(q).wait()

    mate.wait_send()


def finish(basis_in, proj_in, basis_out, proj_out, sem):
    copies = [pltpu.make_async_copy(proj_in, proj_out, sem.at[0])]
    size = basis_in.shape[0] // 4
    for q in range(4):
        rows = pl.ds(q * size, size)
        copies.append(pltpu.make_async_copy(basis_in.at[rows, :], basis_out.at[rows, :], sem.at[1 + q]))
    for copy in copies:
        copy.start()
    for copy in copies:
        copy.wait()


def local(snapshots, sketch):
    rows, columns = snapshots.shape
    rank = sketch.shape[1]
    chips = lax.axis_size("rows") // 2
    total = rows * lax.axis_size("rows")
    shard = rows // RING
    own = rank // chips
    message = shard // PIECES + 16
    dma = pltpu.SemaphoreType.DMA
    outputs = (
        jax.ShapeDtypeStruct((shard, rank), F32),
        jax.ShapeDtypeStruct((own // 2, columns), F32),
    )
    anywhere = pl.BlockSpec(memory_space=pl.ANY)
    basis, projected = pl.pallas_call(
        functools.partial(kernel, total),
        out_shape=outputs,
        in_specs=[anywhere] * 2,
        out_specs=(anywhere, pl.BlockSpec(memory_space=pltpu.VMEM)),
        scratch_shapes=[
            pltpu.VMEM((rows, columns), BF16),
            pltpu.VMEM((columns, rank), BF16),
            pltpu.VMEM((RING, shard, rank), F32),
            pltpu.VMEM((2, EVENTS, message, rank), BF16),
            pltpu.VMEM((2, EVENTS, message, rank), BF16),
            pltpu.VMEM((RING, shard, rank), BF16),
            pltpu.VMEM((rank, columns), F32),
            pltpu.VMEM((2 * rank, 2 * rank), F32),
            pltpu.VMEM((rank, rank), F32),
            pltpu.VMEM((chips, own, rank), F32),
            pltpu.VMEM((2 * RING, own, rank), F32),
            pltpu.VMEM((rank, rank), F32),
            pltpu.VMEM((rank, 2 * rank), F32),
            pltpu.VMEM((chips, own // 2, columns), F32),
            pltpu.VMEM((chips, own // 2, columns), F32),
            pltpu.VMEM((chips, own // 2, columns), F32),
            pltpu.VMEM((chips, own // 2, columns), F32),
            pltpu.VMEM((shard, rank), F32),
            dma((RING + 1,)),
            dma((2, EVENTS)),
            dma((2, EVENTS)),
            dma((2, EVENTS)),
            dma((2, EVENTS)),
            dma((chips,)),
            dma((chips,)),
            dma((2 * RING,)),
            dma((2 * RING,)),
            dma((chips,)),
            dma((chips,)),
            dma((chips,)),
            dma((chips,)),
            dma,
            dma,
            dma((PIECES,)),
        ],
        compiler_params=pltpu.CompilerParams(
            collective_id=0, has_side_effects=True, vmem_limit_bytes=56 * 1024 * 1024
        ),
    )(snapshots, sketch)
    return pl.pallas_call(
        finish,
        out_shape=outputs,
        in_specs=[anywhere] * 2,
        out_specs=(anywhere, anywhere),
        scratch_shapes=[dma((5,))],
        compiler_params=pltpu.CompilerParams(vmem_limit_bytes=63 * 1024 * 1024),
    )(basis, projected)


def solution(mesh):
    in_specs = (P("rows", "snaps"), P("snaps", None))
    out_specs = (P(("rows", "snaps"), None), P("rows", "snaps"))
    return jax.shard_map(local, mesh=mesh, in_specs=in_specs, out_specs=out_specs, check_vma=False)
```

```python
import functools
import math

import jax
import jax.numpy as jnp
from jax import lax
from jax.experimental import pallas as pl
from jax.experimental.pallas import tpu as pltpu
from jax.sharding import PartitionSpec as P

MESH = pl.DeviceIdType.MESH
HIGHEST = lax.Precision.HIGHEST
F32, BF16 = jnp.float32, jnp.bfloat16

RING = 8
PIECES = 4
EVENTS = 2 * (RING - 1)
SPAN = 120.0
BLOCK = 16


def encode(value, buf):
    rows, rank = value.shape
    groups = value.reshape(rows // 16, 16, rank)
    top = (jnp.max(jnp.abs(groups), axis=0) * 1.01 + 1e-30).astype(BF16)
    buf[rows : rows + 16, :] = top
    gain = SPAN / top.astype(F32)
    buf[0:rows, :] = jnp.exp2(groups * gain[None]).reshape(rows, rank).astype(BF16)


def decode(buf):
    rows, rank = buf.shape[0] - 16, buf.shape[1]
    code = buf[0:rows, :].astype(F32).reshape(rows // 16, 16, rank)
    gain = buf[rows : rows + 16, :].astype(F32) * (1.0 / (SPAN * math.log(2.0)))
    return (jnp.log(code) * gain[None]).reshape(rows, rank)


def split(value):
    high = value.astype(BF16)
    return high, (value - high.astype(F32)).astype(BF16)


def factor_block(x, block):
    rank = x.shape[0]
    first = pl.multiple_of(block * BLOCK, BLOCK)
    shape = (BLOCK, rank)
    panel = x[pl.ds(first, BLOCK), :]
    left, right = panel[:, :rank], panel[:, rank:]
    corner = pltpu.roll(left, lax.rem(rank - first, rank), 1)
    row = lax.broadcasted_iota(jnp.int32, shape, 0)
    lane = lax.broadcasted_iota(jnp.int32, shape, 1)
    columns = [jnp.broadcast_to(corner[:, j : j + 1], shape) for j in range(BLOCK)]

    def spread(value, i):
        return jnp.broadcast_to(value[i : i + 1, :], shape)

    first_pivot = cross = determinant = jnp.zeros(shape, F32)
    for i in range(0, BLOCK, 2):
        one, two = columns[i], columns[i + 1]
        a, b, d = spread(one, i), spread(one, i + 1), spread(two, i + 1)
        det = a * d - b * b
        here = (row == i) | (row == i + 1)
        first_pivot = jnp.where(here, a, first_pivot)
        cross = jnp.where(row == i + 1, b, cross)
        determinant = jnp.where(here, det, determinant)
        if i + 2 == BLOCK:
            break
        inverse = jnp.where(row > i + 1, 1.0 / det, 0.0)
        u, v = (one * d - two * b) * inverse, (two * a - one * b) * inverse
        for j in range(i + 2, BLOCK):
            columns[j] = columns[j] - (u * spread(columns[j], i) + v * spread(columns[j], i + 1))
        left = left - (u * spread(left, i) + v * spread(left, i + 1))
        right = right - (u * spread(right, i) + v * spread(right, i + 1))
    odd = row % 2 == 1
    factor = cross / first_pivot
    scale = jnp.where(odd, first_pivot * lax.rsqrt(first_pivot * determinant), lax.rsqrt(first_pivot))
    left = (left - factor * pltpu.roll(left, 1, 0)) * scale
    right = (right - factor * pltpu.roll(right, 1, 0)) * scale
    whole = jnp.concatenate([left, right], axis=1)
    x[pl.ds(first, BLOCK), :] = whole
    r1, r2 = split(whole)
    r3 = (whole - r1.astype(F32) - r2.astype(F32)).astype(BF16)
    later = jnp.where(lane >= first + BLOCK, left, 0.0)
    l1, l2 = split(later)
    l3 = (later - l1.astype(F32) - l2.astype(F32)).astype(BF16)
    x[...] -= lax.dot_general(
        jnp.concatenate([l1, l1, l2, l1, l2, l3], axis=0),
        jnp.concatenate([r1, r2, r1, r3, r2, r1], axis=0),
        (((0,), (0,)), ((), ())),
        preferred_element_type=F32,
    )


def kernel(
    total, s_hbm, k_hbm, basis_hbm, proj_ref,
    s, k, part, tx, rx, everyone, z_sum, gg, g, g1, g2, g3, x, give, take, pair, zr, white,
    load_sem, rs_send, rs_recv, ag_send, ag_recv, g1_send, g1_recv, g2_send, g2_recv, g3_send, g3_recv,
    zr_send, zr_recv, mate_send, mate_recv, out_sem,
):
    chips = lax.axis_size("rows") // 2
    r, z = lax.axis_index("rows"), lax.axis_index("snaps")
    chip, core = lax.div(r, 2), lax.rem(r, 2)
    spot = z * 2 + core
    shard = part.shape[1]
    size = shard // PIECES
    rank = k.shape[1]
    own = rank // chips

    def at(step):
        return lax.rem(z + step + RING, RING)

    def load(offset, slot):
        rows = pl.ds(pl.multiple_of(at(offset) * shard, shard), shard)
        return pltpu.make_async_copy(s_hbm.at[rows, :], s.at[rows, :], load_sem.at[slot])

    order = (4, 3, -3, 2, -2, 1, -1, 0)
    sketch_copy = pltpu.make_async_copy(k_hbm, k, load_sem.at[RING])
    sketch_copy.start()
    for slot, offset in enumerate(order):
        load(offset, slot).start()

    barrier = pltpu.get_barrier_semaphore()

    def other_chip(step):
        return lax.rem(chip + step, chips)

    def other_spot(step):
        return lax.rem(spot + step, 2 * RING)

    def to_chip(step):
        return {"rows": other_chip(step) * 2 + core, "snaps": z}

    def to_spot(step):
        there = other_spot(step)
        return {"rows": chip * 2 + lax.rem(there, 2), "snaps": lax.div(there, 2)}

    @pl.loop(1, chips)
    def _(step):
        pl.semaphore_signal(barrier, inc=1, device_id=to_chip(step), device_id_type=MESH)

    @pl.loop(1, 2 * RING)
    def _(step):
        pl.semaphore_signal(barrier, inc=1, device_id=to_spot(step), device_id_type=MESH)

    def ring(side, src, dst, send, recv):
        return pltpu.make_async_remote_copy(
            src_ref=src,
            dst_ref=dst,
            send_sem=send,
            recv_sem=recv,
            device_id={"rows": r, "snaps": at(1 - 2 * side)},
            device_id_type=MESH,
        )

    def sum_copy(side, t):
        return ring(side, tx.at[side, t], rx.at[side, t], rs_send.at[side, t], rs_recv.at[side, t])

    def piece(q):
        return pl.ds(pl.multiple_of(q * size, size), size)

    def sketch(offset, slot):
        load(offset, slot).wait()
        j = at(offset)

        @pl.loop(0, PIECES)
        def _(q):
            rows = pl.ds(pl.multiple_of(j * shard + q * size, size), size)
            part[j, piece(q), :] = jnp.dot(s[rows, :], k[...], preferred_element_type=F32)

    def head(side, t, offset, q):
        encode(part[at(offset), piece(q), :], tx.at[side, t])
        sum_copy(side, t).start()

    sketch_copy.wait()
    sketch(order[0], 0)
    pl.semaphore_wait(barrier, chips - 1 + 2 * RING - 1)

    @pl.loop(0, 2)
    def _(i):
        head(0, i, 4, i)
        head(1, i, 4, 2 + i)

    sketch(order[1], 1)

    @pl.loop(0, 2)
    def _(i):
        head(0, 2 + i, 3, 2 + i)

    sketch(order[2], 2)

    @pl.loop(0, 2)
    def _(i):
        head(1, 2 + i, -3, i)

    for slot in range(3, RING):
        sketch(order[slot], slot)

    def turn(side, t):
        pair, i = t // 2, t % 2
        odd = pair % 2
        far = 4 - (pair + 1) // 2
        return far, i + 2 * (odd if side == 0 else 1 - odd)

    @pl.loop(0, EVENTS - 4)
    def _(t):
        for side in range(2):
            far, q = turn(side, t)
            j = at((1 - 2 * side) * (far - 1))
            sum_copy(side, t).wait_recv()
            encode(part[j, piece(q), :] + decode(rx.at[side, t]), tx.at[side, t + 4])
            sum_copy(side, t + 4).start()

    def gather_copy(side, e, j, q):
        block = everyone.at[j, piece(q), :]
        return ring(side, block, block, ag_send.at[side, e], ag_recv.at[side, e])

    def gather_piece(side, e):
        hop = jnp.minimum(e // 4 + 1, 4)
        i = jnp.where(e < 12, e % 4, 2 * (e - 12))
        odd = i % 2
        return hop, 2 * (odd if side == 0 else 1 - odd) + i // 2

    @pl.loop(EVENTS - 4, EVENTS - 2)
    def _(t):
        for side in range(2):
            _, q = turn(side, t)
            sum_copy(side, t).wait_recv()
            part[z, piece(q), :] += decode(rx.at[side, t])

    def gram(q):
        both = jnp.concatenate(split(part[z, piece(q), :]), axis=1)
        gg[...] += lax.dot_general(both, both, (((0,), (0,)), ((), ())), preferred_element_type=F32)

    gg[...] = jnp.zeros_like(gg)

    @pl.loop(EVENTS - 2, EVENTS)
    def _(t):
        for side in range(2):
            _, q = turn(side, t)
            sum_copy(side, t).wait_recv()
            mine = part[z, piece(q), :] + decode(rx.at[side, t])
            part[z, piece(q), :] = mine
            everyone[z, piece(q), :] = mine.astype(BF16)
        for side in range(2):
            for odd in range(2):
                e = 2 * (t - (EVENTS - 2)) + odd
                gather_copy(side, e, z, gather_piece(side, e)[1]).start()

        for side in range(2):
            gram(turn(side, t)[1])

    g[...] = gg[:rank, :rank] + gg[:rank, rank:] + gg[rank:, :rank] + gg[rank:, rank:]

    def block_of(index):
        return pl.ds(pl.multiple_of(index * own, own), own)

    def plane_copy(step, src, dst, send, recv, slot):
        return pltpu.make_async_remote_copy(
            src_ref=src,
            dst_ref=dst,
            send_sem=send.at[step],
            recv_sem=recv.at[slot],
            device_id=to_chip(step),
            device_id_type=MESH,
        )

    def g1_copy(step, slot):
        return plane_copy(step, g.at[block_of(other_chip(step)), :], g1.at[slot], g1_send, g1_recv, slot)

    def g2_copy(step, slot):
        return pltpu.make_async_remote_copy(
            src_ref=g2.at[spot],
            dst_ref=g2.at[slot],
            send_sem=g2_send.at[step],
            recv_sem=g2_recv.at[slot],
            device_id=to_spot(step),
            device_id_type=MESH,
        )

    def g3_copy(step, slot):
        return plane_copy(step, g3.at[block_of(chip), :], g3.at[block_of(slot), :], g3_send, g3_recv, slot)

    def zr_copy(step, slot):
        return plane_copy(step, pair.at[other_chip(step)], zr.at[slot], zr_send, zr_recv, slot)

    @pl.loop(1, chips)
    def _(step):
        g1_copy(step, chip).start()

    z_sum[...] = jnp.zeros_like(z_sum)

    def project(j, q):
        rows = pl.ds(pl.multiple_of(j * shard + q * size, size), size)
        z_sum[...] += lax.dot_general(
            everyone[j, piece(q), :], s[rows, :], (((0,), (0,)), ((), ())), preferred_element_type=F32
        )

    def gather(e):
        for side in range(2):
            hop, q = gather_piece(side, e)
            j = at(-(1 - 2 * side) * hop)
            gather_copy(side, e, j, q).wait_recv()

            @pl.when((e < 8) | (e == 8) | (e == 10))
            def _():
                gather_copy(side, jnp.where(e < 8, e + 4, 12 + (e - 8) // 2), j, q).start()

        for side in range(2):
            hop, q = gather_piece(side, e)
            project(at(-(1 - 2 * side) * hop), q)

    @pl.loop(0, PIECES)
    def _(q):
        project(z, q)

    gather(0)

    @pl.loop(1, chips)
    def _(step):
        g1_copy(step, other_chip(step)).wait_recv()

    g1[chip] = g[block_of(chip), :]
    g2[spot] = jnp.sum(g1[...], axis=0)

    @pl.loop(1, 2 * RING)
    def _(step):
        g2_copy(step, spot).start()

    @pl.loop(1, 3)
    def _(e):
        gather(e)

    @pl.loop(1, 2 * RING)
    def _(step):
        g2_copy(step, other_spot(step)).wait_recv()

    g3[block_of(chip), :] = jnp.sum(g2[...], axis=0) * (1.0 / total)

    @pl.loop(1, chips)
    def _(step):
        g3_copy(step, chip).start()

    @pl.loop(3, 5)
    def _(e):
        gather(e)

    @pl.loop(1, chips)
    def _(step):
        g3_copy(step, other_chip(step)).wait_recv()

    eye = lax.broadcasted_iota(jnp.int32, (rank, rank), 0) == lax.broadcasted_iota(jnp.int32, (rank, rank), 1)
    full = g3[...]
    diagonal = jnp.where(eye, full, 0.0)
    down = lax.rsqrt(jnp.sum(diagonal, axis=1, keepdims=True))
    across = lax.rsqrt(jnp.sum(diagonal, axis=0, keepdims=True))
    x[...] = jnp.concatenate([full * down * across, jnp.where(eye, down, 0.0)], axis=1)

    @pl.loop(5, EVENTS - 1)
    def _(e):
        gather(e)
        factor_block(x, e - 5)

    gather(EVENTS - 1)

    l1, l2 = split(x[:, rank:])
    z1, z2 = split(z_sum[...])
    term = jnp.dot(
        jnp.concatenate([l1, l2, l1], axis=1),
        jnp.concatenate([z1, z1, z2], axis=0),
        preferred_element_type=F32,
    ) * (1.0 / math.sqrt(total))
    half = own // 2
    z_sum[...] = term
    for c in range(chips):
        rows = z_sum[c * own : (c + 1) * own, :]
        low, high = rows[:half], rows[half:]
        give[c] = jnp.where(core == 0, high, low)
        pair[c] = jnp.where(core == 0, low, high)
    mate = pltpu.make_async_remote_copy(
        src_ref=give,
        dst_ref=take,
        send_sem=mate_send,
        recv_sem=mate_recv,
        device_id={"rows": chip * 2 + 1 - core, "snaps": z},
        device_id_type=MESH,
    )
    mate.start()
    i1, i2 = split(x[:, rank:])
    mate.wait_recv()
    pair[...] += take[...]

    @pl.loop(1, chips)
    def _(step):
        zr_copy(step, chip).start()

    def basis_copy(q):
        return pltpu.make_async_copy(white.at[piece(q), :], basis_hbm.at[piece(q), :], out_sem.at[q])

    @pl.loop(0, PIECES)
    def _(q):
        y1, y2 = split(part[z, piece(q), :])
        white[piece(q), :] = lax.dot_general(
            jnp.concatenate([y1, y1, y2], axis=1),
            jnp.concatenate([i1, i2, i1], axis=1),
            (((1,), (1,)), ((), ())),
            preferred_element_type=F32,
        )
        basis_copy(q).start()

    @pl.loop(1, chips)
    def _(step):
        zr_copy(step, other_chip(step)).wait_recv()

    zr[chip] = pair[chip]
    proj_ref[...] = jnp.sum(zr[...], axis=0)

    @pl.loop(0, EVENTS)
    def _(t):
        for side in range(2):
            sum_copy(side, t).wait_send()
            gather_copy(side, t, z, 0).wait_send()

    @pl.loop(1, chips)
    def _(step):
        g1_copy(step, chip).wait_send()
        g3_copy(step, chip).wait_send()
        zr_copy(step, chip).wait_send()

    @pl.loop(1, 2 * RING)
    def _(step):
        g2_copy(step, spot).wait_send()

    @pl.loop(0, PIECES)
    def _(q):
        basis_copy(q).wait()

    mate.wait_send()


def finish(basis_in, proj_in, basis_out, proj_out, basis_held, proj_held, came, left):
    size = basis_in.shape[0] // PIECES
    rows = [pl.ds(q * size, size) for q in range(PIECES)]
    trips = [(proj_in, proj_held, proj_out)] + [(basis_in.at[q], basis_held.at[q], basis_out.at[q]) for q in rows]
    first = [pltpu.make_async_copy(a, b, came.at[i]) for i, (a, b, _) in enumerate(trips)]
    second = [pltpu.make_async_copy(b, c, left.at[i]) for i, (_, b, c) in enumerate(trips)]
    for copy in first:
        copy.start()
    for came_in, copy in zip(first, second):
        came_in.wait()
        copy.start()
    for copy in second:
        copy.wait()


def local(snapshots, sketch):
    rows, columns = snapshots.shape
    rank = sketch.shape[1]
    chips = lax.axis_size("rows") // 2
    total = rows * lax.axis_size("rows")
    shard = rows // RING
    own = rank // chips
    message = shard // PIECES + 16
    dma = pltpu.SemaphoreType.DMA
    outputs = (
        jax.ShapeDtypeStruct((shard, rank), F32),
        jax.ShapeDtypeStruct((own // 2, columns), F32),
    )
    anywhere = pl.BlockSpec(memory_space=pl.ANY)
    basis, projected = pl.pallas_call(
        functools.partial(kernel, total),
        out_shape=outputs,
        in_specs=[anywhere] * 2,
        out_specs=(anywhere, pl.BlockSpec(memory_space=pltpu.VMEM)),
        scratch_shapes=[
            pltpu.VMEM((rows, columns), BF16),
            pltpu.VMEM((columns, rank), BF16),
            pltpu.VMEM((RING, shard, rank), F32),
            pltpu.VMEM((2, EVENTS, message, rank), BF16),
            pltpu.VMEM((2, EVENTS, message, rank), BF16),
            pltpu.VMEM((RING, shard, rank), BF16),
            pltpu.VMEM((rank, columns), F32),
            pltpu.VMEM((2 * rank, 2 * rank), F32),
            pltpu.VMEM((rank, rank), F32),
            pltpu.VMEM((chips, own, rank), F32),
            pltpu.VMEM((2 * RING, own, rank), F32),
            pltpu.VMEM((rank, rank), F32),
            pltpu.VMEM((rank, 2 * rank), F32),
            pltpu.VMEM((chips, own // 2, columns), F32),
            pltpu.VMEM((chips, own // 2, columns), F32),
            pltpu.VMEM((chips, own // 2, columns), F32),
            pltpu.VMEM((chips, own // 2, columns), F32),
            pltpu.VMEM((shard, rank), F32),
            dma((RING + 1,)),
            dma((2, EVENTS)),
            dma((2, EVENTS)),
            dma((2, EVENTS)),
            dma((2, EVENTS)),
            dma((chips,)),
            dma((chips,)),
            dma((2 * RING,)),
            dma((2 * RING,)),
            dma((chips,)),
            dma((chips,)),
            dma((chips,)),
            dma((chips,)),
            dma,
            dma,
            dma((PIECES,)),
        ],
        compiler_params=pltpu.CompilerParams(
            collective_id=0, has_side_effects=True, vmem_limit_bytes=56 * 1024 * 1024
        ),
    )(snapshots, sketch)
    return pl.pallas_call(
        finish,
        out_shape=outputs,
        in_specs=[anywhere] * 2,
        out_specs=(anywhere, anywhere),
        scratch_shapes=[
            pltpu.VMEM(basis.shape, F32),
            pltpu.VMEM(projected.shape, F32),
            dma((PIECES + 1,)),
            dma((PIECES + 1,)),
        ],
        compiler_params=pltpu.CompilerParams(vmem_limit_bytes=63 * 1024 * 1024),
    )(basis, projected)


def solution(mesh):
    in_specs = (P("rows", "snaps"), P("snaps", None))
    out_specs = (P(("rows", "snaps"), None), P("rows", "snaps"))
    return jax.shard_map(local, mesh=mesh, in_specs=in_specs, out_specs=out_specs, check_vma=False)
```

```python
import functools
import math

import jax
import jax.numpy as jnp
from jax import lax
from jax.experimental import pallas as pl
from jax.experimental.pallas import tpu as pltpu
from jax.sharding import PartitionSpec as P

MESH = pl.DeviceIdType.MESH
HIGHEST = lax.Precision.HIGHEST
F32, BF16 = jnp.float32, jnp.bfloat16

RING = 8
PIECES = 4
EVENTS = 2 * (RING - 1)
SPAN = 120.0
BLOCK = 16


def encode(value, buf):
    rows, rank = value.shape
    groups = value.reshape(rows // 16, 16, rank)
    top = (jnp.max(jnp.abs(groups), axis=0) * 1.01 + 1e-30).astype(BF16)
    buf[rows : rows + 16, :] = top
    gain = SPAN / top.astype(F32)
    buf[0:rows, :] = jnp.exp2(groups * gain[None]).reshape(rows, rank).astype(BF16)


def decode(buf):
    rows, rank = buf.shape[0] - 16, buf.shape[1]
    code = buf[0:rows, :].astype(F32).reshape(rows // 16, 16, rank)
    gain = buf[rows : rows + 16, :].astype(F32) * (1.0 / (SPAN * math.log(2.0)))
    return (jnp.log(code) * gain[None]).reshape(rows, rank)


def split(value):
    high = value.astype(BF16)
    return high, (value - high.astype(F32)).astype(BF16)


def factor_block(x, block):
    rank = x.shape[0]
    first = pl.multiple_of(block * BLOCK, BLOCK)
    shape = (BLOCK, rank)
    panel = x[pl.ds(first, BLOCK), :]
    left, right = panel[:, :rank], panel[:, rank:]
    corner = pltpu.roll(left, lax.rem(rank - first, rank), 1)
    row = lax.broadcasted_iota(jnp.int32, shape, 0)
    lane = lax.broadcasted_iota(jnp.int32, shape, 1)
    columns = [jnp.broadcast_to(corner[:, j : j + 1], shape) for j in range(BLOCK)]

    def spread(value, i):
        return jnp.broadcast_to(value[i : i + 1, :], shape)

    first_pivot = cross = determinant = jnp.zeros(shape, F32)
    for i in range(0, BLOCK, 2):
        one, two = columns[i], columns[i + 1]
        a, b, d = spread(one, i), spread(one, i + 1), spread(two, i + 1)
        det = a * d - b * b
        here = (row == i) | (row == i + 1)
        first_pivot = jnp.where(here, a, first_pivot)
        cross = jnp.where(row == i + 1, b, cross)
        determinant = jnp.where(here, det, determinant)
        if i + 2 == BLOCK:
            break
        inverse = jnp.where(row > i + 1, 1.0 / det, 0.0)
        u, v = (one * d - two * b) * inverse, (two * a - one * b) * inverse
        for j in range(i + 2, BLOCK):
            columns[j] = columns[j] - (u * spread(columns[j], i) + v * spread(columns[j], i + 1))
        left = left - (u * spread(left, i) + v * spread(left, i + 1))
        right = right - (u * spread(right, i) + v * spread(right, i + 1))
    odd = row % 2 == 1
    factor = cross / first_pivot
    scale = jnp.where(odd, first_pivot * lax.rsqrt(first_pivot * determinant), lax.rsqrt(first_pivot))
    left = (left - factor * pltpu.roll(left, 1, 0)) * scale
    right = (right - factor * pltpu.roll(right, 1, 0)) * scale
    whole = jnp.concatenate([left, right], axis=1)
    x[pl.ds(first, BLOCK), :] = whole
    r1, r2 = split(whole)
    r3 = (whole - r1.astype(F32) - r2.astype(F32)).astype(BF16)
    later = jnp.where(lane >= first + BLOCK, left, 0.0)
    l1, l2 = split(later)
    l3 = (later - l1.astype(F32) - l2.astype(F32)).astype(BF16)
    x[...] -= lax.dot_general(
        jnp.concatenate([l1, l1, l2, l1, l2, l3], axis=0),
        jnp.concatenate([r1, r2, r1, r3, r2, r1], axis=0),
        (((0,), (0,)), ((), ())),
        preferred_element_type=F32,
    )


def kernel(
    total, s_hbm, k_hbm, basis_hbm, proj_hbm,
    s, k, part, tx, rx, everyone, z_sum, gg, g, g1, g2, g3, x, give, take, pair, zr, white, shared,
    load_sem, rs_send, rs_recv, ag_send, ag_recv, g1_send, g1_recv, g2_send, g2_recv, g3_send, g3_recv,
    zr_send, zr_recv, mate_send, mate_recv, out_sem,
):
    chips = lax.axis_size("rows") // 2
    r, z = lax.axis_index("rows"), lax.axis_index("snaps")
    chip, core = lax.div(r, 2), lax.rem(r, 2)
    spot = z * 2 + core
    shard = part.shape[1]
    size = shard // PIECES
    rank = k.shape[1]
    own = rank // chips

    def at(step):
        return lax.rem(z + step + RING, RING)

    def load(offset, slot):
        rows = pl.ds(pl.multiple_of(at(offset) * shard, shard), shard)
        return pltpu.make_async_copy(s_hbm.at[rows, :], s.at[rows, :], load_sem.at[slot])

    def order(slot):
        return (RING - slot) // 2 * (1 - 2 * ((slot + 1) % 2)) if slot else RING // 2

    sketch_copy = pltpu.make_async_copy(k_hbm, k, load_sem.at[RING])
    sketch_copy.start()
    load(order(0), 0).start()
    load(order(1), 1).start()

    barrier = pltpu.get_barrier_semaphore()

    def other_chip(step):
        return lax.rem(chip + step, chips)

    def other_spot(step):
        return lax.rem(spot + step, 2 * RING)

    def to_chip(step):
        return {"rows": other_chip(step) * 2 + core, "snaps": z}

    def to_spot(step):
        there = other_spot(step)
        return {"rows": chip * 2 + lax.rem(there, 2), "snaps": lax.div(there, 2)}

    @pl.loop(1, chips)
    def _(step):
        pl.semaphore_signal(barrier, inc=1, device_id=to_chip(step), device_id_type=MESH)

    @pl.loop(1, 2 * RING)
    def _(step):
        pl.semaphore_signal(barrier, inc=1, device_id=to_spot(step), device_id_type=MESH)

    def ring(side, src, dst, send, recv):
        return pltpu.make_async_remote_copy(
            src_ref=src,
            dst_ref=dst,
            send_sem=send,
            recv_sem=recv,
            device_id={"rows": r, "snaps": at(1 - 2 * side)},
            device_id_type=MESH,
        )

    def sum_copy(side, t):
        return ring(side, tx.at[side, t], rx.at[side, t], rs_send.at[side, t], rs_recv.at[side, t])

    def piece(q):
        return pl.ds(pl.multiple_of(q * size, size), size)

    def sketch(slot):
        if slot + 2 < RING:
            load(order(slot + 2), slot + 2).start()
        load(order(slot), slot).wait()
        j = at(order(slot))
        rows = pl.ds(pl.multiple_of(j * shard, shard), shard)
        part[j] = jnp.dot(s[rows, :], k[...], preferred_element_type=F32)

    def head(side, t, offset, q):
        encode(part[at(offset), piece(q), :], tx.at[side, t])
        sum_copy(side, t).start()

    sketch_copy.wait()
    sketch(0)
    pl.semaphore_wait(barrier, chips - 1 + 2 * RING - 1)

    @pl.loop(0, 2)
    def _(i):
        head(0, i, 4, i)
        head(1, i, 4, 2 + i)

    sketch(1)

    @pl.loop(0, 2)
    def _(i):
        head(0, 2 + i, 3, 2 + i)

    sketch(2)

    @pl.loop(0, 2)
    def _(i):
        head(1, 2 + i, -3, i)

    for slot in range(3, RING):
        sketch(slot)

    def turn(side, t):
        pair, i = t // 2, t % 2
        odd = pair % 2
        far = 4 - (pair + 1) // 2
        return far, i + 2 * (odd if side == 0 else 1 - odd)

    @pl.loop(0, EVENTS - 4)
    def _(t):
        for side in range(2):
            far, q = turn(side, t)
            j = at((1 - 2 * side) * (far - 1))
            sum_copy(side, t).wait_recv()
            encode(part[j, piece(q), :] + decode(rx.at[side, t]), tx.at[side, t + 4])
            sum_copy(side, t + 4).start()

    def gather_copy(side, e, j, q):
        block = everyone.at[j, piece(q), :]
        return ring(side, block, block, ag_send.at[side, e], ag_recv.at[side, e])

    def gather_piece(side, e):
        hop = jnp.minimum(e // 4 + 1, 4)
        i = jnp.where(e < 12, e % 4, 2 * (e - 12))
        odd = i % 2
        return hop, 2 * (odd if side == 0 else 1 - odd) + i // 2

    @pl.loop(EVENTS - 4, EVENTS - 2)
    def _(t):
        for side in range(2):
            _, q = turn(side, t)
            sum_copy(side, t).wait_recv()
            part[z, piece(q), :] += decode(rx.at[side, t])

    def gram(pieces):
        rows = jnp.concatenate([part[z, piece(q), :] for q in pieces], axis=0)
        both = jnp.concatenate(split(rows), axis=1)
        gg[...] += lax.dot_general(both, both, (((0,), (0,)), ((), ())), preferred_element_type=F32)

    gg[...] = jnp.zeros_like(gg)

    @pl.loop(EVENTS - 2, EVENTS)
    def _(t):
        for side in range(2):
            _, q = turn(side, t)
            sum_copy(side, t).wait_recv()
            mine = part[z, piece(q), :] + decode(rx.at[side, t])
            part[z, piece(q), :] = mine
            everyone[z, piece(q), :] = mine.astype(BF16)
        for side in range(2):
            for odd in range(2):
                e = 2 * (t - (EVENTS - 2)) + odd
                gather_copy(side, e, z, gather_piece(side, e)[1]).start()

        gram([turn(side, t)[1] for side in range(2)])

    g[...] = gg[:rank, :rank] + gg[:rank, rank:] + gg[rank:, :rank] + gg[rank:, rank:]

    def block_of(index):
        return pl.ds(pl.multiple_of(index * own, own), own)

    def plane_copy(step, src, dst, send, recv, slot):
        return pltpu.make_async_remote_copy(
            src_ref=src,
            dst_ref=dst,
            send_sem=send.at[step],
            recv_sem=recv.at[slot],
            device_id=to_chip(step),
            device_id_type=MESH,
        )

    def g1_copy(step, slot):
        return plane_copy(step, g.at[block_of(other_chip(step)), :], g1.at[slot], g1_send, g1_recv, slot)

    def g2_copy(step, slot):
        return pltpu.make_async_remote_copy(
            src_ref=g2.at[spot],
            dst_ref=g2.at[slot],
            send_sem=g2_send.at[step],
            recv_sem=g2_recv.at[slot],
            device_id=to_spot(step),
            device_id_type=MESH,
        )

    def g3_copy(step, slot):
        return plane_copy(step, g3.at[block_of(chip), :], g3.at[block_of(slot), :], g3_send, g3_recv, slot)

    def zr_copy(step, slot):
        return plane_copy(step, pair.at[other_chip(step)], zr.at[slot], zr_send, zr_recv, slot)

    @pl.loop(1, chips)
    def _(step):
        g1_copy(step, chip).start()

    def term_of(pairs):
        left = [everyone[j, piece(q), :] for j, q in pairs]
        right = [s[pl.ds(pl.multiple_of(j * shard + q * size, size), size), :] for j, q in pairs]
        return lax.dot_general(
            jnp.concatenate(left, axis=0),
            jnp.concatenate(right, axis=0),
            (((0,), (0,)), ((), ())),
            preferred_element_type=F32,
        )

    def gather(e):
        came = []
        for side in range(2):
            hop, q = gather_piece(side, e)
            j = at(-(1 - 2 * side) * hop)
            came.append((j, q))
            gather_copy(side, e, j, q).wait_recv()

            @pl.when((e < 8) | (e == 8) | (e == 10))
            def _():
                gather_copy(side, jnp.where(e < 8, e + 4, 12 + (e - 8) // 2), j, q).start()

        z_sum[...] += term_of(came)

    z_sum[...] = term_of([(z, q) for q in range(PIECES)])
    gather(0)

    @pl.loop(1, chips)
    def _(step):
        g1_copy(step, other_chip(step)).wait_recv()

    g1[chip] = g[block_of(chip), :]
    g2[spot] = jnp.sum(g1[...], axis=0)

    @pl.loop(1, 2 * RING)
    def _(step):
        g2_copy(step, spot).start()

    @pl.loop(1, 3)
    def _(e):
        gather(e)

    @pl.loop(1, 2 * RING)
    def _(step):
        g2_copy(step, other_spot(step)).wait_recv()

    g3[block_of(chip), :] = jnp.sum(g2[...], axis=0) * (1.0 / total)

    @pl.loop(1, chips)
    def _(step):
        g3_copy(step, chip).start()

    @pl.loop(3, 5)
    def _(e):
        gather(e)

    @pl.loop(1, chips)
    def _(step):
        g3_copy(step, other_chip(step)).wait_recv()

    eye = lax.broadcasted_iota(jnp.int32, (rank, rank), 0) == lax.broadcasted_iota(jnp.int32, (rank, rank), 1)
    full = g3[...]
    diagonal = jnp.where(eye, full, 0.0)
    down = lax.rsqrt(jnp.sum(diagonal, axis=1, keepdims=True))
    across = lax.rsqrt(jnp.sum(diagonal, axis=0, keepdims=True))
    x[...] = jnp.concatenate([full * down * across, jnp.where(eye, down, 0.0)], axis=1)

    @pl.loop(5, EVENTS - 1)
    def _(e):
        gather(e)
        factor_block(x, e - 5)

    gather(EVENTS - 1)

    l1, l2 = split(x[:, rank:])
    z1, z2 = split(z_sum[...])
    term = jnp.dot(
        jnp.concatenate([l1, l2, l1], axis=1),
        jnp.concatenate([z1, z1, z2], axis=0),
        preferred_element_type=F32,
    ) * (1.0 / math.sqrt(total))
    half = own // 2
    z_sum[...] = term
    for c in range(chips):
        rows = z_sum[c * own : (c + 1) * own, :]
        low, high = rows[:half], rows[half:]
        give[c] = jnp.where(core == 0, high, low)
        pair[c] = jnp.where(core == 0, low, high)
    mate = pltpu.make_async_remote_copy(
        src_ref=give,
        dst_ref=take,
        send_sem=mate_send,
        recv_sem=mate_recv,
        device_id={"rows": chip * 2 + 1 - core, "snaps": z},
        device_id_type=MESH,
    )
    mate.start()
    i1, i2 = split(x[:, rank:])
    mate.wait_recv()
    pair[...] += take[...]

    @pl.loop(1, chips)
    def _(step):
        zr_copy(step, chip).start()

    def basis_copy(q):
        return pltpu.make_async_copy(white.at[piece(q), :], basis_hbm.at[piece(q), :], out_sem.at[q])

    @pl.loop(0, PIECES)
    def _(q):
        y1, y2 = split(part[z, piece(q), :])
        white[piece(q), :] = lax.dot_general(
            jnp.concatenate([y1, y1, y2], axis=1),
            jnp.concatenate([i1, i2, i1], axis=1),
            (((1,), (1,)), ((), ())),
            preferred_element_type=F32,
        )
        basis_copy(q).start()

    mate.wait_send()

    @pl.loop(0, EVENTS)
    def _(t):
        for side in range(2):
            sum_copy(side, t).wait_send()
            gather_copy(side, t, z, 0).wait_send()

    @pl.loop(1, chips)
    def _(step):
        g1_copy(step, chip).wait_send()
        g3_copy(step, chip).wait_send()

    @pl.loop(1, 2 * RING)
    def _(step):
        g2_copy(step, spot).wait_send()

    @pl.loop(1, chips)
    def _(step):
        zr_copy(step, other_chip(step)).wait_recv()

    zr[chip] = pair[chip]
    shared[...] = jnp.sum(zr[...], axis=0)
    proj_copy = pltpu.make_async_copy(shared, proj_hbm, out_sem.at[PIECES])
    proj_copy.start()

    @pl.loop(1, chips)
    def _(step):
        zr_copy(step, chip).wait_send()

    @pl.loop(0, PIECES)
    def _(q):
        basis_copy(q).wait()

    proj_copy.wait()


def finish(basis_in, proj_in, basis_out, proj_out, basis_held, proj_held, came, left):
    size = basis_in.shape[0] // PIECES
    rows = [pl.ds(q * size, size) for q in range(PIECES)]
    trips = [(proj_in, proj_held, proj_out)] + [(basis_in.at[q], basis_held.at[q], basis_out.at[q]) for q in rows]
    first = [pltpu.make_async_copy(a, b, came.at[i]) for i, (a, b, _) in enumerate(trips)]
    second = [pltpu.make_async_copy(b, c, left.at[i]) for i, (_, b, c) in enumerate(trips)]
    for copy in first:
        copy.start()
    for came_in, copy in zip(first, second):
        came_in.wait()
        copy.start()
    for copy in second:
        copy.wait()


def local(snapshots, sketch):
    rows, columns = snapshots.shape
    rank = sketch.shape[1]
    chips = lax.axis_size("rows") // 2
    total = rows * lax.axis_size("rows")
    shard = rows // RING
    own = rank // chips
    message = shard // PIECES + 16
    dma = pltpu.SemaphoreType.DMA
    outputs = (
        jax.ShapeDtypeStruct((shard, rank), F32),
        jax.ShapeDtypeStruct((own // 2, columns), F32),
    )
    anywhere = pl.BlockSpec(memory_space=pl.ANY)
    basis, projected = pl.pallas_call(
        functools.partial(kernel, total),
        out_shape=outputs,
        in_specs=[anywhere] * 2,
        out_specs=(anywhere, anywhere),
        scratch_shapes=[
            pltpu.VMEM((rows, columns), BF16),
            pltpu.VMEM((columns, rank), BF16),
            pltpu.VMEM((RING, shard, rank), F32),
            pltpu.VMEM((2, EVENTS, message, rank), BF16),
            pltpu.VMEM((2, EVENTS, message, rank), BF16),
            pltpu.VMEM((RING, shard, rank), BF16),
            pltpu.VMEM((rank, columns), F32),
            pltpu.VMEM((2 * rank, 2 * rank), F32),
            pltpu.VMEM((rank, rank), F32),
            pltpu.VMEM((chips, own, rank), F32),
            pltpu.VMEM((2 * RING, own, rank), F32),
            pltpu.VMEM((rank, rank), F32),
            pltpu.VMEM((rank, 2 * rank), F32),
            pltpu.VMEM((chips, own // 2, columns), F32),
            pltpu.VMEM((chips, own // 2, columns), F32),
            pltpu.VMEM((chips, own // 2, columns), F32),
            pltpu.VMEM((chips, own // 2, columns), F32),
            pltpu.VMEM((shard, rank), F32),
            pltpu.VMEM((own // 2, columns), F32),
            dma((RING + 1,)),
            dma((2, EVENTS)),
            dma((2, EVENTS)),
            dma((2, EVENTS)),
            dma((2, EVENTS)),
            dma((chips,)),
            dma((chips,)),
            dma((2 * RING,)),
            dma((2 * RING,)),
            dma((chips,)),
            dma((chips,)),
            dma((chips,)),
            dma((chips,)),
            dma,
            dma,
            dma((PIECES + 1,)),
        ],
        compiler_params=pltpu.CompilerParams(
            collective_id=0, has_side_effects=True, vmem_limit_bytes=56 * 1024 * 1024
        ),
    )(snapshots, sketch)
    return pl.pallas_call(
        finish,
        out_shape=outputs,
        in_specs=[anywhere] * 2,
        out_specs=(anywhere, anywhere),
        scratch_shapes=[
            pltpu.VMEM(basis.shape, F32),
            pltpu.VMEM(projected.shape, F32),
            dma((PIECES + 1,)),
            dma((PIECES + 1,)),
        ],
        compiler_params=pltpu.CompilerParams(vmem_limit_bytes=63 * 1024 * 1024),
    )(basis, projected)


def solution(mesh):
    in_specs = (P("rows", "snaps"), P("snaps", None))
    out_specs = (P(("rows", "snaps"), None), P("rows", "snaps"))
    return jax.shard_map(local, mesh=mesh, in_specs=in_specs, out_specs=out_specs, check_vma=False)
```

```python
import functools
import math

import jax
import jax.numpy as jnp
from jax import lax
from jax.experimental import pallas as pl
from jax.experimental.pallas import tpu as pltpu
from jax.sharding import PartitionSpec as P

MESH = pl.DeviceIdType.MESH
HIGHEST = lax.Precision.HIGHEST
F32, BF16 = jnp.float32, jnp.bfloat16

RING = 8
PIECES = 4
EVENTS = 2 * (RING - 1)
SPAN = 120.0
BLOCK = 16


def groups_of(value):
    rows, rank = value.shape
    return value.reshape(rows // 16, 16, rank)


def peak(value):
    return jnp.max(jnp.abs(groups_of(value)), axis=0)


def encode(value, top):
    gain = SPAN / top.astype(F32)
    return jnp.exp2(groups_of(value) * gain[None]).reshape(value.shape).astype(BF16)


def decode(code, top):
    gain = top.astype(F32) * (1.0 / (SPAN * math.log(2.0)))
    return (jnp.log(groups_of(code.astype(F32))) * gain[None]).reshape(code.shape)


def split(value):
    high = value.astype(BF16)
    return high, (value - high.astype(F32)).astype(BF16)


def factor_block(x, block):
    rank = x.shape[0]
    first = pl.multiple_of(block * BLOCK, BLOCK)
    shape = (BLOCK, rank)
    panel = x[pl.ds(first, BLOCK), :]
    left, right = panel[:, :rank], panel[:, rank:]
    corner = pltpu.roll(left, lax.rem(rank - first, rank), 1)
    row = lax.broadcasted_iota(jnp.int32, shape, 0)
    lane = lax.broadcasted_iota(jnp.int32, shape, 1)
    columns = [jnp.broadcast_to(corner[:, j : j + 1], shape) for j in range(BLOCK)]

    def spread(value, i):
        return jnp.broadcast_to(value[i : i + 1, :], shape)

    first_pivot = cross = determinant = jnp.zeros(shape, F32)
    for i in range(0, BLOCK, 2):
        one, two = columns[i], columns[i + 1]
        a, b, d = spread(one, i), spread(one, i + 1), spread(two, i + 1)
        det = a * d - b * b
        here = (row == i) | (row == i + 1)
        first_pivot = jnp.where(here, a, first_pivot)
        cross = jnp.where(row == i + 1, b, cross)
        determinant = jnp.where(here, det, determinant)
        if i + 2 == BLOCK:
            break
        inverse = jnp.where(row > i + 1, 1.0 / det, 0.0)
        u, v = (one * d - two * b) * inverse, (two * a - one * b) * inverse
        for j in range(i + 2, BLOCK):
            columns[j] = columns[j] - (u * spread(columns[j], i) + v * spread(columns[j], i + 1))
        left = left - (u * spread(left, i) + v * spread(left, i + 1))
        right = right - (u * spread(right, i) + v * spread(right, i + 1))
    odd = row % 2 == 1
    factor = cross / first_pivot
    scale = jnp.where(odd, first_pivot * lax.rsqrt(first_pivot * determinant), lax.rsqrt(first_pivot))
    left = (left - factor * pltpu.roll(left, 1, 0)) * scale
    right = (right - factor * pltpu.roll(right, 1, 0)) * scale
    whole = jnp.concatenate([left, right], axis=1)
    x[pl.ds(first, BLOCK), :] = whole
    r1, r2 = split(whole)
    r3 = (whole - r1.astype(F32) - r2.astype(F32)).astype(BF16)
    later = jnp.where(lane >= first + BLOCK, left, 0.0)
    l1, l2 = split(later)
    l3 = (later - l1.astype(F32) - l2.astype(F32)).astype(BF16)
    x[...] -= lax.dot_general(
        jnp.concatenate([l1, l1, l2, l1, l2, l3], axis=0),
        jnp.concatenate([r1, r2, r1, r3, r2, r1], axis=0),
        (((0,), (0,)), ((), ())),
        preferred_element_type=F32,
    )


def kernel(
    total, s_hbm, k_hbm, basis_ref, proj_ref,
    s, k, part, tx, rx, everyone, z_sum, gg, g, g0, g1, g2, g3, x, give, take, pair, zr,
    load_sem, rs_send, rs_recv, ag_send, ag_recv, g1_sem, g2_sem, g3_sem, zr_sem, mate_send, mate_recv,
):
    count = lax.axis_size("rows")
    chips = count // 2
    r, z = lax.axis_index("rows"), lax.axis_index("snaps")
    chip, core = lax.div(r, 2), lax.rem(r, 2)
    shard = part.shape[1]
    size = shard // PIECES
    rank = k.shape[1]
    own = rank // chips
    half = rank // count

    def wrap(index, length):
        index = jnp.where(index >= length, index - length, index)
        return jnp.where(index < 0, index + length, index)

    def at(step):
        return wrap(z + step, RING)

    def load(offset, slot, part_of=0, parts=1):
        length = shard // parts
        rows = pl.ds(pl.multiple_of(at(offset) * shard + part_of * length, length), length)
        return pltpu.make_async_copy(s_hbm.at[rows, :], s.at[rows, :], load_sem.at[slot])

    def order(slot):
        return (RING - slot) // 2 * (1 - 2 * ((slot + 1) % 2)) if slot else RING // 2

    sketch_copy = pltpu.make_async_copy(k_hbm, k, load_sem.at[RING])
    sketch_copy.start()
    for side in range(2):
        load(order(0), side * (RING + 1), side, 2).start()
    load(order(1), 1).start()

    barrier = pltpu.get_barrier_semaphore()

    def other_chip(step):
        return wrap(chip + step, chips)

    def other_row(step):
        return wrap(r + step, count)

    def to_chip(step):
        return {"rows": other_chip(step) * 2 + core, "snaps": z}

    def to_row(step):
        return {"rows": other_row(step), "snaps": z}

    def to_depth(step):
        return {"rows": r, "snaps": at(step)}

    @pl.loop(1, count)
    def _(step):
        pl.semaphore_signal(barrier, inc=1, device_id=to_row(step), device_id_type=MESH)

    @pl.loop(1, RING)
    def _(step):
        pl.semaphore_signal(barrier, inc=1, device_id=to_depth(step), device_id_type=MESH)

    def ring(side, src, dst, send, recv):
        return pltpu.make_async_remote_copy(
            src_ref=src,
            dst_ref=dst,
            send_sem=send,
            recv_sem=recv,
            device_id={"rows": r, "snaps": at(1 - 2 * side)},
            device_id_type=MESH,
        )

    def span_of(i):
        return pl.ds(0, size + 16) if i == 0 else pl.ds(size + 16, size)

    def data_of(i):
        return pl.ds(0, size) if i == 0 else pl.ds(size + 16, size)

    scale_rows = pl.ds(size, 16)

    def sum_copy(side, u, i):
        return ring(
            side,
            tx.at[side, u, span_of(i), :],
            rx.at[side, u, span_of(i), :],
            rs_send.at[side],
            rs_recv.at[side, 2 * u + i],
        )

    def piece(q):
        return pl.ds(pl.multiple_of(q * size, size), size)

    def sketch(slot):
        if slot + 2 < RING:
            load(order(slot + 2), slot + 2).start()
        load(order(slot), slot).wait()
        j = at(order(slot))
        rows = pl.ds(pl.multiple_of(j * shard, shard), shard)
        part[j] = jnp.dot(s[rows, :], k[...], preferred_element_type=F32)

    def pair_rows(j, side, u):
        first = 2 * size * (u % 2 if side == 0 else 1 - u % 2)
        return j, pl.ds(pl.multiple_of(first, 2 * size), 2 * size)

    def piece_rows(j, side, u, i):
        first = 2 * size * (u % 2 if side == 0 else 1 - u % 2) + i * size
        return j, pl.ds(pl.multiple_of(first, size), size)

    def set_scale(side, u, top):
        tx[side, u, scale_rows, :] = (top * 1.01 + 1e-30).astype(BF16)

    def send(side, u, i, value):
        tx[side, u, data_of(i), :] = encode(value, tx[side, u, scale_rows, :])
        sum_copy(side, u, i).start()

    def came(side, u, i):
        return decode(rx[side, u, data_of(i), :], rx[side, u, scale_rows, :])

    def head(side, u, offset):
        j = at(offset)
        set_scale(side, u, peak(part[pair_rows(j, side, u)]))
        for i in range(2):
            send(side, u, i, part[piece_rows(j, side, u, i)])

    sketch_copy.wait()
    load(order(2), 2).start()
    for side in range(2):
        load(order(0), side * (RING + 1), side, 2).wait()
        first = side * 2 * size
        rows = pl.ds(pl.multiple_of(at(order(0)) * shard + first, 2 * size), 2 * size)
        part[at(order(0)), pl.ds(first, 2 * size), :] = jnp.dot(s[rows, :], k[...], preferred_element_type=F32)
        if side == 0:
            pl.semaphore_wait(barrier, count - 1 + RING - 1)
        head(side, 0, 4)
    for side in range(2):
        sketch(1 + side)
        head(side, 1, 3 - 6 * side)
    for slot in range(3, RING):
        sketch(slot)

    @pl.loop(0, RING - 3)
    def _(u):
        far = 4 - (u + 1) // 2
        for i in range(2):
            for side in range(2):
                j = at((1 - 2 * side) * (far - 1))
                sum_copy(side, u, i).wait_recv()
                if i == 0:
                    set_scale(side, u + 2, rx[side, u, scale_rows, :].astype(F32) + peak(part[pair_rows(j, side, u)]))
                send(side, u + 2, i, part[piece_rows(j, side, u, i)] + came(side, u, i))

    def gather_copy(side, e, j, q):
        block = everyone.at[j, piece(q), :]
        return ring(side, block, block, ag_send, ag_recv.at[side, e])

    def gather_piece(side, e):
        hop = jnp.minimum(e // 4 + 1, 4)
        i = jnp.where(e < 12, e % 4, 2 * (e - 12))
        odd = i % 2
        return hop, 2 * (odd if side == 0 else 1 - odd) + i // 2

    def gram(pieces):
        rows = jnp.concatenate([part[z, piece(q), :] for q in pieces], axis=0)
        both = jnp.concatenate(split(rows), axis=1)
        gg[...] += lax.dot_general(both, both, (((0,), (0,)), ((), ())), preferred_element_type=F32)

    gg[...] = jnp.zeros_like(gg)
    for i in range(2):
        for side in range(2):
            sum_copy(side, RING - 3, i).wait_recv()
            part[piece_rows(z, side, RING - 3, i)] += came(side, RING - 3, i)
    for i in range(2):
        for side in range(2):
            sum_copy(side, RING - 2, i).wait_recv()
            mine = part[piece_rows(z, side, RING - 2, i)] + came(side, RING - 2, i)
            part[piece_rows(z, side, RING - 2, i)] = mine
            everyone[piece_rows(z, side, RING - 2, i)] = mine.astype(BF16)
        for side in range(2):
            for odd in range(2):
                e = 2 * i + odd
                gather_copy(side, e, z, gather_piece(side, e)[1]).start()
        gram((i, 2 + i))

    g[...] = gg[:rank, :rank] + gg[:rank, rank:] + gg[rank:, :rank] + gg[rank:, rank:]
    for index in range(count):
        g0[index] = g[index * half : (index + 1) * half, :]

    def remote(src, dst, send_sem, recv_sem, there):
        return pltpu.make_async_remote_copy(
            src_ref=src,
            dst_ref=dst,
            send_sem=send_sem,
            recv_sem=recv_sem,
            device_id=there,
            device_id_type=MESH,
        )

    def g1_copy(step):
        return remote(g0.at[other_row(step)], g1.at[step], g1_sem.at[0], g1_sem.at[1], to_row(step))

    def g2_copy(step):
        return remote(g2.at[z], g2.at[z], g2_sem.at[0], g2_sem.at[1], to_depth(step))

    def g3_copy(step):
        return remote(g3.at[r], g3.at[r], g3_sem.at[0], g3_sem.at[1], to_row(step))

    def zr_copy(step):
        return remote(pair.at[other_chip(step)], zr.at[step], zr_sem.at[0], zr_sem.at[1], to_chip(step))

    def all_of(ref, number, sem):
        block = ref.at[pl.ds(0, number)]
        return remote(block, block, sem.at[0], sem.at[1], to_row(1))

    def start_all(copy, number):
        for step in range(1, number):
            copy(step).start()

    start_all(g1_copy, count)

    def term_of(pairs):
        left = [everyone[j, piece(q), :] for j, q in pairs]
        right = [s[pl.ds(pl.multiple_of(j * shard + q * size, size), size), :] for j, q in pairs]
        return lax.dot_general(
            jnp.concatenate(left, axis=0),
            jnp.concatenate(right, axis=0),
            (((0,), (0,)), ((), ())),
            preferred_element_type=F32,
        )

    def gather(e):
        came = []
        for side in range(2):
            hop, q = gather_piece(side, e)
            j = at(-(1 - 2 * side) * hop)
            came.append((j, q))
            gather_copy(side, e, j, q).wait_recv()

            @pl.when((e < 8) | (e == 8) | (e == 10))
            def _():
                gather_copy(side, jnp.where(e < 8, e + 4, 12 + (e - 8) // 2), j, q).start()

        z_sum[...] += term_of(came)

    z_sum[...] = term_of([(z, q) for q in range(PIECES)])
    gather(0)
    all_of(g1, count - 1, g1_sem).wait_recv()
    g1[0] = g0[r]
    g2[z] = jnp.sum(g1[...], axis=0)
    start_all(g2_copy, RING)

    @pl.loop(1, 3)
    def _(e):
        gather(e)

    all_of(g2, RING - 1, g2_sem).wait_recv()
    g3[r] = jnp.sum(g2[...], axis=0) * (1.0 / total)
    start_all(g3_copy, count)
    gather(3)
    all_of(g3, count - 1, g3_sem).wait_recv()
    for index in range(count):
        g[index * half : (index + 1) * half, :] = g3[index]

    eye = lax.broadcasted_iota(jnp.int32, (rank, rank), 0) == lax.broadcasted_iota(jnp.int32, (rank, rank), 1)
    full = g[...]
    diagonal = jnp.where(eye, full, 0.0)
    down = lax.rsqrt(jnp.sum(diagonal, axis=1, keepdims=True))
    across = lax.rsqrt(jnp.sum(diagonal, axis=0, keepdims=True))
    x[...] = jnp.concatenate([full * down * across, jnp.where(eye, down, 0.0)], axis=1)

    @pl.loop(4, EVENTS - 2)
    def _(e):
        gather(e)
        factor_block(x, e - 4)

    @pl.loop(EVENTS - 2, EVENTS)
    def _(e):
        gather(e)

    l1, l2 = split(x[:, rank:])
    z1, z2 = split(z_sum[...])
    term = jnp.dot(
        jnp.concatenate([l1, l2, l1], axis=1),
        jnp.concatenate([z1, z1, z2], axis=0),
        preferred_element_type=F32,
    ) * (1.0 / math.sqrt(total))
    z_sum[...] = term
    for c in range(chips):
        rows = z_sum[c * own : (c + 1) * own, :]
        low, high = rows[:half], rows[half:]
        give[c] = jnp.where(core == 0, high, low)
        pair[c] = jnp.where(core == 0, low, high)
    mate = remote(give, take, mate_send, mate_recv, {"rows": chip * 2 + 1 - core, "snaps": z})
    mate.start()
    i1, i2 = split(x[:, rank:])
    mate.wait_recv()
    pair[...] += take[...]

    start_all(zr_copy, chips)

    @pl.loop(0, PIECES)
    def _(q):
        y1, y2 = split(part[z, piece(q), :])
        basis_ref[piece(q), :] = lax.dot_general(
            jnp.concatenate([y1, y1, y2], axis=1),
            jnp.concatenate([i1, i2, i1], axis=1),
            (((1,), (1,)), ((), ())),
            preferred_element_type=F32,
        )

    mate.wait_send()

    for side in range(2):
        ring(side, tx.at[side], tx.at[side], rs_send.at[side], rs_recv.at[side, 0]).wait_send()
    sent = everyone.at[pl.ds(0, RING - 1)]
    ring(0, sent, sent, ag_send, ag_recv.at[0, 0]).wait_send()
    all_of(g1, count - 1, g1_sem).wait_send()
    all_of(g2, RING - 1, g2_sem).wait_send()
    all_of(g3, count - 1, g3_sem).wait_send()

    all_of(zr, chips - 1, zr_sem).wait_recv()
    zr[0] = pair[chip]
    proj_ref[...] = jnp.sum(zr[...], axis=0)
    all_of(zr, chips - 1, zr_sem).wait_send()


def finish(basis_in, proj_in, basis_out, proj_out, sem):
    copies = [pltpu.make_async_copy(proj_in, proj_out, sem.at[0])]
    size = basis_in.shape[0] // PIECES
    for q in range(PIECES):
        rows = pl.ds(q * size, size)
        copies.append(pltpu.make_async_copy(basis_in.at[rows, :], basis_out.at[rows, :], sem.at[1 + q]))
    for copy in copies:
        copy.start()
    for copy in copies:
        copy.wait()


def local(snapshots, sketch):
    rows, columns = snapshots.shape
    rank = sketch.shape[1]
    count = lax.axis_size("rows")
    chips = count // 2
    total = rows * count
    shard = rows // RING
    half = rank // count
    message = 2 * (shard // PIECES) + 16
    dma = pltpu.SemaphoreType.DMA
    outputs = (
        jax.ShapeDtypeStruct((shard, rank), F32),
        jax.ShapeDtypeStruct((half, columns), F32),
    )
    anywhere = pl.BlockSpec(memory_space=pl.ANY)
    basis, projected = pl.pallas_call(
        functools.partial(kernel, total),
        out_shape=tuple(pltpu.VMEM(out.shape, out.dtype) for out in outputs),
        in_specs=[anywhere] * 2,
        out_specs=(pl.BlockSpec(memory_space=pltpu.VMEM),) * 2,
        scratch_shapes=[
            pltpu.VMEM((rows, columns), BF16),
            pltpu.VMEM((columns, rank), BF16),
            pltpu.VMEM((RING, shard, rank), F32),
            pltpu.VMEM((2, RING - 1, message, rank), BF16),
            pltpu.VMEM((2, RING - 1, message, rank), BF16),
            pltpu.VMEM((RING, shard, rank), BF16),
            pltpu.VMEM((rank, columns), F32),
            pltpu.VMEM((2 * rank, 2 * rank), F32),
            pltpu.VMEM((rank, rank), F32),
            pltpu.VMEM((count, half, rank), F32),
            pltpu.VMEM((count, half, rank), F32),
            pltpu.VMEM((RING, half, rank), F32),
            pltpu.VMEM((count, half, rank), F32),
            pltpu.VMEM((rank, 2 * rank), F32),
            pltpu.VMEM((chips, half, columns), F32),
            pltpu.VMEM((chips, half, columns), F32),
            pltpu.VMEM((chips, half, columns), F32),
            pltpu.VMEM((chips, half, columns), F32),
            dma((RING + 2,)),
            dma((2,)),
            dma((2, EVENTS)),
            dma,
            dma((2, EVENTS)),
            dma((2,)),
            dma((2,)),
            dma((2,)),
            dma((2,)),
            dma,
            dma,
        ],
        compiler_params=pltpu.CompilerParams(
            collective_id=0, has_side_effects=True, vmem_limit_bytes=56 * 1024 * 1024
        ),
    )(snapshots, sketch)
    return pl.pallas_call(
        finish,
        out_shape=outputs,
        in_specs=[pl.BlockSpec(memory_space=pltpu.VMEM)] * 2,
        out_specs=(anywhere, anywhere),
        scratch_shapes=[dma((PIECES + 1,))],
        compiler_params=pltpu.CompilerParams(vmem_limit_bytes=16 * 1024 * 1024),
    )(basis, projected)


def solution(mesh):
    in_specs = (P("rows", "snaps"), P("snaps", None))
    out_specs = (P(("rows", "snaps"), None), P("rows", "snaps"))
    return jax.shard_map(local, mesh=mesh, in_specs=in_specs, out_specs=out_specs, check_vma=False)
```

```python
import functools
import math

import jax
import jax.numpy as jnp
from jax import lax
from jax.experimental import pallas as pl
from jax.experimental.pallas import tpu as pltpu
from jax.sharding import PartitionSpec as P

MESH = pl.DeviceIdType.MESH
HIGHEST = lax.Precision.HIGHEST
F32, BF16 = jnp.float32, jnp.bfloat16

RING = 8
PIECES = 4
EVENTS = 2 * (RING - 1)
SPAN = 120.0
BLOCK = 16


def groups_of(value):
    rows, rank = value.shape
    return value.reshape(rows // 16, 16, rank)


def peak(value):
    return jnp.max(jnp.abs(groups_of(value)), axis=0)


def encode(value, top):
    gain = SPAN / top.astype(F32)
    return jnp.exp2(groups_of(value) * gain[None]).reshape(value.shape).astype(BF16)


def decode(code, top):
    gain = top.astype(F32) * (1.0 / (SPAN * math.log(2.0)))
    return (jnp.log(groups_of(code.astype(F32))) * gain[None]).reshape(code.shape)


def split(value):
    high = value.astype(BF16)
    return high, (value - high.astype(F32)).astype(BF16)


def factor_block(x, block):
    rank = x.shape[0]
    first = pl.multiple_of(block * BLOCK, BLOCK)
    shape = (BLOCK, rank)
    panel = x[pl.ds(first, BLOCK), :]
    left, right = panel[:, :rank], panel[:, rank:]
    corner = pltpu.roll(left, lax.rem(rank - first, rank), 1)
    row = lax.broadcasted_iota(jnp.int32, shape, 0)
    lane = lax.broadcasted_iota(jnp.int32, shape, 1)
    columns = [jnp.broadcast_to(corner[:, j : j + 1], shape) for j in range(BLOCK)]

    def spread(value, i):
        return jnp.broadcast_to(value[i : i + 1, :], shape)

    first_pivot = cross = determinant = jnp.zeros(shape, F32)
    for i in range(0, BLOCK, 2):
        one, two = columns[i], columns[i + 1]
        a, b, d = spread(one, i), spread(one, i + 1), spread(two, i + 1)
        det = a * d - b * b
        here = (row == i) | (row == i + 1)
        first_pivot = jnp.where(here, a, first_pivot)
        cross = jnp.where(row == i + 1, b, cross)
        determinant = jnp.where(here, det, determinant)
        if i + 2 == BLOCK:
            break
        inverse = jnp.where(row > i + 1, 1.0 / det, 0.0)
        u, v = (one * d - two * b) * inverse, (two * a - one * b) * inverse
        for j in range(i + 2, BLOCK):
            columns[j] = columns[j] - (u * spread(columns[j], i) + v * spread(columns[j], i + 1))
        left = left - (u * spread(left, i) + v * spread(left, i + 1))
        right = right - (u * spread(right, i) + v * spread(right, i + 1))
    odd = row % 2 == 1
    factor = cross / first_pivot
    scale = jnp.where(odd, first_pivot * lax.rsqrt(first_pivot * determinant), lax.rsqrt(first_pivot))
    left = (left - factor * pltpu.roll(left, 1, 0)) * scale
    right = (right - factor * pltpu.roll(right, 1, 0)) * scale
    whole = jnp.concatenate([left, right], axis=1)
    x[pl.ds(first, BLOCK), :] = whole
    r1, r2 = split(whole)
    r3 = (whole - r1.astype(F32) - r2.astype(F32)).astype(BF16)
    later = jnp.where(lane >= first + BLOCK, left, 0.0)
    l1, l2 = split(later)
    l3 = (later - l1.astype(F32) - l2.astype(F32)).astype(BF16)
    x[...] -= lax.dot_general(
        jnp.concatenate([l1, l1, l2, l1, l2, l3], axis=0),
        jnp.concatenate([r1, r2, r1, r3, r2, r1], axis=0),
        (((0,), (0,)), ((), ())),
        preferred_element_type=F32,
    )


def kernel(
    total, s_hbm, k_hbm, basis_ref, proj_ref,
    s, k, part, tx, rx, everyone, z_sum, gg, g, g0, g1, g2, g3, x, give, take, pair, zr,
    load_sem, rs_send, rs_recv, ag_send, ag_recv, g1_sem, g2_sem, g3_sem, zr_sem, mate_send, mate_recv,
):
    count = lax.axis_size("rows")
    chips = count // 2
    r, z = lax.axis_index("rows"), lax.axis_index("snaps")
    chip, core = lax.div(r, 2), lax.rem(r, 2)
    shard = part.shape[1]
    size = shard // PIECES
    rank = k.shape[1]
    own = rank // chips
    half = rank // count

    def wrap(index, length):
        index = jnp.where(index >= length, index - length, index)
        return jnp.where(index < 0, index + length, index)

    sense = 1 - 2 * core

    def at(step):
        return wrap(z + sense * step, RING)

    def load(offset, slot, part_of=0, parts=1):
        length = shard // parts
        rows = pl.ds(pl.multiple_of(at(offset) * shard + part_of * length, length), length)
        return pltpu.make_async_copy(s_hbm.at[rows, :], s.at[rows, :], load_sem.at[slot])

    def order(slot):
        return (RING - slot) // 2 * (1 - 2 * ((slot + 1) % 2)) if slot else RING // 2

    sketch_copy = pltpu.make_async_copy(k_hbm, k, load_sem.at[RING])
    sketch_copy.start()
    for side in range(2):
        load(order(0), side * (RING + 1), side, 2).start()
    load(order(1), 1).start()

    barrier = pltpu.get_barrier_semaphore()

    def other_chip(step):
        return wrap(chip + step, chips)

    def other_row(step):
        return wrap(r + step, count)

    def to_chip(step):
        return {"rows": other_chip(step) * 2 + core, "snaps": z}

    def to_row(step):
        return {"rows": other_row(step), "snaps": z}

    def to_depth(step):
        return {"rows": r, "snaps": at(step)}

    for there in [to_depth(step) for step in range(1, RING)] + [to_row(step) for step in range(1, count)]:
        pl.semaphore_signal(barrier, inc=1, device_id=there, device_id_type=MESH)

    def ring(side, src, dst, send, recv):
        return pltpu.make_async_remote_copy(
            src_ref=src,
            dst_ref=dst,
            send_sem=send,
            recv_sem=recv,
            device_id={"rows": r, "snaps": at(1 - 2 * side)},
            device_id_type=MESH,
        )

    def span_of(i):
        return pl.ds(0, size + 16) if i == 0 else pl.ds(size + 16, size)

    def data_of(i):
        return pl.ds(0, size) if i == 0 else pl.ds(size + 16, size)

    scale_rows = pl.ds(size, 16)

    def sum_copy(side, u, i):
        return ring(
            side,
            tx.at[side, u, span_of(i), :],
            rx.at[side, u, span_of(i), :],
            rs_send.at[side],
            rs_recv.at[side, 2 * u + i],
        )

    def piece(q):
        return pl.ds(pl.multiple_of(q * size, size), size)

    def sketch(slot):
        if slot + 2 < RING:
            load(order(slot + 2), slot + 2).start()
        load(order(slot), slot).wait()
        j = at(order(slot))
        rows = pl.ds(pl.multiple_of(j * shard, shard), shard)
        part[j] = jnp.dot(s[rows, :], k[...], preferred_element_type=F32)

    def pair_rows(j, side, u):
        first = 2 * size * (u % 2 if side == 0 else 1 - u % 2)
        return j, pl.ds(pl.multiple_of(first, 2 * size), 2 * size)

    def piece_rows(j, side, u, i):
        first = 2 * size * (u % 2 if side == 0 else 1 - u % 2) + i * size
        return j, pl.ds(pl.multiple_of(first, size), size)

    def set_scale(side, u, top):
        tx[side, u, scale_rows, :] = (top * 1.01 + 1e-30).astype(BF16)

    def send(side, u, i, value):
        tx[side, u, data_of(i), :] = encode(value, tx[side, u, scale_rows, :])
        sum_copy(side, u, i).start()

    def came(side, u, i):
        return decode(rx[side, u, data_of(i), :], rx[side, u, scale_rows, :])

    def head(side, u, offset):
        j = at(offset)
        set_scale(side, u, peak(part[pair_rows(j, side, u)]))
        for i in range(2):
            send(side, u, i, part[piece_rows(j, side, u, i)])

    sketch_copy.wait()
    load(order(2), 2).start()
    for side in range(2):
        load(order(0), side * (RING + 1), side, 2).wait()
        first = side * 2 * size
        rows = pl.ds(pl.multiple_of(at(order(0)) * shard + first, 2 * size), 2 * size)
        part[at(order(0)), pl.ds(first, 2 * size), :] = jnp.dot(s[rows, :], k[...], preferred_element_type=F32)
        if side == 0:
            pl.semaphore_wait(barrier, count - 1 + RING - 1)
        head(side, 0, 4)
    for side in range(2):
        sketch(1 + side)
        head(side, 1, 3 - 6 * side)
    for slot in range(3, RING):
        sketch(slot)

    @pl.loop(0, RING - 3)
    def _(u):
        far = 4 - (u + 1) // 2
        for i in range(2):
            for side in range(2):
                j = at((1 - 2 * side) * (far - 1))
                sum_copy(side, u, i).wait_recv()
                if i == 0:
                    set_scale(side, u + 2, rx[side, u, scale_rows, :].astype(F32) + peak(part[pair_rows(j, side, u)]))
                send(side, u + 2, i, part[piece_rows(j, side, u, i)] + came(side, u, i))

    def gather_copy(side, e, j, q):
        block = everyone.at[j, piece(q), :]
        return ring(side, block, block, ag_send, ag_recv.at[side, e])

    def gather_piece(side, e):
        hop = jnp.minimum(e // 4 + 1, 4)
        i = jnp.where(e < 12, e % 4, 2 * (e - 12))
        odd = i % 2
        return hop, 2 * (odd if side == 0 else 1 - odd) + i // 2

    def gram(pieces):
        rows = jnp.concatenate([part[z, piece(q), :] for q in pieces], axis=0)
        both = jnp.concatenate(split(rows), axis=1)
        gg[...] += lax.dot_general(both, both, (((0,), (0,)), ((), ())), preferred_element_type=F32)

    gg[...] = jnp.zeros_like(gg)
    for i in range(2):
        for side in range(2):
            sum_copy(side, RING - 3, i).wait_recv()
            part[piece_rows(z, side, RING - 3, i)] += came(side, RING - 3, i)
    for i in range(2):
        for side in range(2):
            sum_copy(side, RING - 2, i).wait_recv()
            mine = part[piece_rows(z, side, RING - 2, i)] + came(side, RING - 2, i)
            part[piece_rows(z, side, RING - 2, i)] = mine
            everyone[piece_rows(z, side, RING - 2, i)] = mine.astype(BF16)
        for side in range(2):
            for odd in range(2):
                e = 2 * i + odd
                gather_copy(side, e, z, gather_piece(side, e)[1]).start()
        gram((i, 2 + i))

    g[...] = gg[:rank, :rank] + gg[:rank, rank:] + gg[rank:, :rank] + gg[rank:, rank:]
    for index in range(count):
        g0[index] = g[index * half : (index + 1) * half, :]

    def remote(src, dst, send_sem, recv_sem, there):
        return pltpu.make_async_remote_copy(
            src_ref=src,
            dst_ref=dst,
            send_sem=send_sem,
            recv_sem=recv_sem,
            device_id=there,
            device_id_type=MESH,
        )

    def g1_copy(step):
        return remote(g0.at[other_row(step)], g1.at[step], g1_sem.at[0], g1_sem.at[1], to_row(step))

    def g2_copy(step):
        return remote(g2.at[z], g2.at[z], g2_sem.at[0], g2_sem.at[1], to_depth(step))

    def g3_copy(step):
        return remote(g3.at[r], g3.at[r], g3_sem.at[0], g3_sem.at[1], to_row(step))

    def zr_copy(step):
        return remote(pair.at[other_chip(step)], zr.at[step], zr_sem.at[0], zr_sem.at[1], to_chip(step))

    def all_of(ref, number, sem):
        block = ref.at[pl.ds(0, number)]
        return remote(block, block, sem.at[0], sem.at[1], to_row(1))

    def start_all(copy, number):
        for step in range(1, number):
            copy(step).start()

    start_all(g1_copy, count)

    def term_of(pairs):
        left = [everyone[j, piece(q), :] for j, q in pairs]
        right = [s[pl.ds(pl.multiple_of(j * shard + q * size, size), size), :] for j, q in pairs]
        return lax.dot_general(
            jnp.concatenate(left, axis=0),
            jnp.concatenate(right, axis=0),
            (((0,), (0,)), ((), ())),
            preferred_element_type=F32,
        )

    def gather(e):
        came = []
        for side in range(2):
            hop, q = gather_piece(side, e)
            j = at(-(1 - 2 * side) * hop)
            came.append((j, q))
            gather_copy(side, e, j, q).wait_recv()

            @pl.when((e < 8) | (e == 8) | (e == 10))
            def _():
                gather_copy(side, jnp.where(e < 8, e + 4, 12 + (e - 8) // 2), j, q).start()

        z_sum[...] += term_of(came)

    z_sum[...] = term_of([(z, q) for q in range(PIECES)])
    gather(0)
    all_of(g1, count - 1, g1_sem).wait_recv()
    g1[0] = g0[r]
    g2[z] = jnp.sum(g1[...], axis=0)
    start_all(g2_copy, RING)

    @pl.loop(1, 3)
    def _(e):
        gather(e)

    all_of(g2, RING - 1, g2_sem).wait_recv()
    g3[r] = jnp.sum(g2[...], axis=0) * (1.0 / total)
    start_all(g3_copy, count)
    gather(3)
    all_of(g3, count - 1, g3_sem).wait_recv()
    for index in range(count):
        g[index * half : (index + 1) * half, :] = g3[index]

    eye = lax.broadcasted_iota(jnp.int32, (rank, rank), 0) == lax.broadcasted_iota(jnp.int32, (rank, rank), 1)
    full = g[...]
    diagonal = jnp.where(eye, full, 0.0)
    down = lax.rsqrt(jnp.sum(diagonal, axis=1, keepdims=True))
    across = lax.rsqrt(jnp.sum(diagonal, axis=0, keepdims=True))
    x[...] = jnp.concatenate([full * down * across, jnp.where(eye, down, 0.0)], axis=1)

    @pl.loop(4, EVENTS - 2)
    def _(e):
        gather(e)
        factor_block(x, e - 4)

    @pl.loop(EVENTS - 2, EVENTS)
    def _(e):
        gather(e)

    l1, l2 = split(x[:, rank:])
    z1, z2 = split(z_sum[...])
    term = jnp.dot(
        jnp.concatenate([l1, l2, l1], axis=1),
        jnp.concatenate([z1, z1, z2], axis=0),
        preferred_element_type=F32,
    ) * (1.0 / math.sqrt(total))
    z_sum[...] = term
    for c in range(chips):
        rows = z_sum[c * own : (c + 1) * own, :]
        low, high = rows[:half], rows[half:]
        give[c] = jnp.where(core == 0, high, low)
        pair[c] = jnp.where(core == 0, low, high)
    mate = remote(give, take, mate_send, mate_recv, {"rows": chip * 2 + 1 - core, "snaps": z})
    mate.start()
    i1, i2 = split(x[:, rank:])
    mate.wait_recv()
    pair[...] += take[...]

    start_all(zr_copy, chips)

    @pl.loop(0, PIECES)
    def _(q):
        y1, y2 = split(part[z, piece(q), :])
        basis_ref[piece(q), :] = lax.dot_general(
            jnp.concatenate([y1, y1, y2], axis=1),
            jnp.concatenate([i1, i2, i1], axis=1),
            (((1,), (1,)), ((), ())),
            preferred_element_type=F32,
        )

    mate.wait_send()

    for side in range(2):
        ring(side, tx.at[side], tx.at[side], rs_send.at[side], rs_recv.at[side, 0]).wait_send()
    sent = everyone.at[pl.ds(0, RING - 1)]
    ring(0, sent, sent, ag_send, ag_recv.at[0, 0]).wait_send()
    all_of(g1, count - 1, g1_sem).wait_send()
    all_of(g2, RING - 1, g2_sem).wait_send()
    all_of(g3, count - 1, g3_sem).wait_send()

    all_of(zr, chips - 1, zr_sem).wait_recv()
    zr[0] = pair[chip]
    proj_ref[...] = jnp.sum(zr[...], axis=0)
    all_of(zr, chips - 1, zr_sem).wait_send()


def finish(basis_in, proj_in, basis_out, proj_out, sem):
    copies = [pltpu.make_async_copy(proj_in, proj_out, sem.at[0])]
    size = basis_in.shape[0] // PIECES
    for q in range(PIECES):
        rows = pl.ds(q * size, size)
        copies.append(pltpu.make_async_copy(basis_in.at[rows, :], basis_out.at[rows, :], sem.at[1 + q]))
    for copy in copies:
        copy.start()
    for copy in copies:
        copy.wait()


def local(snapshots, sketch):
    rows, columns = snapshots.shape
    rank = sketch.shape[1]
    count = lax.axis_size("rows")
    chips = count // 2
    total = rows * count
    shard = rows // RING
    half = rank // count
    message = 2 * (shard // PIECES) + 16
    dma = pltpu.SemaphoreType.DMA
    outputs = (
        jax.ShapeDtypeStruct((shard, rank), F32),
        jax.ShapeDtypeStruct((half, columns), F32),
    )
    anywhere = pl.BlockSpec(memory_space=pl.ANY)
    basis, projected = pl.pallas_call(
        functools.partial(kernel, total),
        out_shape=tuple(pltpu.VMEM(out.shape, out.dtype) for out in outputs),
        in_specs=[anywhere] * 2,
        out_specs=(pl.BlockSpec(memory_space=pltpu.VMEM),) * 2,
        scratch_shapes=[
            pltpu.VMEM((rows, columns), BF16),
            pltpu.VMEM((columns, rank), BF16),
            pltpu.VMEM((RING, shard, rank), F32),
            pltpu.VMEM((2, RING - 1, message, rank), BF16),
            pltpu.VMEM((2, RING - 1, message, rank), BF16),
            pltpu.VMEM((RING, shard, rank), BF16),
            pltpu.VMEM((rank, columns), F32),
            pltpu.VMEM((2 * rank, 2 * rank), F32),
            pltpu.VMEM((rank, rank), F32),
            pltpu.VMEM((count, half, rank), F32),
            pltpu.VMEM((count, half, rank), F32),
            pltpu.VMEM((RING, half, rank), F32),
            pltpu.VMEM((count, half, rank), F32),
            pltpu.VMEM((rank, 2 * rank), F32),
            pltpu.VMEM((chips, half, columns), F32),
            pltpu.VMEM((chips, half, columns), F32),
            pltpu.VMEM((chips, half, columns), F32),
            pltpu.VMEM((chips, half, columns), F32),
            dma((RING + 2,)),
            dma((2,)),
            dma((2, EVENTS)),
            dma,
            dma((2, EVENTS)),
            dma((2,)),
            dma((2,)),
            dma((2,)),
            dma((2,)),
            dma,
            dma,
        ],
        compiler_params=pltpu.CompilerParams(
            collective_id=0, has_side_effects=True, vmem_limit_bytes=56 * 1024 * 1024
        ),
    )(snapshots, sketch)
    return pl.pallas_call(
        finish,
        out_shape=outputs,
        in_specs=[pl.BlockSpec(memory_space=pltpu.VMEM)] * 2,
        out_specs=(anywhere, anywhere),
        scratch_shapes=[dma((PIECES + 1,))],
        compiler_params=pltpu.CompilerParams(vmem_limit_bytes=16 * 1024 * 1024),
    )(basis, projected)


def solution(mesh):
    in_specs = (P("rows", "snaps"), P("snaps", None))
    out_specs = (P(("rows", "snaps"), None), P("rows", "snaps"))
    return jax.shard_map(local, mesh=mesh, in_specs=in_specs, out_specs=out_specs, check_vma=False)
```

```python
import functools
import math

import jax
import jax.numpy as jnp
from jax import lax
from jax.experimental import pallas as pl
from jax.experimental.pallas import tpu as pltpu
from jax.sharding import PartitionSpec as P

MESH = pl.DeviceIdType.MESH
HIGHEST = lax.Precision.HIGHEST
F32, BF16 = jnp.float32, jnp.bfloat16

RING = 8
PIECES = 4
EVENTS = 2 * (RING - 1)
SPAN = 120.0
BLOCK = 16


def groups_of(value):
    rows, rank = value.shape
    return value.reshape(rows // 16, 16, rank)


def peak(value):
    return jnp.max(jnp.abs(groups_of(value)), axis=0)


def encode(value, top):
    gain = SPAN / top.astype(F32)
    return jnp.exp2(groups_of(value) * gain[None]).reshape(value.shape).astype(BF16)


def decode(code, top):
    gain = top.astype(F32) * (1.0 / (SPAN * math.log(2.0)))
    return (jnp.log(groups_of(code.astype(F32))) * gain[None]).reshape(code.shape)


def split(value):
    high = value.astype(BF16)
    return high, (value - high.astype(F32)).astype(BF16)


def factor_block(x, block):
    rank = x.shape[0]
    first = pl.multiple_of(block * BLOCK, BLOCK)
    shape = (BLOCK, rank)
    panel = x[pl.ds(first, BLOCK), :]
    left, right = panel[:, :rank], panel[:, rank:]
    corner = pltpu.roll(left, lax.rem(rank - first, rank), 1)
    row = lax.broadcasted_iota(jnp.int32, shape, 0)
    lane = lax.broadcasted_iota(jnp.int32, shape, 1)
    columns = [jnp.broadcast_to(corner[:, j : j + 1], shape) for j in range(BLOCK)]

    def spread(value, i):
        return jnp.broadcast_to(value[i : i + 1, :], shape)

    first_pivot = cross = determinant = jnp.zeros(shape, F32)
    for i in range(0, BLOCK, 2):
        one, two = columns[i], columns[i + 1]
        a, b, d = spread(one, i), spread(one, i + 1), spread(two, i + 1)
        det = a * d - b * b
        here = (row == i) | (row == i + 1)
        first_pivot = jnp.where(here, a, first_pivot)
        cross = jnp.where(row == i + 1, b, cross)
        determinant = jnp.where(here, det, determinant)
        if i + 2 == BLOCK:
            break
        inverse = jnp.where(row > i + 1, 1.0 / det, 0.0)
        u, v = (one * d - two * b) * inverse, (two * a - one * b) * inverse
        for j in range(i + 2, BLOCK):
            columns[j] = columns[j] - (u * spread(columns[j], i) + v * spread(columns[j], i + 1))
        left = left - (u * spread(left, i) + v * spread(left, i + 1))
        right = right - (u * spread(right, i) + v * spread(right, i + 1))
    odd = row % 2 == 1
    factor = cross / first_pivot
    scale = jnp.where(odd, first_pivot * lax.rsqrt(first_pivot * determinant), lax.rsqrt(first_pivot))
    left = (left - factor * pltpu.roll(left, 1, 0)) * scale
    right = (right - factor * pltpu.roll(right, 1, 0)) * scale
    whole = jnp.concatenate([left, right], axis=1)
    x[pl.ds(first, BLOCK), :] = whole
    r1, r2 = split(whole)
    r3 = (whole - r1.astype(F32) - r2.astype(F32)).astype(BF16)
    later = jnp.where(lane >= first + BLOCK, left, 0.0)
    l1, l2 = split(later)
    l3 = (later - l1.astype(F32) - l2.astype(F32)).astype(BF16)
    x[...] -= lax.dot_general(
        jnp.concatenate([l1, l1, l2, l1, l2, l3], axis=0),
        jnp.concatenate([r1, r2, r1, r3, r2, r1], axis=0),
        (((0,), (0,)), ((), ())),
        preferred_element_type=F32,
    )


def kernel(
    total, s_hbm, k_hbm, basis_ref, proj_ref,
    s, k, part, tx, rx, everyone, z_sum, gg, g, g0, g1, g2, g3, x, give, take, pair, zr,
    load_sem, rs_send, rs_recv, ag_send, ag_recv, g1_sem, g2_sem, g3_sem, zr_sem, mate_send, mate_recv,
):
    count = lax.axis_size("rows")
    chips = count // 2
    r, z = lax.axis_index("rows"), lax.axis_index("snaps")
    chip, core = lax.div(r, 2), lax.rem(r, 2)
    shard = part.shape[1]
    size = shard // PIECES
    rank = k.shape[1]
    own = rank // chips
    half = rank // count

    def wrap(index, length):
        index = jnp.where(index >= length, index - length, index)
        return jnp.where(index < 0, index + length, index)

    def at(step):
        return wrap(z + step, RING)

    def load(offset, slot, part_of=0, parts=1):
        length = shard // parts
        rows = pl.ds(pl.multiple_of(at(offset) * shard + part_of * length, length), length)
        return pltpu.make_async_copy(s_hbm.at[rows, :], s.at[rows, :], load_sem.at[slot])

    def order(slot):
        return (RING - slot) // 2 * (1 - 2 * ((slot + 1) % 2)) if slot else RING // 2

    sketch_copy = pltpu.make_async_copy(k_hbm, k, load_sem.at[RING])
    sketch_copy.start()
    for side in range(2):
        load(order(0), side * (RING + 1), side, 2).start()
    load(order(1), 1).start()

    barrier = pltpu.get_barrier_semaphore()

    def other_chip(step):
        return wrap(chip + step, chips)

    def other_row(step):
        return wrap(r + step, count)

    def to_chip(step):
        return {"rows": other_chip(step) * 2 + core, "snaps": z}

    def to_row(step):
        return {"rows": other_row(step), "snaps": z}

    def to_depth(step):
        return {"rows": r, "snaps": at(step)}

    @pl.loop(1, count)
    def _(step):
        pl.semaphore_signal(barrier, inc=1, device_id=to_row(step), device_id_type=MESH)

    @pl.loop(1, RING)
    def _(step):
        pl.semaphore_signal(barrier, inc=1, device_id=to_depth(step), device_id_type=MESH)

    def ring(side, src, dst, send, recv):
        return pltpu.make_async_remote_copy(
            src_ref=src,
            dst_ref=dst,
            send_sem=send,
            recv_sem=recv,
            device_id={"rows": r, "snaps": at(1 - 2 * side)},
            device_id_type=MESH,
        )

    def span_of(i):
        return pl.ds(0, size + 16) if i == 0 else pl.ds(size + 16, size)

    def data_of(i):
        return pl.ds(0, size) if i == 0 else pl.ds(size + 16, size)

    scale_rows = pl.ds(size, 16)

    def sum_copy(side, u, i):
        return ring(
            side,
            tx.at[side, u, span_of(i), :],
            rx.at[side, u, span_of(i), :],
            rs_send.at[side],
            rs_recv.at[side, 2 * u + i],
        )

    def piece(q):
        return pl.ds(pl.multiple_of(q * size, size), size)

    def sketch(slot):
        if slot + 2 < RING:
            load(order(slot + 2), slot + 2).start()
        load(order(slot), slot).wait()
        j = at(order(slot))
        rows = pl.ds(pl.multiple_of(j * shard, shard), shard)
        part[j] = jnp.dot(s[rows, :], k[...], preferred_element_type=F32)

    def pair_rows(j, side, u):
        first = 2 * size * (u % 2 if side == 0 else 1 - u % 2)
        return j, pl.ds(pl.multiple_of(first, 2 * size), 2 * size)

    def piece_rows(j, side, u, i):
        first = 2 * size * (u % 2 if side == 0 else 1 - u % 2) + i * size
        return j, pl.ds(pl.multiple_of(first, size), size)

    def set_scale(side, u, top):
        tx[side, u, scale_rows, :] = (top * 1.01 + 1e-30).astype(BF16)

    def set_data(side, u, i, value):
        tx[side, u, data_of(i), :] = encode(value, tx[side, u, scale_rows, :])

    def send(side, u, i, value):
        set_data(side, u, i, value)
        sum_copy(side, u, i).start()

    def came(side, u, i):
        return decode(rx[side, u, data_of(i), :], rx[side, u, scale_rows, :])

    def head(side, u, offset):
        j = at(offset)
        set_scale(side, u, peak(part[pair_rows(j, side, u)]))
        for i in range(2):
            send(side, u, i, part[piece_rows(j, side, u, i)])

    sketch_copy.wait()
    load(order(2), 2).start()
    for side in range(2):
        load(order(0), side * (RING + 1), side, 2).wait()
        first = side * 2 * size
        rows = pl.ds(pl.multiple_of(at(order(0)) * shard + first, 2 * size), 2 * size)
        part[at(order(0)), pl.ds(first, 2 * size), :] = jnp.dot(s[rows, :], k[...], preferred_element_type=F32)
        j = at(4)
        set_scale(side, 0, peak(part[pair_rows(j, side, 0)]))
        for i in range(2):
            set_data(side, 0, i, part[piece_rows(j, side, 0, i)])
        if side == 0:
            pl.semaphore_wait(barrier, count - 1 + RING - 1)
        for i in range(2):
            sum_copy(side, 0, i).start()
    for side in range(2):
        sketch(1 + side)
        head(side, 1, 3 - 6 * side)
    for slot in range(3, RING):
        sketch(slot)

    @pl.loop(0, RING - 3)
    def _(u):
        far = 4 - (u + 1) // 2
        for i in range(2):
            for side in range(2):
                j = at((1 - 2 * side) * (far - 1))
                sum_copy(side, u, i).wait_recv()
                if i == 0:
                    set_scale(side, u + 2, rx[side, u, scale_rows, :].astype(F32) + peak(part[pair_rows(j, side, u)]))
                send(side, u + 2, i, part[piece_rows(j, side, u, i)] + came(side, u, i))

    def gather_copy(side, e, j, q):
        block = everyone.at[j, piece(q), :]
        return ring(side, block, block, ag_send, ag_recv.at[side, e])

    def gather_piece(side, e):
        hop = jnp.minimum(e // 4 + 1, 4)
        i = jnp.where(e < 12, e % 4, 2 * (e - 12))
        odd = i % 2
        return hop, 2 * (odd if side == 0 else 1 - odd) + i // 2

    def start_own(i):
        for side in range(2):
            for odd in range(2):
                e = 2 * i + odd
                gather_copy(side, e, z, gather_piece(side, e)[1]).start()

    def gram(pieces):
        rows = jnp.concatenate([part[z, piece(q), :] for q in pieces], axis=0)
        both = jnp.concatenate(split(rows), axis=1)
        gg[...] += lax.dot_general(both, both, (((0,), (0,)), ((), ())), preferred_element_type=F32)

    gg[...] = jnp.zeros_like(gg)
    for i in range(2):
        for side in range(2):
            sum_copy(side, RING - 3, i).wait_recv()
            part[piece_rows(z, side, RING - 3, i)] += came(side, RING - 3, i)
    for i in range(2):
        for side in range(2):
            sum_copy(side, RING - 2, i).wait_recv()
            mine = part[piece_rows(z, side, RING - 2, i)] + came(side, RING - 2, i)
            part[piece_rows(z, side, RING - 2, i)] = mine
            everyone[piece_rows(z, side, RING - 2, i)] = mine.astype(BF16)
        if i == 0:
            start_own(0)
        gram((i, 2 + i))

    g[...] = gg[:rank, :rank] + gg[:rank, rank:] + gg[rank:, :rank] + gg[rank:, rank:]
    for index in range(count):
        g0[index] = g[index * half : (index + 1) * half, :]

    def remote(src, dst, send_sem, recv_sem, there):
        return pltpu.make_async_remote_copy(
            src_ref=src,
            dst_ref=dst,
            send_sem=send_sem,
            recv_sem=recv_sem,
            device_id=there,
            device_id_type=MESH,
        )

    def g1_copy(step):
        return remote(g0.at[other_row(step)], g1.at[step], g1_sem.at[0], g1_sem.at[1], to_row(step))

    def g2_copy(step):
        return remote(g2.at[z], g2.at[z], g2_sem.at[0], g2_sem.at[1], to_depth(step))

    def g3_copy(step):
        return remote(g3.at[r], g3.at[r], g3_sem.at[0], g3_sem.at[1], to_row(step))

    def zr_copy(step):
        return remote(pair.at[other_chip(step)], zr.at[step], zr_sem.at[0], zr_sem.at[1], to_chip(step))

    def all_of(ref, number, sem):
        block = ref.at[pl.ds(0, number)]
        return remote(block, block, sem.at[0], sem.at[1], to_row(1))

    def start_all(copy, number):
        for step in range(1, number):
            copy(step).start()

    start_all(g1_copy, count)
    start_own(1)

    def term_of(pairs):
        left = [everyone[j, piece(q), :] for j, q in pairs]
        right = [s[pl.ds(pl.multiple_of(j * shard + q * size, size), size), :] for j, q in pairs]
        return lax.dot_general(
            jnp.concatenate(left, axis=0),
            jnp.concatenate(right, axis=0),
            (((0,), (0,)), ((), ())),
            preferred_element_type=F32,
        )

    def gather(e):
        came = []
        for side in range(2):
            hop, q = gather_piece(side, e)
            j = at(-(1 - 2 * side) * hop)
            came.append((j, q))
            gather_copy(side, e, j, q).wait_recv()

            @pl.when((e < 8) | (e == 8) | (e == 10))
            def _():
                gather_copy(side, jnp.where(e < 8, e + 4, 12 + (e - 8) // 2), j, q).start()

        return term_of(came)

    z_sum[...] = term_of([(z, q) for q in range(PIECES)])
    all_of(g1, count - 1, g1_sem).wait_recv()
    g1[0] = g0[r]
    g2[z] = jnp.sum(g1[...], axis=0)
    start_all(g2_copy, RING)

    @pl.loop(0, 2)
    def _(e):
        z_sum[...] += gather(e)

    all_of(g2, RING - 1, g2_sem).wait_recv()
    g3[r] = jnp.sum(g2[...], axis=0) * (1.0 / total)
    start_all(g3_copy, count)

    @pl.loop(2, 4)
    def _(e):
        z_sum[...] += gather(e)

    all_of(g3, count - 1, g3_sem).wait_recv()
    for index in range(count):
        g[index * half : (index + 1) * half, :] = g3[index]

    eye = lax.broadcasted_iota(jnp.int32, (rank, rank), 0) == lax.broadcasted_iota(jnp.int32, (rank, rank), 1)
    full = g[...]
    diagonal = jnp.where(eye, full, 0.0)
    down = lax.rsqrt(jnp.sum(diagonal, axis=1, keepdims=True))
    across = lax.rsqrt(jnp.sum(diagonal, axis=0, keepdims=True))
    x[...] = jnp.concatenate([full * down * across, jnp.where(eye, down, 0.0)], axis=1)

    @pl.loop(4, EVENTS - 2)
    def _(e):
        z_sum[...] += gather(e)
        factor_block(x, e - 4)

    z_sum[...] += gather(EVENTS - 2)

    l1, l2 = split(x[:, rank:])
    z1, z2 = split(z_sum[...] + gather(EVENTS - 1))
    term = jnp.dot(
        jnp.concatenate([l1, l2, l1], axis=1),
        jnp.concatenate([z1, z1, z2], axis=0),
        preferred_element_type=F32,
    ) * (1.0 / math.sqrt(total))
    z_sum[...] = term
    for c in range(chips):
        rows = z_sum[c * own : (c + 1) * own, :]
        low, high = rows[:half], rows[half:]
        give[c] = jnp.where(core == 0, high, low)
        pair[c] = jnp.where(core == 0, low, high)
    mate = remote(give, take, mate_send, mate_recv, {"rows": chip * 2 + 1 - core, "snaps": z})
    mate.start()
    i1, i2 = split(x[:, rank:])
    mate.wait_recv()
    pair[...] += take[...]

    start_all(zr_copy, chips)

    @pl.loop(0, PIECES)
    def _(q):
        y1, y2 = split(part[z, piece(q), :])
        basis_ref[piece(q), :] = lax.dot_general(
            jnp.concatenate([y1, y1, y2], axis=1),
            jnp.concatenate([i1, i2, i1], axis=1),
            (((1,), (1,)), ((), ())),
            preferred_element_type=F32,
        )

    mate.wait_send()

    for side in range(2):
        ring(side, tx.at[side], tx.at[side], rs_send.at[side], rs_recv.at[side, 0]).wait_send()
    sent = everyone.at[pl.ds(0, RING - 1)]
    ring(0, sent, sent, ag_send, ag_recv.at[0, 0]).wait_send()
    all_of(g1, count - 1, g1_sem).wait_send()
    all_of(g2, RING - 1, g2_sem).wait_send()
    all_of(g3, count - 1, g3_sem).wait_send()

    all_of(zr, chips - 1, zr_sem).wait_recv()
    zr[0] = pair[chip]
    proj_ref[...] = jnp.sum(zr[...], axis=0)
    all_of(zr, chips - 1, zr_sem).wait_send()


def finish(basis_in, proj_in, basis_out, proj_out, sem):
    copies = [pltpu.make_async_copy(proj_in, proj_out, sem.at[0])]
    size = basis_in.shape[0] // PIECES
    for q in range(PIECES):
        rows = pl.ds(q * size, size)
        copies.append(pltpu.make_async_copy(basis_in.at[rows, :], basis_out.at[rows, :], sem.at[1 + q]))
    for copy in copies:
        copy.start()
    for copy in copies:
        copy.wait()


def local(snapshots, sketch):
    rows, columns = snapshots.shape
    rank = sketch.shape[1]
    count = lax.axis_size("rows")
    chips = count // 2
    total = rows * count
    shard = rows // RING
    half = rank // count
    message = 2 * (shard // PIECES) + 16
    dma = pltpu.SemaphoreType.DMA
    outputs = (
        jax.ShapeDtypeStruct((shard, rank), F32),
        jax.ShapeDtypeStruct((half, columns), F32),
    )
    anywhere = pl.BlockSpec(memory_space=pl.ANY)
    basis, projected = pl.pallas_call(
        functools.partial(kernel, total),
        out_shape=tuple(pltpu.VMEM(out.shape, out.dtype) for out in outputs),
        in_specs=[anywhere] * 2,
        out_specs=(pl.BlockSpec(memory_space=pltpu.VMEM),) * 2,
        scratch_shapes=[
            pltpu.VMEM((rows, columns), BF16),
            pltpu.VMEM((columns, rank), BF16),
            pltpu.VMEM((RING, shard, rank), F32),
            pltpu.VMEM((2, RING - 1, message, rank), BF16),
            pltpu.VMEM((2, RING - 1, message, rank), BF16),
            pltpu.VMEM((RING, shard, rank), BF16),
            pltpu.VMEM((rank, columns), F32),
            pltpu.VMEM((2 * rank, 2 * rank), F32),
            pltpu.VMEM((rank, rank), F32),
            pltpu.VMEM((count, half, rank), F32),
            pltpu.VMEM((count, half, rank), F32),
            pltpu.VMEM((RING, half, rank), F32),
            pltpu.VMEM((count, half, rank), F32),
            pltpu.VMEM((rank, 2 * rank), F32),
            pltpu.VMEM((chips, half, columns), F32),
            pltpu.VMEM((chips, half, columns), F32),
            pltpu.VMEM((chips, half, columns), F32),
            pltpu.VMEM((chips, half, columns), F32),
            dma((RING + 2,)),
            dma((2,)),
            dma((2, EVENTS)),
            dma,
            dma((2, EVENTS)),
            dma((2,)),
            dma((2,)),
            dma((2,)),
            dma((2,)),
            dma,
            dma,
        ],
        compiler_params=pltpu.CompilerParams(
            collective_id=0, has_side_effects=True, vmem_limit_bytes=56 * 1024 * 1024
        ),
    )(snapshots, sketch)
    return pl.pallas_call(
        finish,
        out_shape=outputs,
        in_specs=[pl.BlockSpec(memory_space=pltpu.VMEM)] * 2,
        out_specs=(anywhere, anywhere),
        scratch_shapes=[dma((PIECES + 1,))],
        compiler_params=pltpu.CompilerParams(vmem_limit_bytes=16 * 1024 * 1024),
    )(basis, projected)


def solution(mesh):
    in_specs = (P("rows", "snaps"), P("snaps", None))
    out_specs = (P(("rows", "snaps"), None), P("rows", "snaps"))
    return jax.shard_map(local, mesh=mesh, in_specs=in_specs, out_specs=out_specs, check_vma=False)
```

```python
import functools
import math

import jax
import jax.numpy as jnp
from jax import lax
from jax.experimental import pallas as pl
from jax.experimental.pallas import tpu as pltpu
from jax.sharding import PartitionSpec as P

MESH = pl.DeviceIdType.MESH
HIGHEST = lax.Precision.HIGHEST
F32, BF16 = jnp.float32, jnp.bfloat16

RING = 8
PIECES = 4
EVENTS = 2 * (RING - 1)
SPAN = 120.0
BLOCK = 16


def groups_of(value):
    rows, rank = value.shape
    return value.reshape(rows // 16, 16, rank)


def peak(value):
    return jnp.max(jnp.abs(groups_of(value)), axis=0)


def encode(value, top):
    gain = SPAN / top.astype(F32)
    return jnp.exp2(groups_of(value) * gain[None]).reshape(value.shape).astype(BF16)


def decode(code, top):
    gain = top.astype(F32) * (1.0 / (SPAN * math.log(2.0)))
    return (jnp.log(groups_of(code.astype(F32))) * gain[None]).reshape(code.shape)


def split(value):
    high = value.astype(BF16)
    return high, (value - high.astype(F32)).astype(BF16)


def factor_block(x, block):
    rank = x.shape[0]
    first = pl.multiple_of(block * BLOCK, BLOCK)
    shape = (BLOCK, rank)
    panel = x[pl.ds(first, BLOCK), :]
    left, right = panel[:, :rank], panel[:, rank:]
    corner = pltpu.roll(left, lax.rem(rank - first, rank), 1)
    row = lax.broadcasted_iota(jnp.int32, shape, 0)
    lane = lax.broadcasted_iota(jnp.int32, shape, 1)
    columns = [jnp.broadcast_to(corner[:, j : j + 1], shape) for j in range(BLOCK)]

    def spread(value, i):
        return jnp.broadcast_to(value[i : i + 1, :], shape)

    first_pivot = cross = determinant = jnp.zeros(shape, F32)
    for i in range(0, BLOCK, 2):
        one, two = columns[i], columns[i + 1]
        a, b, d = spread(one, i), spread(one, i + 1), spread(two, i + 1)
        det = a * d - b * b
        here = (row == i) | (row == i + 1)
        first_pivot = jnp.where(here, a, first_pivot)
        cross = jnp.where(row == i + 1, b, cross)
        determinant = jnp.where(here, det, determinant)
        if i + 2 == BLOCK:
            break
        inverse = jnp.where(row > i + 1, 1.0 / det, 0.0)
        u, v = (one * d - two * b) * inverse, (two * a - one * b) * inverse
        for j in range(i + 2, BLOCK):
            columns[j] = columns[j] - (u * spread(columns[j], i) + v * spread(columns[j], i + 1))
        left = left - (u * spread(left, i) + v * spread(left, i + 1))
        right = right - (u * spread(right, i) + v * spread(right, i + 1))
    odd = row % 2 == 1
    factor = cross / first_pivot
    scale = jnp.where(odd, first_pivot * lax.rsqrt(first_pivot * determinant), lax.rsqrt(first_pivot))
    left = (left - factor * pltpu.roll(left, 1, 0)) * scale
    right = (right - factor * pltpu.roll(right, 1, 0)) * scale
    whole = jnp.concatenate([left, right], axis=1)
    x[pl.ds(first, BLOCK), :] = whole
    r1, r2 = split(whole)
    r3 = (whole - r1.astype(F32) - r2.astype(F32)).astype(BF16)
    later = jnp.where(lane >= first + BLOCK, left, 0.0)
    l1, l2 = split(later)
    l3 = (later - l1.astype(F32) - l2.astype(F32)).astype(BF16)
    x[...] -= lax.dot_general(
        jnp.concatenate([l1, l1, l2, l1, l2, l3], axis=0),
        jnp.concatenate([r1, r2, r1, r3, r2, r1], axis=0),
        (((0,), (0,)), ((), ())),
        preferred_element_type=F32,
    )


def kernel(
    total, s_hbm, k_hbm, basis_ref, proj_ref,
    s, k, part, tx, rx, everyone, z_sum, gg, g, g0, g1, g2, g3, x, give, take, pair, zr,
    load_sem, rs_send, rs_recv, ag_send, ag_recv, g1_sem, g2_sem, g3_sem, zr_sem, mate_send, mate_recv,
):
    count = lax.axis_size("rows")
    chips = count // 2
    r, z = lax.axis_index("rows"), lax.axis_index("snaps")
    chip, core = lax.div(r, 2), lax.rem(r, 2)
    shard = part.shape[1]
    size = shard // PIECES
    rank = k.shape[1]
    own = rank // chips
    half = rank // count

    def wrap(index, length):
        index = jnp.where(index >= length, index - length, index)
        return jnp.where(index < 0, index + length, index)

    def at(step):
        return wrap(z + step, RING)

    def load(offset, slot, part_of=0, parts=1):
        length = shard // parts
        rows = pl.ds(pl.multiple_of(at(offset) * shard + part_of * length, length), length)
        return pltpu.make_async_copy(s_hbm.at[rows, :], s.at[rows, :], load_sem.at[slot])

    def order(slot):
        return (RING - slot) // 2 * (1 - 2 * ((slot + 1) % 2)) if slot else RING // 2

    sketch_copy = pltpu.make_async_copy(k_hbm, k, load_sem.at[RING])
    sketch_copy.start()
    for side in range(2):
        load(order(0), side * (RING + 1), side, 2).start(priority=1)
    load(order(1), 1).start(priority=1)

    barrier = pltpu.get_barrier_semaphore()

    def other_chip(step):
        return wrap(chip + step, chips)

    def other_row(step):
        return wrap(r + step, count)

    def to_chip(step):
        return {"rows": other_chip(step) * 2 + core, "snaps": z}

    def to_row(step):
        return {"rows": other_row(step), "snaps": z}

    def to_depth(step):
        return {"rows": r, "snaps": at(step)}

    @pl.loop(1, count)
    def _(step):
        pl.semaphore_signal(barrier, inc=1, device_id=to_row(step), device_id_type=MESH)

    @pl.loop(1, RING)
    def _(step):
        pl.semaphore_signal(barrier, inc=1, device_id=to_depth(step), device_id_type=MESH)

    def ring(side, src, dst, send, recv):
        return pltpu.make_async_remote_copy(
            src_ref=src,
            dst_ref=dst,
            send_sem=send,
            recv_sem=recv,
            device_id={"rows": r, "snaps": at(1 - 2 * side)},
            device_id_type=MESH,
        )

    def span_of(i):
        return pl.ds(0, size + 16) if i == 0 else pl.ds(size + 16, size)

    def data_of(i):
        return pl.ds(0, size) if i == 0 else pl.ds(size + 16, size)

    scale_rows = pl.ds(size, 16)

    def sum_copy(side, u, i):
        return ring(
            side,
            tx.at[side, u, span_of(i), :],
            rx.at[side, u, span_of(i), :],
            rs_send.at[side],
            rs_recv.at[side, 2 * u + i],
        )

    def piece(q):
        return pl.ds(pl.multiple_of(q * size, size), size)

    def sketch(slot):
        if slot + 2 < RING:
            load(order(slot + 2), slot + 2).start(priority=1)
        load(order(slot), slot).wait()
        j = at(order(slot))
        rows = pl.ds(pl.multiple_of(j * shard, shard), shard)
        part[j] = jnp.dot(s[rows, :], k[...], preferred_element_type=F32)

    def pair_rows(j, side, u):
        first = 2 * size * (u % 2 if side == 0 else 1 - u % 2)
        return j, pl.ds(pl.multiple_of(first, 2 * size), 2 * size)

    def piece_rows(j, side, u, i):
        first = 2 * size * (u % 2 if side == 0 else 1 - u % 2) + i * size
        return j, pl.ds(pl.multiple_of(first, size), size)

    def set_scale(side, u, top):
        tx[side, u, scale_rows, :] = (top * 1.01 + 1e-30).astype(BF16)

    def set_data(side, u, i, value):
        tx[side, u, data_of(i), :] = encode(value, tx[side, u, scale_rows, :])

    def send(side, u, i, value):
        set_data(side, u, i, value)
        sum_copy(side, u, i).start()

    def came(side, u, i):
        return decode(rx[side, u, data_of(i), :], rx[side, u, scale_rows, :])

    def head(side, u, offset):
        j = at(offset)
        set_scale(side, u, peak(part[pair_rows(j, side, u)]))
        for i in range(2):
            send(side, u, i, part[piece_rows(j, side, u, i)])

    sketch_copy.wait()
    load(order(2), 2).start(priority=1)
    for side in range(2):
        load(order(0), side * (RING + 1), side, 2).wait()
        first = side * 2 * size
        rows = pl.ds(pl.multiple_of(at(order(0)) * shard + first, 2 * size), 2 * size)
        part[at(order(0)), pl.ds(first, 2 * size), :] = jnp.dot(s[rows, :], k[...], preferred_element_type=F32)
        j = at(4)
        set_scale(side, 0, peak(part[pair_rows(j, side, 0)]))
        for i in range(2):
            set_data(side, 0, i, part[piece_rows(j, side, 0, i)])
        if side == 0:
            pl.semaphore_wait(barrier, count - 1 + RING - 1)
        for i in range(2):
            sum_copy(side, 0, i).start()
    for side in range(2):
        sketch(1 + side)
        head(side, 1, 3 - 6 * side)
    for slot in range(3, RING):
        sketch(slot)

    @pl.loop(0, RING - 3)
    def _(u):
        far = 4 - (u + 1) // 2
        for i in range(2):
            for side in range(2):
                j = at((1 - 2 * side) * (far - 1))
                sum_copy(side, u, i).wait_recv()
                if i == 0:
                    set_scale(side, u + 2, rx[side, u, scale_rows, :].astype(F32) + peak(part[pair_rows(j, side, u)]))
                send(side, u + 2, i, part[piece_rows(j, side, u, i)] + came(side, u, i))

    def gather_copy(side, e, j, q):
        block = everyone.at[j, piece(q), :]
        return ring(side, block, block, ag_send, ag_recv.at[side, e])

    def gather_piece(side, e):
        hop = jnp.minimum(e // 4 + 1, 4)
        i = jnp.where(e < 12, e % 4, 2 * (e - 12))
        odd = i % 2
        return hop, 2 * (odd if side == 0 else 1 - odd) + i // 2

    def start_own(i):
        for side in range(2):
            for odd in range(2):
                e = 2 * i + odd
                gather_copy(side, e, z, gather_piece(side, e)[1]).start()

    def gram(pieces):
        rows = jnp.concatenate([part[z, piece(q), :] for q in pieces], axis=0)
        both = jnp.concatenate(split(rows), axis=1)
        gg[...] += lax.dot_general(both, both, (((0,), (0,)), ((), ())), preferred_element_type=F32)

    gg[...] = jnp.zeros_like(gg)
    for i in range(2):
        for side in range(2):
            sum_copy(side, RING - 3, i).wait_recv()
            part[piece_rows(z, side, RING - 3, i)] += came(side, RING - 3, i)
    for i in range(2):
        for side in range(2):
            sum_copy(side, RING - 2, i).wait_recv()
            mine = part[piece_rows(z, side, RING - 2, i)] + came(side, RING - 2, i)
            part[piece_rows(z, side, RING - 2, i)] = mine
            everyone[piece_rows(z, side, RING - 2, i)] = mine.astype(BF16)
        if i == 0:
            start_own(0)
        gram((i, 2 + i))

    g[...] = gg[:rank, :rank] + gg[:rank, rank:] + gg[rank:, :rank] + gg[rank:, rank:]
    for index in range(count):
        g0[index] = g[index * half : (index + 1) * half, :]

    def remote(src, dst, send_sem, recv_sem, there):
        return pltpu.make_async_remote_copy(
            src_ref=src,
            dst_ref=dst,
            send_sem=send_sem,
            recv_sem=recv_sem,
            device_id=there,
            device_id_type=MESH,
        )

    def g1_copy(step):
        return remote(g0.at[other_row(step)], g1.at[step], g1_sem.at[0], g1_sem.at[1], to_row(step))

    def g2_copy(step):
        return remote(g2.at[z], g2.at[z], g2_sem.at[0], g2_sem.at[1], to_depth(step))

    def g3_copy(step):
        return remote(g3.at[r], g3.at[r], g3_sem.at[0], g3_sem.at[1], to_row(step))

    def zr_copy(step):
        return remote(pair.at[other_chip(step)], zr.at[step], zr_sem.at[0], zr_sem.at[1], to_chip(step))

    def all_of(ref, number, sem):
        block = ref.at[pl.ds(0, number)]
        return remote(block, block, sem.at[0], sem.at[1], to_row(1))

    def start_all(copy, number):
        for step in range(1, number):
            copy(step).start()

    start_all(g1_copy, count)
    start_own(1)

    def term_of(pairs):
        left = [everyone[j, piece(q), :] for j, q in pairs]
        right = [s[pl.ds(pl.multiple_of(j * shard + q * size, size), size), :] for j, q in pairs]
        return lax.dot_general(
            jnp.concatenate(left, axis=0),
            jnp.concatenate(right, axis=0),
            (((0,), (0,)), ((), ())),
            preferred_element_type=F32,
        )

    def gather(e):
        came = []
        for side in range(2):
            hop, q = gather_piece(side, e)
            j = at(-(1 - 2 * side) * hop)
            came.append((j, q))
            gather_copy(side, e, j, q).wait_recv()

            @pl.when((e < 8) | (e == 8) | (e == 10))
            def _():
                gather_copy(side, jnp.where(e < 8, e + 4, 12 + (e - 8) // 2), j, q).start()

        return term_of(came)

    z_sum[...] = term_of([(z, q) for q in range(PIECES)])
    all_of(g1, count - 1, g1_sem).wait_recv()
    g1[0] = g0[r]
    g2[z] = jnp.sum(g1[...], axis=0)
    start_all(g2_copy, RING)

    @pl.loop(0, 2)
    def _(e):
        z_sum[...] += gather(e)

    all_of(g2, RING - 1, g2_sem).wait_recv()
    g3[r] = jnp.sum(g2[...], axis=0) * (1.0 / total)
    start_all(g3_copy, count)

    @pl.loop(2, 4)
    def _(e):
        z_sum[...] += gather(e)

    all_of(g3, count - 1, g3_sem).wait_recv()
    for index in range(count):
        g[index * half : (index + 1) * half, :] = g3[index]

    eye = lax.broadcasted_iota(jnp.int32, (rank, rank), 0) == lax.broadcasted_iota(jnp.int32, (rank, rank), 1)
    full = g[...]
    diagonal = jnp.where(eye, full, 0.0)
    down = lax.rsqrt(jnp.sum(diagonal, axis=1, keepdims=True))
    across = lax.rsqrt(jnp.sum(diagonal, axis=0, keepdims=True))
    x[...] = jnp.concatenate([full * down * across, jnp.where(eye, down, 0.0)], axis=1)

    @pl.loop(4, EVENTS - 2)
    def _(e):
        z_sum[...] += gather(e)
        factor_block(x, e - 4)

    z_sum[...] += gather(EVENTS - 2)

    l1, l2 = split(x[:, rank:])
    z1, z2 = split(z_sum[...] + gather(EVENTS - 1))
    term = jnp.dot(
        jnp.concatenate([l1, l2, l1], axis=1),
        jnp.concatenate([z1, z1, z2], axis=0),
        preferred_element_type=F32,
    ) * (1.0 / math.sqrt(total))
    z_sum[...] = term
    for c in range(chips):
        rows = z_sum[c * own : (c + 1) * own, :]
        low, high = rows[:half], rows[half:]
        give[c] = jnp.where(core == 0, high, low)
        pair[c] = jnp.where(core == 0, low, high)
    mate = remote(give, take, mate_send, mate_recv, {"rows": chip * 2 + 1 - core, "snaps": z})
    mate.start()
    i1, i2 = split(x[:, rank:])
    mate.wait_recv()
    pair[...] += take[...]

    start_all(zr_copy, chips)

    @pl.loop(0, PIECES)
    def _(q):
        y1, y2 = split(part[z, piece(q), :])
        basis_ref[piece(q), :] = lax.dot_general(
            jnp.concatenate([y1, y1, y2], axis=1),
            jnp.concatenate([i1, i2, i1], axis=1),
            (((1,), (1,)), ((), ())),
            preferred_element_type=F32,
        )

    mate.wait_send()

    for side in range(2):
        ring(side, tx.at[side], tx.at[side], rs_send.at[side], rs_recv.at[side, 0]).wait_send()
    sent = everyone.at[pl.ds(0, RING - 1)]
    ring(0, sent, sent, ag_send, ag_recv.at[0, 0]).wait_send()
    all_of(g1, count - 1, g1_sem).wait_send()
    all_of(g2, RING - 1, g2_sem).wait_send()
    all_of(g3, count - 1, g3_sem).wait_send()

    all_of(zr, chips - 1, zr_sem).wait_recv()
    zr[0] = pair[chip]
    proj_ref[...] = jnp.sum(zr[...], axis=0)
    all_of(zr, chips - 1, zr_sem).wait_send()


def finish(basis_in, proj_in, basis_out, proj_out, sem):
    copies = [pltpu.make_async_copy(proj_in, proj_out, sem.at[0])]
    size = basis_in.shape[0] // PIECES
    for q in range(PIECES):
        rows = pl.ds(q * size, size)
        copies.append(pltpu.make_async_copy(basis_in.at[rows, :], basis_out.at[rows, :], sem.at[1 + q]))
    for copy in copies:
        copy.start()
    for copy in copies:
        copy.wait()


def local(snapshots, sketch):
    rows, columns = snapshots.shape
    rank = sketch.shape[1]
    count = lax.axis_size("rows")
    chips = count // 2
    total = rows * count
    shard = rows // RING
    half = rank // count
    message = 2 * (shard // PIECES) + 16
    dma = pltpu.SemaphoreType.DMA
    outputs = (
        jax.ShapeDtypeStruct((shard, rank), F32),
        jax.ShapeDtypeStruct((half, columns), F32),
    )
    anywhere = pl.BlockSpec(memory_space=pl.ANY)
    basis, projected = pl.pallas_call(
        functools.partial(kernel, total),
        out_shape=tuple(pltpu.VMEM(out.shape, out.dtype) for out in outputs),
        in_specs=[anywhere] * 2,
        out_specs=(pl.BlockSpec(memory_space=pltpu.VMEM),) * 2,
        scratch_shapes=[
            pltpu.VMEM((rows, columns), BF16),
            pltpu.VMEM((columns, rank), BF16),
            pltpu.VMEM((RING, shard, rank), F32),
            pltpu.VMEM((2, RING - 1, message, rank), BF16),
            pltpu.VMEM((2, RING - 1, message, rank), BF16),
            pltpu.VMEM((RING, shard, rank), BF16),
            pltpu.VMEM((rank, columns), F32),
            pltpu.VMEM((2 * rank, 2 * rank), F32),
            pltpu.VMEM((rank, rank), F32),
            pltpu.VMEM((count, half, rank), F32),
            pltpu.VMEM((count, half, rank), F32),
            pltpu.VMEM((RING, half, rank), F32),
            pltpu.VMEM((count, half, rank), F32),
            pltpu.VMEM((rank, 2 * rank), F32),
            pltpu.VMEM((chips, half, columns), F32),
            pltpu.VMEM((chips, half, columns), F32),
            pltpu.VMEM((chips, half, columns), F32),
            pltpu.VMEM((chips, half, columns), F32),
            dma((RING + 2,)),
            dma((2,)),
            dma((2, EVENTS)),
            dma,
            dma((2, EVENTS)),
            dma((2,)),
            dma((2,)),
            dma((2,)),
            dma((2,)),
            dma,
            dma,
        ],
        compiler_params=pltpu.CompilerParams(
            collective_id=0, has_side_effects=True, vmem_limit_bytes=56 * 1024 * 1024
        ),
    )(snapshots, sketch)
    return pl.pallas_call(
        finish,
        out_shape=outputs,
        in_specs=[pl.BlockSpec(memory_space=pltpu.VMEM)] * 2,
        out_specs=(anywhere, anywhere),
        scratch_shapes=[dma((PIECES + 1,))],
        compiler_params=pltpu.CompilerParams(vmem_limit_bytes=16 * 1024 * 1024),
    )(basis, projected)


def solution(mesh):
    in_specs = (P("rows", "snaps"), P("snaps", None))
    out_specs = (P(("rows", "snaps"), None), P("rows", "snaps"))
    return jax.shard_map(local, mesh=mesh, in_specs=in_specs, out_specs=out_specs, check_vma=False)
```

```python
import functools
import math

import jax
import jax.numpy as jnp
from jax import lax
from jax.experimental import pallas as pl
from jax.experimental.pallas import tpu as pltpu
from jax.sharding import PartitionSpec as P

MESH = pl.DeviceIdType.MESH
HIGHEST = lax.Precision.HIGHEST
F32, BF16 = jnp.float32, jnp.bfloat16

RING = 8
PIECES = 4
EVENTS = 2 * (RING - 1)
SPAN = 120.0
BLOCK = 16


def groups_of(value):
    rows, rank = value.shape
    return value.reshape(rows // 16, 16, rank)


def peak(value):
    return jnp.max(jnp.abs(groups_of(value)), axis=0)


def encode(value, top):
    gain = SPAN / top.astype(F32)
    return jnp.exp2(groups_of(value) * gain[None]).reshape(value.shape).astype(BF16)


def decode(code, top):
    gain = top.astype(F32) * (1.0 / (SPAN * math.log(2.0)))
    return (jnp.log(groups_of(code.astype(F32))) * gain[None]).reshape(code.shape)


def split(value):
    high = value.astype(BF16)
    return high, (value - high.astype(F32)).astype(BF16)


def factor_block(x, block):
    rank = x.shape[0]
    first = pl.multiple_of(block * BLOCK, BLOCK)
    shape = (BLOCK, rank)
    panel = x[pl.ds(first, BLOCK), :]
    left, right = panel[:, :rank], panel[:, rank:]
    corner = pltpu.roll(left, lax.rem(rank - first, rank), 1)
    row = lax.broadcasted_iota(jnp.int32, shape, 0)
    lane = lax.broadcasted_iota(jnp.int32, shape, 1)
    columns = [jnp.broadcast_to(corner[:, j : j + 1], shape) for j in range(BLOCK)]

    def spread(value, i):
        return jnp.broadcast_to(value[i : i + 1, :], shape)

    first_pivot = cross = determinant = jnp.zeros(shape, F32)
    for i in range(0, BLOCK, 2):
        one, two = columns[i], columns[i + 1]
        a, b, d = spread(one, i), spread(one, i + 1), spread(two, i + 1)
        det = a * d - b * b
        here = (row == i) | (row == i + 1)
        first_pivot = jnp.where(here, a, first_pivot)
        cross = jnp.where(row == i + 1, b, cross)
        determinant = jnp.where(here, det, determinant)
        if i + 2 == BLOCK:
            break
        inverse = jnp.where(row > i + 1, 1.0 / det, 0.0)
        u, v = (one * d - two * b) * inverse, (two * a - one * b) * inverse
        for j in range(i + 2, BLOCK):
            columns[j] = columns[j] - (u * spread(columns[j], i) + v * spread(columns[j], i + 1))
        left = left - (u * spread(left, i) + v * spread(left, i + 1))
        right = right - (u * spread(right, i) + v * spread(right, i + 1))
    odd = row % 2 == 1
    factor = cross / first_pivot
    scale = jnp.where(odd, first_pivot * lax.rsqrt(first_pivot * determinant), lax.rsqrt(first_pivot))
    left = (left - factor * pltpu.roll(left, 1, 0)) * scale
    right = (right - factor * pltpu.roll(right, 1, 0)) * scale
    whole = jnp.concatenate([left, right], axis=1)
    x[pl.ds(first, BLOCK), :] = whole
    r1, r2 = split(whole)
    r3 = (whole - r1.astype(F32) - r2.astype(F32)).astype(BF16)
    later = jnp.where(lane >= first + BLOCK, left, 0.0)
    l1, l2 = split(later)
    l3 = (later - l1.astype(F32) - l2.astype(F32)).astype(BF16)
    x[...] -= lax.dot_general(
        jnp.concatenate([l1, l1, l2, l1, l2, l3], axis=0),
        jnp.concatenate([r1, r2, r1, r3, r2, r1], axis=0),
        (((0,), (0,)), ((), ())),
        preferred_element_type=F32,
    )


def kernel(
    total, s_hbm, k_hbm, basis_ref, proj_ref,
    s, k, part, tx, rx, everyone, z_sum, gg, g, g0, g1, g2, g3, x, give, take, pair, zr,
    load_sem, rs_send, rs_recv, ag_send, ag_recv, g1_sem, g2_sem, g3_sem, zr_sem, mate_send, mate_recv,
):
    count = lax.axis_size("rows")
    chips = count // 2
    r, z = lax.axis_index("rows"), lax.axis_index("snaps")
    chip, core = lax.div(r, 2), lax.rem(r, 2)
    shard = part.shape[1]
    size = shard // PIECES
    rank = k.shape[1]
    own = rank // chips
    half = rank // count

    def wrap(index, length):
        index = jnp.where(index >= length, index - length, index)
        return jnp.where(index < 0, index + length, index)

    def at(step):
        return wrap(z + step, RING)

    def load(offset, slot, part_of=0, parts=1):
        length = shard // parts
        rows = pl.ds(pl.multiple_of(at(offset) * shard + part_of * length, length), length)
        return pltpu.make_async_copy(s_hbm.at[rows, :], s.at[rows, :], load_sem.at[slot])

    def order(slot):
        return (RING - slot) // 2 * (1 - 2 * ((slot + 1) % 2))

    sketch_copy = pltpu.make_async_copy(k_hbm, k, load_sem.at[RING])
    sketch_copy.start()
    for side in range(2):
        load(RING // 2, side * (RING + 1), side, 2).start()
    load(order(1), 1).start()

    barrier = pltpu.get_barrier_semaphore()

    def other_chip(step):
        return wrap(chip + step, chips)

    def other_row(step):
        return wrap(r + step, count)

    def to_chip(step):
        return {"rows": other_chip(step) * 2 + core, "snaps": z}

    def to_row(step):
        return {"rows": other_row(step), "snaps": z}

    def to_depth(step):
        return {"rows": r, "snaps": at(step)}

    @pl.loop(1, count)
    def _(step):
        pl.semaphore_signal(barrier, inc=1, device_id=to_row(step), device_id_type=MESH)

    @pl.loop(1, RING)
    def _(step):
        pl.semaphore_signal(barrier, inc=1, device_id=to_depth(step), device_id_type=MESH)

    def ring(side, src, dst, send, recv):
        return pltpu.make_async_remote_copy(
            src_ref=src,
            dst_ref=dst,
            send_sem=send,
            recv_sem=recv,
            device_id={"rows": r, "snaps": at(1 - 2 * side)},
            device_id_type=MESH,
        )

    def span_of(i):
        return pl.ds(0, size + 16) if i == 0 else pl.ds(size + 16, size)

    def data_of(i):
        return pl.ds(0, size) if i == 0 else pl.ds(size + 16, size)

    scale_rows = pl.ds(size, 16)

    def sum_copy(side, u, i):
        return ring(
            side,
            tx.at[side, u, span_of(i), :],
            rx.at[side, u, span_of(i), :],
            rs_send.at[side],
            rs_recv.at[side, 2 * u + i],
        )

    def piece(q):
        return pl.ds(pl.multiple_of(q * size, size), size)

    def sketch(slot):
        @pl.when(slot + 2 < RING)
        def _():
            load(order(slot + 2), slot + 2).start()

        load(order(slot), slot).wait()
        j = at(order(slot))
        rows = pl.ds(pl.multiple_of(j * shard, shard), shard)
        part[j] = jnp.dot(s[rows, :], k[...], preferred_element_type=F32)

    def pair_rows(j, side, u):
        first = 2 * size * (u % 2 if side == 0 else 1 - u % 2)
        return j, pl.ds(pl.multiple_of(first, 2 * size), 2 * size)

    def piece_rows(j, side, u, i):
        first = 2 * size * (u % 2 if side == 0 else 1 - u % 2) + i * size
        return j, pl.ds(pl.multiple_of(first, size), size)

    def set_scale(side, u, top):
        tx[side, u, scale_rows, :] = (top * 1.01 + 1e-30).astype(BF16)

    def set_data(side, u, i, value):
        tx[side, u, data_of(i), :] = encode(value, tx[side, u, scale_rows, :])

    def send(side, u, i, value):
        set_data(side, u, i, value)
        sum_copy(side, u, i).start()

    def came(side, u, i):
        return decode(rx[side, u, data_of(i), :], rx[side, u, scale_rows, :])

    def head(side, u, offset):
        j = at(offset)
        set_scale(side, u, peak(part[pair_rows(j, side, u)]))
        for i in range(2):
            send(side, u, i, part[piece_rows(j, side, u, i)])

    sketch_copy.wait()
    load(order(2), 2).start()
    for side in range(2):
        load(RING // 2, side * (RING + 1), side, 2).wait()
        first = side * 2 * size
        rows = pl.ds(pl.multiple_of(at(RING // 2) * shard + first, 2 * size), 2 * size)
        part[at(RING // 2), pl.ds(first, 2 * size), :] = jnp.dot(s[rows, :], k[...], preferred_element_type=F32)
        j = at(4)
        set_scale(side, 0, peak(part[pair_rows(j, side, 0)]))
        for i in range(2):
            set_data(side, 0, i, part[piece_rows(j, side, 0, i)])
        if side == 0:
            pl.semaphore_wait(barrier, count - 1 + RING - 1)
        for i in range(2):
            sum_copy(side, 0, i).start()
    for side in range(2):
        sketch(1 + side)
        head(side, 1, 3 - 6 * side)
    @pl.loop(3, RING)
    def _(slot):
        sketch(slot)

    @pl.loop(0, RING - 3)
    def _(u):
        far = 4 - (u + 1) // 2
        for i in range(2):
            for side in range(2):
                j = at((1 - 2 * side) * (far - 1))
                sum_copy(side, u, i).wait_recv()
                if i == 0:
                    set_scale(side, u + 2, rx[side, u, scale_rows, :].astype(F32) + peak(part[pair_rows(j, side, u)]))
                send(side, u + 2, i, part[piece_rows(j, side, u, i)] + came(side, u, i))

    def gather_copy(side, e, j, q):
        block = everyone.at[j, piece(q), :]
        return ring(side, block, block, ag_send, ag_recv.at[side, e])

    def gather_piece(side, e):
        hop = jnp.minimum(e // 4 + 1, 4)
        i = jnp.where(e < 12, e % 4, 2 * (e - 12))
        odd = i % 2
        return hop, 2 * (odd if side == 0 else 1 - odd) + i // 2

    def start_own(i):
        for side in range(2):
            for odd in range(2):
                e = 2 * i + odd
                gather_copy(side, e, z, gather_piece(side, e)[1]).start()

    def gram(pieces):
        rows = jnp.concatenate([part[z, piece(q), :] for q in pieces], axis=0)
        both = jnp.concatenate(split(rows), axis=1)
        gg[...] += lax.dot_general(both, both, (((0,), (0,)), ((), ())), preferred_element_type=F32)

    gg[...] = jnp.zeros_like(gg)
    for i in range(2):
        for side in range(2):
            sum_copy(side, RING - 3, i).wait_recv()
            part[piece_rows(z, side, RING - 3, i)] += came(side, RING - 3, i)
    for i in range(2):
        for side in range(2):
            sum_copy(side, RING - 2, i).wait_recv()
            mine = part[piece_rows(z, side, RING - 2, i)] + came(side, RING - 2, i)
            part[piece_rows(z, side, RING - 2, i)] = mine
            everyone[piece_rows(z, side, RING - 2, i)] = mine.astype(BF16)
        if i == 0:
            start_own(0)
        gram((i, 2 + i))

    g[...] = gg[:rank, :rank] + gg[:rank, rank:] + gg[rank:, :rank] + gg[rank:, rank:]
    for index in range(count):
        g0[index] = g[index * half : (index + 1) * half, :]

    def remote(src, dst, send_sem, recv_sem, there):
        return pltpu.make_async_remote_copy(
            src_ref=src,
            dst_ref=dst,
            send_sem=send_sem,
            recv_sem=recv_sem,
            device_id=there,
            device_id_type=MESH,
        )

    def g1_copy(step):
        return remote(g0.at[other_row(step)], g1.at[step], g1_sem.at[0], g1_sem.at[1], to_row(step))

    def g2_copy(step):
        return remote(g2.at[z], g2.at[z], g2_sem.at[0], g2_sem.at[1], to_depth(step))

    def g3_copy(step):
        return remote(g3.at[r], g3.at[r], g3_sem.at[0], g3_sem.at[1], to_row(step))

    def zr_copy(step):
        return remote(pair.at[other_chip(step)], zr.at[step], zr_sem.at[0], zr_sem.at[1], to_chip(step))

    def all_of(ref, number, sem):
        block = ref.at[pl.ds(0, number)]
        return remote(block, block, sem.at[0], sem.at[1], to_row(1))

    def start_all(copy, number):
        for step in range(1, number):
            copy(step).start()

    start_all(g1_copy, count)
    start_own(1)

    def term_of(pairs):
        left = [everyone[j, piece(q), :] for j, q in pairs]
        right = [s[pl.ds(pl.multiple_of(j * shard + q * size, size), size), :] for j, q in pairs]
        return lax.dot_general(
            jnp.concatenate(left, axis=0),
            jnp.concatenate(right, axis=0),
            (((0,), (0,)), ((), ())),
            preferred_element_type=F32,
        )

    def gather(e):
        came = []
        for side in range(2):
            hop, q = gather_piece(side, e)
            j = at(-(1 - 2 * side) * hop)
            came.append((j, q))
            gather_copy(side, e, j, q).wait_recv()

            @pl.when((e < 8) | (e == 8) | (e == 10))
            def _():
                gather_copy(side, jnp.where(e < 8, e + 4, 12 + (e - 8) // 2), j, q).start()

        return term_of(came)

    z_sum[...] = term_of([(z, q) for q in range(PIECES)])
    all_of(g1, count - 1, g1_sem).wait_recv()
    g1[0] = g0[r]
    g2[z] = jnp.sum(g1[...], axis=0)
    start_all(g2_copy, RING)

    @pl.loop(0, 2)
    def _(e):
        z_sum[...] += gather(e)

    all_of(g2, RING - 1, g2_sem).wait_recv()
    g3[r] = jnp.sum(g2[...], axis=0) * (1.0 / total)
    start_all(g3_copy, count)

    @pl.loop(2, 4)
    def _(e):
        z_sum[...] += gather(e)

    all_of(g3, count - 1, g3_sem).wait_recv()
    for index in range(count):
        g[index * half : (index + 1) * half, :] = g3[index]

    eye = lax.broadcasted_iota(jnp.int32, (rank, rank), 0) == lax.broadcasted_iota(jnp.int32, (rank, rank), 1)
    full = g[...]
    diagonal = jnp.where(eye, full, 0.0)
    down = lax.rsqrt(jnp.sum(diagonal, axis=1, keepdims=True))
    across = lax.rsqrt(jnp.sum(diagonal, axis=0, keepdims=True))
    x[...] = jnp.concatenate([full * down * across, jnp.where(eye, down, 0.0)], axis=1)

    @pl.loop(4, EVENTS - 2)
    def _(e):
        z_sum[...] += gather(e)
        factor_block(x, e - 4)

    z_sum[...] += gather(EVENTS - 2)

    l1, l2 = split(x[:, rank:])
    z1, z2 = split(z_sum[...] + gather(EVENTS - 1))
    term = jnp.dot(
        jnp.concatenate([l1, l2, l1], axis=1),
        jnp.concatenate([z1, z1, z2], axis=0),
        preferred_element_type=F32,
    ) * (1.0 / math.sqrt(total))
    z_sum[...] = term
    for c in range(chips):
        rows = z_sum[c * own : (c + 1) * own, :]
        low, high = rows[:half], rows[half:]
        give[c] = jnp.where(core == 0, high, low)
        pair[c] = jnp.where(core == 0, low, high)
    mate = remote(give, take, mate_send, mate_recv, {"rows": chip * 2 + 1 - core, "snaps": z})
    mate.start()
    i1, i2 = split(x[:, rank:])
    mate.wait_recv()
    pair[...] += take[...]

    start_all(zr_copy, chips)

    @pl.loop(0, PIECES)
    def _(q):
        y1, y2 = split(part[z, piece(q), :])
        basis_ref[piece(q), :] = lax.dot_general(
            jnp.concatenate([y1, y1, y2], axis=1),
            jnp.concatenate([i1, i2, i1], axis=1),
            (((1,), (1,)), ((), ())),
            preferred_element_type=F32,
        )

    mate.wait_send()

    for side in range(2):
        ring(side, tx.at[side], tx.at[side], rs_send.at[side], rs_recv.at[side, 0]).wait_send()
    sent = everyone.at[pl.ds(0, RING - 1)]
    ring(0, sent, sent, ag_send, ag_recv.at[0, 0]).wait_send()
    all_of(g1, count - 1, g1_sem).wait_send()
    all_of(g2, RING - 1, g2_sem).wait_send()
    all_of(g3, count - 1, g3_sem).wait_send()

    all_of(zr, chips - 1, zr_sem).wait_recv()
    zr[0] = pair[chip]
    proj_ref[...] = jnp.sum(zr[...], axis=0)
    all_of(zr, chips - 1, zr_sem).wait_send()


def finish(basis_in, proj_in, basis_out, proj_out, sem):
    copies = [pltpu.make_async_copy(proj_in, proj_out, sem.at[0])]
    size = basis_in.shape[0] // PIECES
    for q in range(PIECES):
        rows = pl.ds(q * size, size)
        copies.append(pltpu.make_async_copy(basis_in.at[rows, :], basis_out.at[rows, :], sem.at[1 + q]))
    for copy in copies:
        copy.start()
    for copy in copies:
        copy.wait()


def local(snapshots, sketch):
    rows, columns = snapshots.shape
    rank = sketch.shape[1]
    count = lax.axis_size("rows")
    chips = count // 2
    total = rows * count
    shard = rows // RING
    half = rank // count
    message = 2 * (shard // PIECES) + 16
    dma = pltpu.SemaphoreType.DMA
    outputs = (
        jax.ShapeDtypeStruct((shard, rank), F32),
        jax.ShapeDtypeStruct((half, columns), F32),
    )
    anywhere = pl.BlockSpec(memory_space=pl.ANY)
    basis, projected = pl.pallas_call(
        functools.partial(kernel, total),
        out_shape=tuple(pltpu.VMEM(out.shape, out.dtype) for out in outputs),
        in_specs=[anywhere] * 2,
        out_specs=(pl.BlockSpec(memory_space=pltpu.VMEM),) * 2,
        scratch_shapes=[
            pltpu.VMEM((rows, columns), BF16),
            pltpu.VMEM((columns, rank), BF16),
            pltpu.VMEM((RING, shard, rank), F32),
            pltpu.VMEM((2, RING - 1, message, rank), BF16),
            pltpu.VMEM((2, RING - 1, message, rank), BF16),
            pltpu.VMEM((RING, shard, rank), BF16),
            pltpu.VMEM((rank, columns), F32),
            pltpu.VMEM((2 * rank, 2 * rank), F32),
            pltpu.VMEM((rank, rank), F32),
            pltpu.VMEM((count, half, rank), F32),
            pltpu.VMEM((count, half, rank), F32),
            pltpu.VMEM((RING, half, rank), F32),
            pltpu.VMEM((count, half, rank), F32),
            pltpu.VMEM((rank, 2 * rank), F32),
            pltpu.VMEM((chips, half, columns), F32),
            pltpu.VMEM((chips, half, columns), F32),
            pltpu.VMEM((chips, half, columns), F32),
            pltpu.VMEM((chips, half, columns), F32),
            dma((RING + 2,)),
            dma((2,)),
            dma((2, EVENTS)),
            dma,
            dma((2, EVENTS)),
            dma((2,)),
            dma((2,)),
            dma((2,)),
            dma((2,)),
            dma,
            dma,
        ],
        compiler_params=pltpu.CompilerParams(
            collective_id=0, has_side_effects=True, vmem_limit_bytes=56 * 1024 * 1024
        ),
    )(snapshots, sketch)
    return pl.pallas_call(
        finish,
        out_shape=outputs,
        in_specs=[pl.BlockSpec(memory_space=pltpu.VMEM)] * 2,
        out_specs=(anywhere, anywhere),
        scratch_shapes=[dma((PIECES + 1,))],
        compiler_params=pltpu.CompilerParams(vmem_limit_bytes=16 * 1024 * 1024),
    )(basis, projected)


def solution(mesh):
    in_specs = (P("rows", "snaps"), P("snaps", None))
    out_specs = (P(("rows", "snaps"), None), P("rows", "snaps"))
    return jax.shard_map(local, mesh=mesh, in_specs=in_specs, out_specs=out_specs, check_vma=False)
```

```python
import functools
import math

import jax
import jax.numpy as jnp
from jax import lax
from jax.experimental import pallas as pl
from jax.experimental.pallas import tpu as pltpu
from jax.sharding import PartitionSpec as P

MESH = pl.DeviceIdType.MESH
HIGHEST = lax.Precision.HIGHEST
F32, BF16 = jnp.float32, jnp.bfloat16

RING = 8
PIECES = 4
EVENTS = 2 * (RING - 1)
SPAN = 120.0
BLOCK = 16


def groups_of(value):
    rows, rank = value.shape
    return value.reshape(rows // 16, 16, rank)


def peak(value):
    return jnp.max(jnp.abs(groups_of(value)), axis=0)


def encode(value, top):
    gain = SPAN / top.astype(F32)
    return jnp.exp2(groups_of(value) * gain[None]).reshape(value.shape).astype(BF16)


def decode(code, top):
    gain = top.astype(F32) * (1.0 / (SPAN * math.log(2.0)))
    return (jnp.log(groups_of(code.astype(F32))) * gain[None]).reshape(code.shape)


def split(value):
    high = value.astype(BF16)
    return high, (value - high.astype(F32)).astype(BF16)


def factor_block(x, block):
    rank = x.shape[0]
    first = pl.multiple_of(block * BLOCK, BLOCK)
    shape = (BLOCK, rank)
    panel = x[pl.ds(first, BLOCK), :]
    left, right = panel[:, :rank], panel[:, rank:]
    corner = pltpu.roll(left, lax.rem(rank - first, rank), 1)
    row = lax.broadcasted_iota(jnp.int32, shape, 0)
    lane = lax.broadcasted_iota(jnp.int32, shape, 1)
    columns = [jnp.broadcast_to(corner[:, j : j + 1], shape) for j in range(BLOCK)]

    def spread(value, i):
        return jnp.broadcast_to(value[i : i + 1, :], shape)

    first_pivot = cross = determinant = jnp.zeros(shape, F32)
    for i in range(0, BLOCK, 2):
        one, two = columns[i], columns[i + 1]
        a, b, d = spread(one, i), spread(one, i + 1), spread(two, i + 1)
        det = a * d - b * b
        here = (row == i) | (row == i + 1)
        first_pivot = jnp.where(here, a, first_pivot)
        cross = jnp.where(row == i + 1, b, cross)
        determinant = jnp.where(here, det, determinant)
        if i + 2 == BLOCK:
            break
        inverse = jnp.where(row > i + 1, 1.0 / det, 0.0)
        u, v = (one * d - two * b) * inverse, (two * a - one * b) * inverse
        for j in range(i + 2, BLOCK):
            columns[j] = columns[j] - (u * spread(columns[j], i) + v * spread(columns[j], i + 1))
        left = left - (u * spread(left, i) + v * spread(left, i + 1))
        right = right - (u * spread(right, i) + v * spread(right, i + 1))
    odd = row % 2 == 1
    factor = cross / first_pivot
    scale = jnp.where(odd, first_pivot * lax.rsqrt(first_pivot * determinant), lax.rsqrt(first_pivot))
    left = (left - factor * pltpu.roll(left, 1, 0)) * scale
    right = (right - factor * pltpu.roll(right, 1, 0)) * scale
    whole = jnp.concatenate([left, right], axis=1)
    x[pl.ds(first, BLOCK), :] = whole
    r1, r2 = split(whole)
    r3 = (whole - r1.astype(F32) - r2.astype(F32)).astype(BF16)
    later = jnp.where(lane >= first + BLOCK, left, 0.0)
    l1, l2 = split(later)
    l3 = (later - l1.astype(F32) - l2.astype(F32)).astype(BF16)
    x[...] -= lax.dot_general(
        jnp.concatenate([l1, l1, l2, l1, l2, l3], axis=0),
        jnp.concatenate([r1, r2, r1, r3, r2, r1], axis=0),
        (((0,), (0,)), ((), ())),
        preferred_element_type=F32,
    )


def kernel(
    total, s_hbm, k_hbm, basis_ref, proj_ref,
    s, k, part, tx, rx, everyone, z_sum, gg, g, g0, g1, g2, g3, x, give, take, pair, zr,
    load_sem, rs_send, rs_recv, ag_send, ag_recv, g1_sem, g2_sem, g3_sem, zr_sem, mate_send, mate_recv,
):
    count = lax.axis_size("rows")
    chips = count // 2
    r, z = lax.axis_index("rows"), lax.axis_index("snaps")
    chip, core = lax.div(r, 2), lax.rem(r, 2)
    shard = part.shape[1]
    size = shard // PIECES
    rank = k.shape[1]
    own = rank // chips
    half = rank // count

    def wrap(index, length):
        index = jnp.where(index >= length, index - length, index)
        return jnp.where(index < 0, index + length, index)

    def at(step):
        return wrap(z + step, RING)

    def load(offset, slot, part_of=0, parts=1):
        length = shard // parts
        rows = pl.ds(pl.multiple_of(at(offset) * shard + part_of * length, length), length)
        return pltpu.make_async_copy(s_hbm.at[rows, :], s.at[rows, :], load_sem.at[slot])

    def order(slot):
        return (RING - slot) // 2 * (1 - 2 * ((slot + 1) % 2))

    sketch_copy = pltpu.make_async_copy(k_hbm, k, load_sem.at[RING])
    sketch_copy.start()
    for side in range(2):
        load(RING // 2, side * (RING + 1), side, 2).start()
    load(order(1), 1).start()

    barrier = pltpu.get_barrier_semaphore()

    def other_chip(step):
        return wrap(chip + step, chips)

    def other_row(step):
        return wrap(r + step, count)

    def to_chip(step):
        return {"rows": other_chip(step) * 2 + core, "snaps": z}

    def to_row(step):
        return {"rows": other_row(step), "snaps": z}

    def to_depth(step):
        return {"rows": r, "snaps": at(step)}

    for there in [to_depth(step) for step in range(1, RING)] + [to_row(step) for step in range(1, count)]:
        pl.semaphore_signal(barrier, inc=1, device_id=there, device_id_type=MESH)

    def ring(side, src, dst, send, recv):
        return pltpu.make_async_remote_copy(
            src_ref=src,
            dst_ref=dst,
            send_sem=send,
            recv_sem=recv,
            device_id={"rows": r, "snaps": at(1 - 2 * side)},
            device_id_type=MESH,
        )

    def span_of(i):
        return pl.ds(0, size + 16) if i == 0 else pl.ds(size + 16, size)

    def data_of(i):
        return pl.ds(0, size) if i == 0 else pl.ds(size + 16, size)

    scale_rows = pl.ds(size, 16)

    def sum_copy(side, u, i):
        return ring(
            side,
            tx.at[side, u, span_of(i), :],
            rx.at[side, u, span_of(i), :],
            rs_send.at[side],
            rs_recv.at[side, 2 * u + i],
        )

    def piece(q):
        return pl.ds(pl.multiple_of(q * size, size), size)

    def sketch(slot):
        @pl.when(slot + 2 < RING)
        def _():
            load(order(slot + 2), slot + 2).start()

        load(order(slot), slot).wait()
        j = at(order(slot))
        rows = pl.ds(pl.multiple_of(j * shard, shard), shard)
        part[j] = jnp.dot(s[rows, :], k[...], preferred_element_type=F32)

    def pair_rows(j, side, u):
        first = 2 * size * (u % 2 if side == 0 else 1 - u % 2)
        return j, pl.ds(pl.multiple_of(first, 2 * size), 2 * size)

    def piece_rows(j, side, u, i):
        first = 2 * size * (u % 2 if side == 0 else 1 - u % 2) + i * size
        return j, pl.ds(pl.multiple_of(first, size), size)

    def set_scale(side, u, top):
        tx[side, u, scale_rows, :] = (top * 1.01 + 1e-30).astype(BF16)

    def set_data(side, u, i, value):
        tx[side, u, data_of(i), :] = encode(value, tx[side, u, scale_rows, :])

    def send(side, u, i, value):
        set_data(side, u, i, value)
        sum_copy(side, u, i).start()

    def came(side, u, i):
        return decode(rx[side, u, data_of(i), :], rx[side, u, scale_rows, :])

    def head(side, u, offset):
        j = at(offset)
        set_scale(side, u, peak(part[pair_rows(j, side, u)]))
        for i in range(2):
            send(side, u, i, part[piece_rows(j, side, u, i)])

    sketch_copy.wait()
    load(order(2), 2).start()
    for side in range(2):
        load(RING // 2, side * (RING + 1), side, 2).wait()
        first = side * 2 * size
        rows = pl.ds(pl.multiple_of(at(RING // 2) * shard + first, 2 * size), 2 * size)
        part[at(RING // 2), pl.ds(first, 2 * size), :] = jnp.dot(s[rows, :], k[...], preferred_element_type=F32)
        j = at(4)
        set_scale(side, 0, peak(part[pair_rows(j, side, 0)]))
        for i in range(2):
            set_data(side, 0, i, part[piece_rows(j, side, 0, i)])
        if side == 0:
            pl.semaphore_wait(barrier, count - 1 + RING - 1)
        for i in range(2):
            sum_copy(side, 0, i).start()
    for side in range(2):
        sketch(1 + side)
        head(side, 1, 3 - 6 * side)
    @pl.loop(3, RING)
    def _(slot):
        sketch(slot)

    @pl.loop(0, RING - 3)
    def _(u):
        far = 4 - (u + 1) // 2
        for i in range(2):
            for side in range(2):
                j = at((1 - 2 * side) * (far - 1))
                sum_copy(side, u, i).wait_recv()
                if i == 0:
                    set_scale(side, u + 2, rx[side, u, scale_rows, :].astype(F32) + peak(part[pair_rows(j, side, u)]))
                send(side, u + 2, i, part[piece_rows(j, side, u, i)] + came(side, u, i))

    def gather_copy(side, e, j, q):
        block = everyone.at[j, piece(q), :]
        return ring(side, block, block, ag_send, ag_recv.at[side, e])

    def gather_piece(side, e):
        hop = jnp.minimum(e // 4 + 1, 4)
        i = jnp.where(e < 12, e % 4, 2 * (e - 12))
        odd = i % 2
        return hop, 2 * (odd if side == 0 else 1 - odd) + i // 2

    def start_own(i):
        for side in range(2):
            for odd in range(2):
                e = 2 * i + odd
                gather_copy(side, e, z, gather_piece(side, e)[1]).start()

    def gram(pieces):
        rows = jnp.concatenate([part[z, piece(q), :] for q in pieces], axis=0)
        both = jnp.concatenate(split(rows), axis=1)
        gg[...] += lax.dot_general(both, both, (((0,), (0,)), ((), ())), preferred_element_type=F32)

    gg[...] = jnp.zeros_like(gg)
    for i in range(2):
        for side in range(2):
            sum_copy(side, RING - 3, i).wait_recv()
            part[piece_rows(z, side, RING - 3, i)] += came(side, RING - 3, i)
    for i in range(2):
        for side in range(2):
            sum_copy(side, RING - 2, i).wait_recv()
            mine = part[piece_rows(z, side, RING - 2, i)] + came(side, RING - 2, i)
            part[piece_rows(z, side, RING - 2, i)] = mine
            everyone[piece_rows(z, side, RING - 2, i)] = mine.astype(BF16)
        if i == 0:
            start_own(0)
        gram((i, 2 + i))

    g[...] = gg[:rank, :rank] + gg[:rank, rank:] + gg[rank:, :rank] + gg[rank:, rank:]
    for index in range(count):
        g0[index] = g[index * half : (index + 1) * half, :]

    def remote(src, dst, send_sem, recv_sem, there):
        return pltpu.make_async_remote_copy(
            src_ref=src,
            dst_ref=dst,
            send_sem=send_sem,
            recv_sem=recv_sem,
            device_id=there,
            device_id_type=MESH,
        )

    def g1_copy(step):
        return remote(g0.at[other_row(step)], g1.at[step], g1_sem.at[0], g1_sem.at[1], to_row(step))

    def g2_copy(step):
        return remote(g2.at[z], g2.at[z], g2_sem.at[0], g2_sem.at[1], to_depth(step))

    def g3_copy(step):
        return remote(g3.at[r], g3.at[r], g3_sem.at[0], g3_sem.at[1], to_row(step))

    def zr_copy(step):
        return remote(pair.at[other_chip(step)], zr.at[step], zr_sem.at[0], zr_sem.at[1], to_chip(step))

    def all_of(ref, number, sem):
        block = ref.at[pl.ds(0, number)]
        return remote(block, block, sem.at[0], sem.at[1], to_row(1))

    def start_all(copy, number):
        for step in range(1, number):
            copy(step).start()

    start_all(g1_copy, count)
    start_own(1)

    def term_of(pairs):
        left = [everyone[j, piece(q), :] for j, q in pairs]
        right = [s[pl.ds(pl.multiple_of(j * shard + q * size, size), size), :] for j, q in pairs]
        return lax.dot_general(
            jnp.concatenate(left, axis=0),
            jnp.concatenate(right, axis=0),
            (((0,), (0,)), ((), ())),
            preferred_element_type=F32,
        )

    def gather(e):
        came = []
        for side in range(2):
            hop, q = gather_piece(side, e)
            j = at(-(1 - 2 * side) * hop)
            came.append((j, q))
            gather_copy(side, e, j, q).wait_recv()

            @pl.when((e < 8) | (e == 8) | (e == 10))
            def _():
                gather_copy(side, jnp.where(e < 8, e + 4, 12 + (e - 8) // 2), j, q).start()

        return term_of(came)

    z_sum[...] = term_of([(z, q) for q in range(PIECES)])
    all_of(g1, count - 1, g1_sem).wait_recv()
    g1[0] = g0[r]
    g2[z] = jnp.sum(g1[...], axis=0)
    start_all(g2_copy, RING)

    @pl.loop(0, 2)
    def _(e):
        z_sum[...] += gather(e)

    all_of(g2, RING - 1, g2_sem).wait_recv()
    g3[r] = jnp.sum(g2[...], axis=0) * (1.0 / total)
    start_all(g3_copy, count)

    @pl.loop(2, 4)
    def _(e):
        z_sum[...] += gather(e)

    all_of(g3, count - 1, g3_sem).wait_recv()
    for index in range(count):
        g[index * half : (index + 1) * half, :] = g3[index]

    eye = lax.broadcasted_iota(jnp.int32, (rank, rank), 0) == lax.broadcasted_iota(jnp.int32, (rank, rank), 1)
    full = g[...]
    diagonal = jnp.where(eye, full, 0.0)
    down = lax.rsqrt(jnp.sum(diagonal, axis=1, keepdims=True))
    across = lax.rsqrt(jnp.sum(diagonal, axis=0, keepdims=True))
    x[...] = jnp.concatenate([full * down * across, jnp.where(eye, down, 0.0)], axis=1)

    @pl.loop(4, EVENTS - 2)
    def _(e):
        z_sum[...] += gather(e)
        factor_block(x, e - 4)

    z_sum[...] += gather(EVENTS - 2)

    l1, l2 = split(x[:, rank:])
    z1, z2 = split(z_sum[...] + gather(EVENTS - 1))
    term = jnp.dot(
        jnp.concatenate([l1, l2, l1], axis=1),
        jnp.concatenate([z1, z1, z2], axis=0),
        preferred_element_type=F32,
    ) * (1.0 / math.sqrt(total))
    z_sum[...] = term
    for c in range(chips):
        rows = z_sum[c * own : (c + 1) * own, :]
        low, high = rows[:half], rows[half:]
        give[c] = jnp.where(core == 0, high, low)
        pair[c] = jnp.where(core == 0, low, high)
    mate = remote(give, take, mate_send, mate_recv, {"rows": chip * 2 + 1 - core, "snaps": z})
    mate.start()
    i1, i2 = split(x[:, rank:])
    mate.wait_recv()
    pair[...] += take[...]

    start_all(zr_copy, chips)

    @pl.loop(0, PIECES)
    def _(q):
        y1, y2 = split(part[z, piece(q), :])
        basis_ref[piece(q), :] = lax.dot_general(
            jnp.concatenate([y1, y1, y2], axis=1),
            jnp.concatenate([i1, i2, i1], axis=1),
            (((1,), (1,)), ((), ())),
            preferred_element_type=F32,
        )

    mate.wait_send()

    for side in range(2):
        ring(side, tx.at[side], tx.at[side], rs_send.at[side], rs_recv.at[side, 0]).wait_send()
    sent = everyone.at[pl.ds(0, RING - 1)]
    ring(0, sent, sent, ag_send, ag_recv.at[0, 0]).wait_send()
    all_of(g1, count - 1, g1_sem).wait_send()
    all_of(g2, RING - 1, g2_sem).wait_send()
    all_of(g3, count - 1, g3_sem).wait_send()

    all_of(zr, chips - 1, zr_sem).wait_recv()
    zr[0] = pair[chip]
    proj_ref[...] = jnp.sum(zr[...], axis=0)
    all_of(zr, chips - 1, zr_sem).wait_send()


def finish(basis_in, proj_in, basis_out, proj_out, sem):
    copies = [pltpu.make_async_copy(proj_in, proj_out, sem.at[0])]
    size = basis_in.shape[0] // PIECES
    for q in range(PIECES):
        rows = pl.ds(q * size, size)
        copies.append(pltpu.make_async_copy(basis_in.at[rows, :], basis_out.at[rows, :], sem.at[1 + q]))
    for copy in copies:
        copy.start()
    for copy in copies:
        copy.wait()


def local(snapshots, sketch):
    rows, columns = snapshots.shape
    rank = sketch.shape[1]
    count = lax.axis_size("rows")
    chips = count // 2
    total = rows * count
    shard = rows // RING
    half = rank // count
    message = 2 * (shard // PIECES) + 16
    dma = pltpu.SemaphoreType.DMA
    outputs = (
        jax.ShapeDtypeStruct((shard, rank), F32),
        jax.ShapeDtypeStruct((half, columns), F32),
    )
    anywhere = pl.BlockSpec(memory_space=pl.ANY)
    basis, projected = pl.pallas_call(
        functools.partial(kernel, total),
        out_shape=tuple(pltpu.VMEM(out.shape, out.dtype) for out in outputs),
        in_specs=[anywhere] * 2,
        out_specs=(pl.BlockSpec(memory_space=pltpu.VMEM),) * 2,
        scratch_shapes=[
            pltpu.VMEM((rows, columns), BF16),
            pltpu.VMEM((columns, rank), BF16),
            pltpu.VMEM((RING, shard, rank), F32),
            pltpu.VMEM((2, RING - 1, message, rank), BF16),
            pltpu.VMEM((2, RING - 1, message, rank), BF16),
            pltpu.VMEM((RING, shard, rank), BF16),
            pltpu.VMEM((rank, columns), F32),
            pltpu.VMEM((2 * rank, 2 * rank), F32),
            pltpu.VMEM((rank, rank), F32),
            pltpu.VMEM((count, half, rank), F32),
            pltpu.VMEM((count, half, rank), F32),
            pltpu.VMEM((RING, half, rank), F32),
            pltpu.VMEM((count, half, rank), F32),
            pltpu.VMEM((rank, 2 * rank), F32),
            pltpu.VMEM((chips, half, columns), F32),
            pltpu.VMEM((chips, half, columns), F32),
            pltpu.VMEM((chips, half, columns), F32),
            pltpu.VMEM((chips, half, columns), F32),
            dma((RING + 2,)),
            dma((2,)),
            dma((2, EVENTS)),
            dma,
            dma((2, EVENTS)),
            dma((2,)),
            dma((2,)),
            dma((2,)),
            dma((2,)),
            dma,
            dma,
        ],
        compiler_params=pltpu.CompilerParams(
            collective_id=0, has_side_effects=True, vmem_limit_bytes=56 * 1024 * 1024
        ),
    )(snapshots, sketch)
    return pl.pallas_call(
        finish,
        out_shape=outputs,
        in_specs=[pl.BlockSpec(memory_space=pltpu.VMEM)] * 2,
        out_specs=(anywhere, anywhere),
        scratch_shapes=[dma((PIECES + 1,))],
        compiler_params=pltpu.CompilerParams(vmem_limit_bytes=16 * 1024 * 1024),
    )(basis, projected)


def solution(mesh):
    in_specs = (P("rows", "snaps"), P("snaps", None))
    out_specs = (P(("rows", "snaps"), None), P("rows", "snaps"))
    return jax.shard_map(local, mesh=mesh, in_specs=in_specs, out_specs=out_specs, check_vma=False)
```

```python
import functools
import math

import jax
import jax.numpy as jnp
from jax import lax
from jax.experimental import pallas as pl
from jax.experimental.pallas import tpu as pltpu
from jax.sharding import PartitionSpec as P

MESH = pl.DeviceIdType.MESH
HIGHEST = lax.Precision.HIGHEST
F32, BF16 = jnp.float32, jnp.bfloat16

RING = 8
PIECES = 4
EVENTS = 2 * (RING - 1)
SPAN = 120.0
BLOCK = 16


def groups_of(value):
    rows, rank = value.shape
    return value.reshape(rows // 16, 16, rank)


def peak(value):
    return jnp.max(jnp.abs(groups_of(value)), axis=0)


def encode(value, top):
    gain = SPAN / top.astype(F32)
    return jnp.exp2(groups_of(value) * gain[None]).reshape(value.shape).astype(BF16)


def decode(code, top):
    gain = top.astype(F32) * (1.0 / (SPAN * math.log(2.0)))
    return (jnp.log(groups_of(code.astype(F32))) * gain[None]).reshape(code.shape)


def split(value):
    high = value.astype(BF16)
    return high, (value - high.astype(F32)).astype(BF16)


def factor_block(x, block):
    rank = x.shape[0]
    first = pl.multiple_of(block * BLOCK, BLOCK)
    shape = (BLOCK, rank)
    panel = x[pl.ds(first, BLOCK), :]
    left, right = panel[:, :rank], panel[:, rank:]
    corner = pltpu.roll(left, lax.rem(rank - first, rank), 1)
    row = lax.broadcasted_iota(jnp.int32, shape, 0)
    lane = lax.broadcasted_iota(jnp.int32, shape, 1)
    columns = [jnp.broadcast_to(corner[:, j : j + 1], shape) for j in range(BLOCK)]

    def spread(value, i):
        return jnp.broadcast_to(value[i : i + 1, :], shape)

    first_pivot = cross = determinant = jnp.zeros(shape, F32)
    for i in range(0, BLOCK, 2):
        one, two = columns[i], columns[i + 1]
        a, b, d = spread(one, i), spread(one, i + 1), spread(two, i + 1)
        det = a * d - b * b
        here = (row == i) | (row == i + 1)
        first_pivot = jnp.where(here, a, first_pivot)
        cross = jnp.where(row == i + 1, b, cross)
        determinant = jnp.where(here, det, determinant)
        if i + 2 == BLOCK:
            break
        inverse = jnp.where(row > i + 1, 1.0 / det, 0.0)
        u, v = (one * d - two * b) * inverse, (two * a - one * b) * inverse
        for j in range(i + 2, BLOCK):
            columns[j] = columns[j] - (u * spread(columns[j], i) + v * spread(columns[j], i + 1))
        left = left - (u * spread(left, i) + v * spread(left, i + 1))
        right = right - (u * spread(right, i) + v * spread(right, i + 1))
    odd = row % 2 == 1
    factor = cross / first_pivot
    scale = jnp.where(odd, first_pivot * lax.rsqrt(first_pivot * determinant), lax.rsqrt(first_pivot))
    left = (left - factor * pltpu.roll(left, 1, 0)) * scale
    right = (right - factor * pltpu.roll(right, 1, 0)) * scale
    whole = jnp.concatenate([left, right], axis=1)
    x[pl.ds(first, BLOCK), :] = whole
    r1, r2 = split(whole)
    r3 = (whole - r1.astype(F32) - r2.astype(F32)).astype(BF16)
    later = jnp.where(lane >= first + BLOCK, left, 0.0)
    l1, l2 = split(later)
    l3 = (later - l1.astype(F32) - l2.astype(F32)).astype(BF16)
    x[...] -= lax.dot_general(
        jnp.concatenate([l1, l1, l2, l1, l2, l3], axis=0),
        jnp.concatenate([r1, r2, r1, r3, r2, r1], axis=0),
        (((0,), (0,)), ((), ())),
        preferred_element_type=F32,
    )


def kernel(
    total, s_hbm, k_hbm, basis_ref, proj_ref,
    s, k, part, tx, rx, everyone, z_sum, gg, g, g0, g1, g2, g3, x, pair, zr,
    load_sem, rs_send, rs_recv, ag_send, ag_recv, g1_sem, g2_sem, g3_sem, zr_sem,
):
    count = lax.axis_size("rows")
    r, z = lax.axis_index("rows"), lax.axis_index("snaps")
    shard = part.shape[1]
    size = shard // PIECES
    rank = k.shape[1]
    half = rank // count

    def wrap(index, length):
        index = jnp.where(index >= length, index - length, index)
        return jnp.where(index < 0, index + length, index)

    def at(step):
        return wrap(z + step, RING)

    def load(offset, slot, part_of=0, parts=1):
        length = shard // parts
        rows = pl.ds(pl.multiple_of(at(offset) * shard + part_of * length, length), length)
        return pltpu.make_async_copy(s_hbm.at[rows, :], s.at[rows, :], load_sem.at[slot])

    def order(slot):
        return (RING - slot) // 2 * (1 - 2 * ((slot + 1) % 2))

    sketch_copy = pltpu.make_async_copy(k_hbm, k, load_sem.at[RING])
    sketch_copy.start()
    for side in range(2):
        load(RING // 2, side * (RING + 1), side, 2).start()
    load(order(1), 1).start()

    barrier = pltpu.get_barrier_semaphore()

    def other_row(step):
        return wrap(r + step, count)

    def to_row(step):
        return {"rows": other_row(step), "snaps": z}

    def to_depth(step):
        return {"rows": r, "snaps": at(step)}

    for there in [to_depth(step) for step in range(1, RING)] + [to_row(step) for step in range(1, count)]:
        pl.semaphore_signal(barrier, inc=1, device_id=there, device_id_type=MESH)

    def ring(side, src, dst, send, recv):
        return pltpu.make_async_remote_copy(
            src_ref=src,
            dst_ref=dst,
            send_sem=send,
            recv_sem=recv,
            device_id={"rows": r, "snaps": at(1 - 2 * side)},
            device_id_type=MESH,
        )

    def span_of(i):
        return pl.ds(0, size + 16) if i == 0 else pl.ds(size + 16, size)

    def data_of(i):
        return pl.ds(0, size) if i == 0 else pl.ds(size + 16, size)

    scale_rows = pl.ds(size, 16)

    def sum_copy(side, u, i):
        return ring(
            side,
            tx.at[side, u, span_of(i), :],
            rx.at[side, u, span_of(i), :],
            rs_send.at[side],
            rs_recv.at[side, 2 * u + i],
        )

    def piece(q):
        return pl.ds(pl.multiple_of(q * size, size), size)

    def sketch(slot):
        @pl.when(slot + 2 < RING)
        def _():
            load(order(slot + 2), slot + 2).start()

        load(order(slot), slot).wait()
        j = at(order(slot))
        rows = pl.ds(pl.multiple_of(j * shard, shard), shard)
        part[j] = jnp.dot(s[rows, :], k[...], preferred_element_type=F32)

    def pair_rows(j, side, u):
        first = 2 * size * (u % 2 if side == 0 else 1 - u % 2)
        return j, pl.ds(pl.multiple_of(first, 2 * size), 2 * size)

    def piece_rows(j, side, u, i):
        first = 2 * size * (u % 2 if side == 0 else 1 - u % 2) + i * size
        return j, pl.ds(pl.multiple_of(first, size), size)

    def set_scale(side, u, top):
        tx[side, u, scale_rows, :] = (top * 1.01 + 1e-30).astype(BF16)

    def set_data(side, u, i, value):
        tx[side, u, data_of(i), :] = encode(value, tx[side, u, scale_rows, :])

    def send(side, u, i, value):
        set_data(side, u, i, value)
        sum_copy(side, u, i).start()

    def came(side, u, i):
        return decode(rx[side, u, data_of(i), :], rx[side, u, scale_rows, :])

    def head(side, u, offset):
        j = at(offset)
        set_scale(side, u, peak(part[pair_rows(j, side, u)]))
        for i in range(2):
            send(side, u, i, part[piece_rows(j, side, u, i)])

    sketch_copy.wait()
    load(order(2), 2).start()
    for side in range(2):
        load(RING // 2, side * (RING + 1), side, 2).wait()
        first = side * 2 * size
        rows = pl.ds(pl.multiple_of(at(RING // 2) * shard + first, 2 * size), 2 * size)
        part[at(RING // 2), pl.ds(first, 2 * size), :] = jnp.dot(s[rows, :], k[...], preferred_element_type=F32)
        j = at(4)
        set_scale(side, 0, peak(part[pair_rows(j, side, 0)]))
        for i in range(2):
            set_data(side, 0, i, part[piece_rows(j, side, 0, i)])
        if side == 0:
            pl.semaphore_wait(barrier, count - 1 + RING - 1)
        for i in range(2):
            sum_copy(side, 0, i).start()
    for side in range(2):
        sketch(1 + side)
        head(side, 1, 3 - 6 * side)
    @pl.loop(3, RING)
    def _(slot):
        sketch(slot)

    @pl.loop(0, RING - 3)
    def _(u):
        far = 4 - (u + 1) // 2
        for i in range(2):
            for side in range(2):
                j = at((1 - 2 * side) * (far - 1))
                sum_copy(side, u, i).wait_recv()
                if i == 0:
                    set_scale(side, u + 2, rx[side, u, scale_rows, :].astype(F32) + peak(part[pair_rows(j, side, u)]))
                send(side, u + 2, i, part[piece_rows(j, side, u, i)] + came(side, u, i))

    def gather_copy(side, e, j, q):
        block = everyone.at[j, piece(q), :]
        return ring(side, block, block, ag_send, ag_recv.at[side, e])

    def gather_piece(side, e):
        hop = jnp.minimum(e // 4 + 1, 4)
        i = jnp.where(e < 12, e % 4, 2 * (e - 12))
        odd = i % 2
        return hop, 2 * (odd if side == 0 else 1 - odd) + i // 2

    def start_own(i):
        for side in range(2):
            for odd in range(2):
                e = 2 * i + odd
                gather_copy(side, e, z, gather_piece(side, e)[1]).start()

    def gram(pieces):
        rows = jnp.concatenate([part[z, piece(q), :] for q in pieces], axis=0)
        both = jnp.concatenate(split(rows), axis=1)
        gg[...] += lax.dot_general(both, both, (((0,), (0,)), ((), ())), preferred_element_type=F32)

    gg[...] = jnp.zeros_like(gg)
    for i in range(2):
        for side in range(2):
            sum_copy(side, RING - 3, i).wait_recv()
            part[piece_rows(z, side, RING - 3, i)] += came(side, RING - 3, i)
    for i in range(2):
        for side in range(2):
            sum_copy(side, RING - 2, i).wait_recv()
            mine = part[piece_rows(z, side, RING - 2, i)] + came(side, RING - 2, i)
            part[piece_rows(z, side, RING - 2, i)] = mine
            everyone[piece_rows(z, side, RING - 2, i)] = mine.astype(BF16)
        if i == 0:
            start_own(0)
        gram((i, 2 + i))

    g[...] = gg[:rank, :rank] + gg[:rank, rank:] + gg[rank:, :rank] + gg[rank:, rank:]
    for index in range(count):
        g0[index] = g[index * half : (index + 1) * half, :]

    def remote(src, dst, send_sem, recv_sem, there):
        return pltpu.make_async_remote_copy(
            src_ref=src,
            dst_ref=dst,
            send_sem=send_sem,
            recv_sem=recv_sem,
            device_id=there,
            device_id_type=MESH,
        )

    def g1_copy(step):
        return remote(g0.at[other_row(step)], g1.at[step], g1_sem.at[0], g1_sem.at[1], to_row(step))

    def g2_copy(step):
        return remote(g2.at[z], g2.at[z], g2_sem.at[0], g2_sem.at[1], to_depth(step))

    def g3_copy(step):
        return remote(g3.at[r], g3.at[r], g3_sem.at[0], g3_sem.at[1], to_row(step))

    def zr_copy(step):
        return remote(pair.at[other_row(step)], zr.at[step], zr_sem.at[0], zr_sem.at[1], to_row(step))

    def all_of(ref, number, sem):
        block = ref.at[pl.ds(0, number)]
        return remote(block, block, sem.at[0], sem.at[1], to_row(1))

    def start_all(copy, number):
        for step in range(1, number):
            copy(step).start()

    start_all(g1_copy, count)
    start_own(1)

    def term_of(pairs):
        left = [everyone[j, piece(q), :] for j, q in pairs]
        right = [s[pl.ds(pl.multiple_of(j * shard + q * size, size), size), :] for j, q in pairs]
        return lax.dot_general(
            jnp.concatenate(left, axis=0),
            jnp.concatenate(right, axis=0),
            (((0,), (0,)), ((), ())),
            preferred_element_type=F32,
        )

    def gather(e):
        came = []
        for side in range(2):
            hop, q = gather_piece(side, e)
            j = at(-(1 - 2 * side) * hop)
            came.append((j, q))
            gather_copy(side, e, j, q).wait_recv()

            @pl.when((e < 8) | (e == 8) | (e == 10))
            def _():
                gather_copy(side, jnp.where(e < 8, e + 4, 12 + (e - 8) // 2), j, q).start()

        return term_of(came)

    z_sum[...] = term_of([(z, q) for q in range(PIECES)])
    all_of(g1, count - 1, g1_sem).wait_recv()
    g1[0] = g0[r]
    g2[z] = jnp.sum(g1[...], axis=0)
    start_all(g2_copy, RING)

    @pl.loop(0, 2)
    def _(e):
        z_sum[...] += gather(e)

    all_of(g2, RING - 1, g2_sem).wait_recv()
    g3[r] = jnp.sum(g2[...], axis=0) * (1.0 / total)
    start_all(g3_copy, count)

    @pl.loop(2, 4)
    def _(e):
        z_sum[...] += gather(e)

    all_of(g3, count - 1, g3_sem).wait_recv()
    for index in range(count):
        g[index * half : (index + 1) * half, :] = g3[index]

    eye = lax.broadcasted_iota(jnp.int32, (rank, rank), 0) == lax.broadcasted_iota(jnp.int32, (rank, rank), 1)
    full = g[...]
    diagonal = jnp.where(eye, full, 0.0)
    down = lax.rsqrt(jnp.sum(diagonal, axis=1, keepdims=True))
    across = lax.rsqrt(jnp.sum(diagonal, axis=0, keepdims=True))
    x[...] = jnp.concatenate([full * down * across, jnp.where(eye, down, 0.0)], axis=1)

    @pl.loop(4, EVENTS - 2)
    def _(e):
        z_sum[...] += gather(e)
        factor_block(x, e - 4)

    z_sum[...] += gather(EVENTS - 2)

    l1, l2 = split(x[:, rank:])
    z1, z2 = split(z_sum[...] + gather(EVENTS - 1))
    term = jnp.dot(
        jnp.concatenate([l1, l2, l1], axis=1),
        jnp.concatenate([z1, z1, z2], axis=0),
        preferred_element_type=F32,
    ) * (1.0 / math.sqrt(total))
    z_sum[...] = term
    for index in range(count):
        pair[index] = z_sum[index * half : (index + 1) * half, :]
    start_all(zr_copy, count)
    i1, i2 = split(x[:, rank:])

    @pl.loop(0, PIECES)
    def _(q):
        y1, y2 = split(part[z, piece(q), :])
        basis_ref[piece(q), :] = lax.dot_general(
            jnp.concatenate([y1, y1, y2], axis=1),
            jnp.concatenate([i1, i2, i1], axis=1),
            (((1,), (1,)), ((), ())),
            preferred_element_type=F32,
        )

    for side in range(2):
        ring(side, tx.at[side], tx.at[side], rs_send.at[side], rs_recv.at[side, 0]).wait_send()
    sent = everyone.at[pl.ds(0, RING - 1)]
    ring(0, sent, sent, ag_send, ag_recv.at[0, 0]).wait_send()
    all_of(g1, count - 1, g1_sem).wait_send()
    all_of(g2, RING - 1, g2_sem).wait_send()
    all_of(g3, count - 1, g3_sem).wait_send()

    all_of(zr, count - 1, zr_sem).wait_recv()
    zr[0] = pair[r]
    proj_ref[...] = jnp.sum(zr[...], axis=0)
    all_of(zr, count - 1, zr_sem).wait_send()


def finish(basis_in, proj_in, basis_out, proj_out, sem):
    copies = [pltpu.make_async_copy(proj_in, proj_out, sem.at[0])]
    size = basis_in.shape[0] // PIECES
    for q in range(PIECES):
        rows = pl.ds(q * size, size)
        copies.append(pltpu.make_async_copy(basis_in.at[rows, :], basis_out.at[rows, :], sem.at[1 + q]))
    for copy in copies:
        copy.start()
    for copy in copies:
        copy.wait()


def local(snapshots, sketch):
    rows, columns = snapshots.shape
    rank = sketch.shape[1]
    count = lax.axis_size("rows")
    total = rows * count
    shard = rows // RING
    half = rank // count
    message = 2 * (shard // PIECES) + 16
    dma = pltpu.SemaphoreType.DMA
    outputs = (
        jax.ShapeDtypeStruct((shard, rank), F32),
        jax.ShapeDtypeStruct((half, columns), F32),
    )
    anywhere = pl.BlockSpec(memory_space=pl.ANY)
    basis, projected = pl.pallas_call(
        functools.partial(kernel, total),
        out_shape=tuple(pltpu.VMEM(out.shape, out.dtype) for out in outputs),
        in_specs=[anywhere] * 2,
        out_specs=(pl.BlockSpec(memory_space=pltpu.VMEM),) * 2,
        scratch_shapes=[
            pltpu.VMEM((rows, columns), BF16),
            pltpu.VMEM((columns, rank), BF16),
            pltpu.VMEM((RING, shard, rank), F32),
            pltpu.VMEM((2, RING - 1, message, rank), BF16),
            pltpu.VMEM((2, RING - 1, message, rank), BF16),
            pltpu.VMEM((RING, shard, rank), BF16),
            pltpu.VMEM((rank, columns), F32),
            pltpu.VMEM((2 * rank, 2 * rank), F32),
            pltpu.VMEM((rank, rank), F32),
            pltpu.VMEM((count, half, rank), F32),
            pltpu.VMEM((count, half, rank), F32),
            pltpu.VMEM((RING, half, rank), F32),
            pltpu.VMEM((count, half, rank), F32),
            pltpu.VMEM((rank, 2 * rank), F32),
            pltpu.VMEM((count, half, columns), F32),
            pltpu.VMEM((count, half, columns), F32),
            dma((RING + 2,)),
            dma((2,)),
            dma((2, EVENTS)),
            dma,
            dma((2, EVENTS)),
            dma((2,)),
            dma((2,)),
            dma((2,)),
            dma((2,)),
        ],
        compiler_params=pltpu.CompilerParams(
            collective_id=0, has_side_effects=True, vmem_limit_bytes=56 * 1024 * 1024
        ),
    )(snapshots, sketch)
    return pl.pallas_call(
        finish,
        out_shape=outputs,
        in_specs=[pl.BlockSpec(memory_space=pltpu.VMEM)] * 2,
        out_specs=(anywhere, anywhere),
        scratch_shapes=[dma((PIECES + 1,))],
        compiler_params=pltpu.CompilerParams(vmem_limit_bytes=16 * 1024 * 1024),
    )(basis, projected)


def solution(mesh):
    in_specs = (P("rows", "snaps"), P("snaps", None))
    out_specs = (P(("rows", "snaps"), None), P("rows", "snaps"))
    return jax.shard_map(local, mesh=mesh, in_specs=in_specs, out_specs=out_specs, check_vma=False)
```

```python
import functools
import math

import jax
import jax.numpy as jnp
from jax import lax
from jax.experimental import pallas as pl
from jax.experimental.pallas import tpu as pltpu
from jax.sharding import PartitionSpec as P

MESH = pl.DeviceIdType.MESH
HIGHEST = lax.Precision.HIGHEST
F32, BF16 = jnp.float32, jnp.bfloat16

RING = 8
PIECES = 4
EVENTS = 2 * (RING - 1)
SPAN = 120.0
BLOCK = 16


def groups_of(value):
    rows, rank = value.shape
    return value.reshape(rows // 16, 16, rank)


def peak(value):
    return jnp.max(jnp.abs(groups_of(value)), axis=0)


def encode(value, top):
    gain = SPAN / top.astype(F32)
    return jnp.exp2(groups_of(value) * gain[None]).reshape(value.shape).astype(BF16)


def decode(code, top):
    gain = top.astype(F32) * (1.0 / (SPAN * math.log(2.0)))
    return (jnp.log(groups_of(code.astype(F32))) * gain[None]).reshape(code.shape)


def split(value):
    high = value.astype(BF16)
    return high, (value - high.astype(F32)).astype(BF16)


def factor_block(x, block):
    rank = x.shape[0]
    first = pl.multiple_of(block * BLOCK, BLOCK)
    shape = (BLOCK, rank)
    panel = x[pl.ds(first, BLOCK), :]
    left, right = panel[:, :rank], panel[:, rank:]
    corner = pltpu.roll(left, lax.rem(rank - first, rank), 1)
    row = lax.broadcasted_iota(jnp.int32, shape, 0)
    lane = lax.broadcasted_iota(jnp.int32, shape, 1)
    columns = [jnp.broadcast_to(corner[:, j : j + 1], shape) for j in range(BLOCK)]

    def spread(value, i):
        return jnp.broadcast_to(value[i : i + 1, :], shape)

    first_pivot = cross = determinant = jnp.zeros(shape, F32)
    for i in range(0, BLOCK, 2):
        one, two = columns[i], columns[i + 1]
        a, b, d = spread(one, i), spread(one, i + 1), spread(two, i + 1)
        det = a * d - b * b
        here = (row == i) | (row == i + 1)
        first_pivot = jnp.where(here, a, first_pivot)
        cross = jnp.where(row == i + 1, b, cross)
        determinant = jnp.where(here, det, determinant)
        if i + 2 == BLOCK:
            break
        inverse = jnp.where(row > i + 1, 1.0 / det, 0.0)
        u, v = (one * d - two * b) * inverse, (two * a - one * b) * inverse
        for j in range(i + 2, BLOCK):
            columns[j] = columns[j] - (u * spread(columns[j], i) + v * spread(columns[j], i + 1))
        left = left - (u * spread(left, i) + v * spread(left, i + 1))
        right = right - (u * spread(right, i) + v * spread(right, i + 1))
    odd = row % 2 == 1
    factor = cross / first_pivot
    scale = jnp.where(odd, first_pivot * lax.rsqrt(first_pivot * determinant), lax.rsqrt(first_pivot))
    left = (left - factor * pltpu.roll(left, 1, 0)) * scale
    right = (right - factor * pltpu.roll(right, 1, 0)) * scale
    whole = jnp.concatenate([left, right], axis=1)
    x[pl.ds(first, BLOCK), :] = whole
    r1, r2 = split(whole)
    r3 = (whole - r1.astype(F32) - r2.astype(F32)).astype(BF16)
    later = jnp.where(lane >= first + BLOCK, left, 0.0)
    l1, l2 = split(later)
    l3 = (later - l1.astype(F32) - l2.astype(F32)).astype(BF16)
    x[...] -= lax.dot_general(
        jnp.concatenate([l1, l1, l2, l1, l2, l3], axis=0),
        jnp.concatenate([r1, r2, r1, r3, r2, r1], axis=0),
        (((0,), (0,)), ((), ())),
        preferred_element_type=F32,
    )


def kernel(
    total, s_hbm, k_hbm, basis_ref, proj_ref,
    s, k, part, tx, rx, everyone, z_sum, gg, g, g0, g1, g2, g3, x, give, take, pair, zr,
    load_sem, rs_send, rs_recv, ag_send, ag_recv, g1_sem, g2_sem, g3_sem, zr_sem, mate_send, mate_recv,
):
    count = lax.axis_size("rows")
    chips = count // 2
    r, z = lax.axis_index("rows"), lax.axis_index("snaps")
    chip, core = lax.div(r, 2), lax.rem(r, 2)
    shard = part.shape[1]
    size = shard // PIECES
    rank = k.shape[1]
    own = rank // chips
    half = rank // count

    def wrap(index, length):
        index = jnp.where(index >= length, index - length, index)
        return jnp.where(index < 0, index + length, index)

    def at(step):
        return wrap(z + step, RING)

    def load(offset, slot, part_of=0, parts=1):
        length = shard // parts
        rows = pl.ds(pl.multiple_of(at(offset) * shard + part_of * length, length), length)
        return pltpu.make_async_copy(s_hbm.at[rows, :], s.at[rows, :], load_sem.at[slot])

    def order(slot):
        return (RING - slot) // 2 * (1 - 2 * ((slot + 1) % 2))

    sketch_copy = pltpu.make_async_copy(k_hbm, k, load_sem.at[RING])
    sketch_copy.start()
    for side in range(2):
        load(RING // 2, side * (RING + 1), side, 2).start()
    load(order(1), 1).start()

    barrier = pltpu.get_barrier_semaphore()

    def other_chip(step):
        return wrap(chip + step, chips)

    def other_row(step):
        return wrap(r + step, count)

    def to_chip(step):
        return {"rows": other_chip(step) * 2 + core, "snaps": z}

    def to_row(step):
        return {"rows": other_row(step), "snaps": z}

    def to_depth(step):
        return {"rows": r, "snaps": at(step)}

    for there in [to_depth(step) for step in range(1, RING)] + [to_row(step) for step in range(1, count)]:
        pl.semaphore_signal(barrier, inc=1, device_id=there, device_id_type=MESH)

    def ring(side, src, dst, send, recv):
        return pltpu.make_async_remote_copy(
            src_ref=src,
            dst_ref=dst,
            send_sem=send,
            recv_sem=recv,
            device_id={"rows": r, "snaps": at(1 - 2 * side)},
            device_id_type=MESH,
        )

    def span_of(i):
        return pl.ds(0, size + 16) if i == 0 else pl.ds(size + 16, size)

    def data_of(i):
        return pl.ds(0, size) if i == 0 else pl.ds(size + 16, size)

    scale_rows = pl.ds(size, 16)

    def sum_copy(side, u, i):
        return ring(
            side,
            tx.at[side, u, span_of(i), :],
            rx.at[side, u, span_of(i), :],
            rs_send.at[side],
            rs_recv.at[side, 2 * u + i],
        )

    def piece(q):
        return pl.ds(pl.multiple_of(q * size, size), size)

    def sketch(slot):
        @pl.when(slot + 2 < RING)
        def _():
            load(order(slot + 2), slot + 2).start()

        load(order(slot), slot).wait()
        j = at(order(slot))
        rows = pl.ds(pl.multiple_of(j * shard, shard), shard)
        part[j] = jnp.dot(s[rows, :], k[...], preferred_element_type=F32)

    def pair_rows(j, side, u):
        first = 2 * size * (u % 2 if side == 0 else 1 - u % 2)
        return j, pl.ds(pl.multiple_of(first, 2 * size), 2 * size)

    def piece_rows(j, side, u, i):
        first = 2 * size * (u % 2 if side == 0 else 1 - u % 2) + i * size
        return j, pl.ds(pl.multiple_of(first, size), size)

    def set_scale(side, u, top):
        tx[side, u, scale_rows, :] = (top * 1.01 + 1e-30).astype(BF16)

    def set_data(side, u, i, value):
        tx[side, u, data_of(i), :] = encode(value, tx[side, u, scale_rows, :])

    def send(side, u, i, value):
        set_data(side, u, i, value)
        sum_copy(side, u, i).start()

    def came(side, u, i):
        return decode(rx[side, u, data_of(i), :], rx[side, u, scale_rows, :])

    def head(side, u, offset):
        j = at(offset)
        set_scale(side, u, peak(part[pair_rows(j, side, u)]))
        for i in range(2):
            send(side, u, i, part[piece_rows(j, side, u, i)])

    sketch_copy.wait()
    load(order(2), 2).start()
    for side in range(2):
        load(RING // 2, side * (RING + 1), side, 2).wait()
        first = side * 2 * size
        rows = pl.ds(pl.multiple_of(at(RING // 2) * shard + first, 2 * size), 2 * size)
        part[at(RING // 2), pl.ds(first, 2 * size), :] = jnp.dot(s[rows, :], k[...], preferred_element_type=F32)
        j = at(4)
        set_scale(side, 0, peak(part[pair_rows(j, side, 0)]))
        for i in range(2):
            set_data(side, 0, i, part[piece_rows(j, side, 0, i)])
        if side == 0:
            pl.semaphore_wait(barrier, count - 1 + RING - 1)
        for i in range(2):
            sum_copy(side, 0, i).start()
    for side in range(2):
        sketch(1 + side)
        head(side, 1, 3 - 6 * side)
    @pl.loop(3, RING)
    def _(slot):
        sketch(slot)

    @pl.loop(0, RING - 3)
    def _(u):
        far = 4 - (u + 1) // 2
        for i in range(2):
            for side in range(2):
                j = at((1 - 2 * side) * (far - 1))
                sum_copy(side, u, i).wait_recv()
                if i == 0:
                    set_scale(side, u + 2, rx[side, u, scale_rows, :].astype(F32) + peak(part[pair_rows(j, side, u)]))
                send(side, u + 2, i, part[piece_rows(j, side, u, i)] + came(side, u, i))

    def gather_copy(side, e, j, q):
        block = everyone.at[j, piece(q), :]
        return ring(side, block, block, ag_send, ag_recv.at[side, e])

    def gather_piece(side, e):
        hop = jnp.minimum(e // 4 + 1, 4)
        i = jnp.where(e < 12, e % 4, 2 * (e - 12))
        odd = i % 2
        return hop, 2 * (odd if side == 0 else 1 - odd) + i // 2

    def start_own(i):
        for side in range(2):
            for odd in range(2):
                e = 2 * i + odd
                gather_copy(side, e, z, gather_piece(side, e)[1]).start()

    def gram(pieces):
        rows = jnp.concatenate([part[z, piece(q), :] for q in pieces], axis=0)
        both = jnp.concatenate(split(rows), axis=1)
        gg[...] += lax.dot_general(both, both, (((0,), (0,)), ((), ())), preferred_element_type=F32)

    gg[...] = jnp.zeros_like(gg)
    for i in range(2):
        for side in range(2):
            sum_copy(side, RING - 3, i).wait_recv()
            part[piece_rows(z, side, RING - 3, i)] += came(side, RING - 3, i)
    for i in range(2):
        for side in range(2):
            sum_copy(side, RING - 2, i).wait_recv()
            mine = part[piece_rows(z, side, RING - 2, i)] + came(side, RING - 2, i)
            part[piece_rows(z, side, RING - 2, i)] = mine
            everyone[piece_rows(z, side, RING - 2, i)] = mine.astype(BF16)
        if i == 0:
            start_own(0)
        gram((i, 2 + i))

    g[...] = gg[:rank, :rank] + gg[:rank, rank:] + gg[rank:, :rank] + gg[rank:, rank:]
    for index in range(count):
        g0[index] = g[index * half : (index + 1) * half, :]

    def remote(src, dst, send_sem, recv_sem, there):
        return pltpu.make_async_remote_copy(
            src_ref=src,
            dst_ref=dst,
            send_sem=send_sem,
            recv_sem=recv_sem,
            device_id=there,
            device_id_type=MESH,
        )

    def g1_copy(step):
        return remote(g0.at[other_row(step)], g1.at[step], g1_sem.at[0], g1_sem.at[1], to_row(step))

    def g2_copy(step):
        return remote(g2.at[z], g2.at[z], g2_sem.at[0], g2_sem.at[1], to_depth(step))

    def g3_copy(step):
        return remote(g3.at[r], g3.at[r], g3_sem.at[0], g3_sem.at[1], to_row(step))

    def zr_copy(step):
        return remote(pair.at[other_chip(step)], zr.at[step], zr_sem.at[0], zr_sem.at[1], to_chip(step))

    def all_of(ref, number, sem):
        block = ref.at[pl.ds(0, number)]
        return remote(block, block, sem.at[0], sem.at[1], to_row(1))

    def start_all(copy, number):
        for step in range(1, number):
            copy(step).start()

    start_all(g1_copy, count)
    start_own(1)

    def term_of(pairs):
        left = [everyone[j, piece(q), :] for j, q in pairs]
        right = [s[pl.ds(pl.multiple_of(j * shard + q * size, size), size), :] for j, q in pairs]
        return lax.dot_general(
            jnp.concatenate(left, axis=0),
            jnp.concatenate(right, axis=0),
            (((0,), (0,)), ((), ())),
            preferred_element_type=F32,
        )

    def gather(e):
        came = []
        for side in range(2):
            hop, q = gather_piece(side, e)
            j = at(-(1 - 2 * side) * hop)
            came.append((j, q))
            gather_copy(side, e, j, q).wait_recv()

            @pl.when((e < 8) | (e == 8) | (e == 10))
            def _():
                gather_copy(side, jnp.where(e < 8, e + 4, 12 + (e - 8) // 2), j, q).start()

        return term_of(came)

    z_sum[...] = term_of([(z, q) for q in range(PIECES)])
    all_of(g1, count - 1, g1_sem).wait_recv()
    g1[0] = g0[r]
    g2[z] = jnp.sum(g1[...], axis=0)
    start_all(g2_copy, RING)

    @pl.loop(0, 2)
    def _(e):
        z_sum[...] += gather(e)

    all_of(g2, RING - 1, g2_sem).wait_recv()
    g3[r] = jnp.sum(g2[...], axis=0) * (1.0 / total)
    start_all(g3_copy, count)

    @pl.loop(2, 4)
    def _(e):
        z_sum[...] += gather(e)

    all_of(g3, count - 1, g3_sem).wait_recv()
    for index in range(count):
        g[index * half : (index + 1) * half, :] = g3[index]

    eye = lax.broadcasted_iota(jnp.int32, (rank, rank), 0) == lax.broadcasted_iota(jnp.int32, (rank, rank), 1)
    full = g[...]
    diagonal = jnp.where(eye, full, 0.0)
    down = lax.rsqrt(jnp.sum(diagonal, axis=1, keepdims=True))
    across = lax.rsqrt(jnp.sum(diagonal, axis=0, keepdims=True))
    x[...] = jnp.concatenate([full * down * across, jnp.where(eye, down, 0.0)], axis=1)

    @pl.loop(4, EVENTS - 2)
    def _(e):
        z_sum[...] += gather(e)
        factor_block(x, e - 4)

    z_sum[...] += gather(EVENTS - 2)

    l1, l2 = split(x[:, rank:])
    whole = z_sum[...]
    for side in range(2):
        hop, q = gather_piece(side, EVENTS - 1)
        j = at(-(1 - 2 * side) * hop)
        gather_copy(side, EVENTS - 1, j, q).wait_recv()
        whole = whole + term_of([(j, q)])
    z1, z2 = split(whole)
    term = jnp.dot(
        jnp.concatenate([l1, l2, l1], axis=1),
        jnp.concatenate([z1, z1, z2], axis=0),
        preferred_element_type=F32,
    ) * (1.0 / math.sqrt(total))
    z_sum[...] = term
    for c in range(chips):
        rows = z_sum[c * own : (c + 1) * own, :]
        low, high = rows[:half], rows[half:]
        give[c] = jnp.where(core == 0, high, low)
        pair[c] = jnp.where(core == 0, low, high)
    mate = remote(give, take, mate_send, mate_recv, {"rows": chip * 2 + 1 - core, "snaps": z})
    mate.start()
    i1, i2 = split(x[:, rank:])
    mate.wait_recv()
    pair[...] += take[...]

    for step in sorted(range(1, chips), key=lambda step: -min(step // 4, 4 - step // 4) - min(step % 4, 4 - step % 4)):
        zr_copy(step).start()

    @pl.loop(0, PIECES)
    def _(q):
        y1, y2 = split(part[z, piece(q), :])
        basis_ref[piece(q), :] = lax.dot_general(
            jnp.concatenate([y1, y1, y2], axis=1),
            jnp.concatenate([i1, i2, i1], axis=1),
            (((1,), (1,)), ((), ())),
            preferred_element_type=F32,
        )

    mate.wait_send()

    for side in range(2):
        ring(side, tx.at[side], tx.at[side], rs_send.at[side], rs_recv.at[side, 0]).wait_send()
    sent = everyone.at[pl.ds(0, RING - 1)]
    ring(0, sent, sent, ag_send, ag_recv.at[0, 0]).wait_send()
    all_of(g1, count - 1, g1_sem).wait_send()
    all_of(g2, RING - 1, g2_sem).wait_send()
    all_of(g3, count - 1, g3_sem).wait_send()

    all_of(zr, chips - 1, zr_sem).wait_recv()
    zr[0] = pair[chip]
    proj_ref[...] = jnp.sum(zr[...], axis=0)
    all_of(zr, chips - 1, zr_sem).wait_send()


def finish(basis_in, proj_in, basis_out, proj_out, sem):
    copies = [pltpu.make_async_copy(proj_in, proj_out, sem.at[0])]
    size = basis_in.shape[0] // PIECES
    for q in range(PIECES):
        rows = pl.ds(q * size, size)
        copies.append(pltpu.make_async_copy(basis_in.at[rows, :], basis_out.at[rows, :], sem.at[1 + q]))
    for copy in copies:
        copy.start()
    for copy in copies:
        copy.wait()


def local(snapshots, sketch):
    rows, columns = snapshots.shape
    rank = sketch.shape[1]
    count = lax.axis_size("rows")
    chips = count // 2
    total = rows * count
    shard = rows // RING
    half = rank // count
    message = 2 * (shard // PIECES) + 16
    dma = pltpu.SemaphoreType.DMA
    outputs = (
        jax.ShapeDtypeStruct((shard, rank), F32),
        jax.ShapeDtypeStruct((half, columns), F32),
    )
    anywhere = pl.BlockSpec(memory_space=pl.ANY)
    basis, projected = pl.pallas_call(
        functools.partial(kernel, total),
        out_shape=tuple(pltpu.VMEM(out.shape, out.dtype) for out in outputs),
        in_specs=[anywhere] * 2,
        out_specs=(pl.BlockSpec(memory_space=pltpu.VMEM),) * 2,
        scratch_shapes=[
            pltpu.VMEM((rows, columns), BF16),
            pltpu.VMEM((columns, rank), BF16),
            pltpu.VMEM((RING, shard, rank), F32),
            pltpu.VMEM((2, RING - 1, message, rank), BF16),
            pltpu.VMEM((2, RING - 1, message, rank), BF16),
            pltpu.VMEM((RING, shard, rank), BF16),
            pltpu.VMEM((rank, columns), F32),
            pltpu.VMEM((2 * rank, 2 * rank), F32),
            pltpu.VMEM((rank, rank), F32),
            pltpu.VMEM((count, half, rank), F32),
            pltpu.VMEM((count, half, rank), F32),
            pltpu.VMEM((RING, half, rank), F32),
            pltpu.VMEM((count, half, rank), F32),
            pltpu.VMEM((rank, 2 * rank), F32),
            pltpu.VMEM((chips, half, columns), F32),
            pltpu.VMEM((chips, half, columns), F32),
            pltpu.VMEM((chips, half, columns), F32),
            pltpu.VMEM((chips, half, columns), F32),
            dma((RING + 2,)),
            dma((2,)),
            dma((2, EVENTS)),
            dma,
            dma((2, EVENTS)),
            dma((2,)),
            dma((2,)),
            dma((2,)),
            dma((2,)),
            dma,
            dma,
        ],
        compiler_params=pltpu.CompilerParams(
            collective_id=0, has_side_effects=True, vmem_limit_bytes=56 * 1024 * 1024
        ),
    )(snapshots, sketch)
    return pl.pallas_call(
        finish,
        out_shape=outputs,
        in_specs=[pl.BlockSpec(memory_space=pltpu.VMEM)] * 2,
        out_specs=(anywhere, anywhere),
        scratch_shapes=[dma((PIECES + 1,))],
        compiler_params=pltpu.CompilerParams(vmem_limit_bytes=16 * 1024 * 1024),
    )(basis, projected)


def solution(mesh):
    in_specs = (P("rows", "snaps"), P("snaps", None))
    out_specs = (P(("rows", "snaps"), None), P("rows", "snaps"))
    return jax.shard_map(local, mesh=mesh, in_specs=in_specs, out_specs=out_specs, check_vma=False)
```
